32 devices in a mesh: group: 2 (over x), dp: 16 (over z, y, core).
Axes of the slice: x: 2, y: 2, z: 4, core: 2. Of those that a mesh axis runs over, the one named last changes fastest.
Arguments:
- attn_out: bfloat16 [4608, 12288], P('group', 'dp'), parts along dimension 0, may hold values from -6 to 6
- out_grad: bfloat16 [4608, 4096], P(('group', 'dp')), parts along dimension 0, may hold values from -6 to 6
- o_weight: bfloat16 [12288, 4096], P('dp'), may hold values from -0.09375 to 0.09375
- head_counts: int32 [16], P('dp'), may hold values from 2 to 6, as said below
- seq_counts: int32 [32], P(('group', 'dp')), parts along dimension 0, may hold values from 7 to 9, as said below
Outputs:
- attn_grad: bfloat16 [4608, 12288], P('group', 'dp'), parts along dimension 0
- weight_grad: bfloat16 [24576, 4096], P(('group', 'dp')), parts along dimension 0
The draws below stay inside these ranges and needn't reach their ends.
There are 2 independent parts, one for each index of `group`. The reference program is written for one: setup_inputs(seed, part) draws one part's arguments, and reference() takes and returns one part's arrays. A program takes and returns all parts, laid end to end along the dimension named above; an argument that names none is the same for every part. Nothing has to cross between parts.
Inputs may be any that keep to these rules, and one draw needn't show every extreme that they name: `head_counts`: entry b is the number of 128-feature heads at the start of device b's block of 6 heads; the entries sum to 64, never fall from one device to the next, and both the least and the most are reached. `seq_counts`: entry b is the number of 16-token sequences at the start of device b's 144 token slots; the entries sum to 128, and the most is reached.
All inputs are finite; a program needn't handle non-finite values.
Results may differ from the reference program's by a relative error of at most 0.0004.
Values may be sent and summed in bfloat16 or wider, within the bound.
No kernel may reach another device: no remote copies, remote signals or barrier semaphores. Data moves between devices by JAX's collectives and lax.ppermute only.
A program may use at most 128 MiB of HBM per device.

```python
import jax
import jax.numpy as jnp

D = 4096
HEADS = 64
HEAD_DIM = 128
SEQ = 16
MEAN_SEQ = 8
SEQ_EXTRA = 1
ROWS = 144
SLOTS = 2304
CAP_HD = 768
HD_PAD = 12288
N_DP = 16


def paired_counts(key, mean_count, spread, devices):
    order_key, shift_key = jax.random.split(key)
    shifts = jax.random.randint(shift_key, (devices // 2,), 0, spread + 1)
    shifts = shifts.at[0].set(spread)
    signed = jnp.concatenate([shifts, -shifts])
    return ((mean_count + signed).astype(jnp.int32), order_key)


def draw_head_counts(key, part):
    key = jax.random.fold_in(key, 5)
    counts, order_key = paired_counts(key, HEADS // N_DP, HEADS // N_DP // 2, N_DP)
    return jnp.sort(counts).astype(jnp.int32)


def draw_seq_counts(key, part):
    key = jax.random.fold_in(key, 9)
    counts, order_key = paired_counts(key, MEAN_SEQ, SEQ_EXTRA, N_DP)
    device_order = jax.random.permutation(order_key, N_DP)
    return jnp.zeros((N_DP,), jnp.int32).at[device_order].set(counts)


def steps_of(rng, dims, shards, least, largest):
    def one(position, shards_of):
        heights = jax.random.uniform(jax.random.fold_in(jax.random.fold_in(rng, 6), position), (shards_of,), jnp.float32, least / len(shards), largest / len(shards))
        return jnp.repeat(jnp.exp(heights), dims[position] // shards_of).reshape((-1,) + (1,) * (len(dims) - position - 1))

    gain = one(*shards[0])
    for cut in shards[1:]:
        gain = gain * one(*cut)
    return gain


def centred(key, shape, deviation, reach, pieces=(), kind=jnp.bfloat16):
    gain = steps_of(key, shape, pieces, -0.22, 0.18) if pieces else 1.0
    drawn = jax.random.normal(key, shape, jnp.float32) * deviation * gain
    return jnp.minimum(jnp.maximum(drawn, -reach), reach).astype(kind)


def setup_inputs(seed: int = 0, part: int = 0) -> dict:
    streams_of = jax.random.split(jax.random.key(seed), 6)
    part_splits = jax.random.split(jax.random.fold_in(streams_of[5], part), 6)
    return {
        "attn_out": centred(part_splits[0], (SLOTS, HD_PAD), 1.0, 6.0, ((1, 16),)),
        "out_grad": centred(part_splits[1], (SLOTS, D), 1.0, 6.0, ((0, 16),)),
        "o_weight": centred(streams_of[2], (HD_PAD, D), D ** -0.5, 0.09375, ((0, 16),)),
        "head_counts": draw_head_counts(jax.random.fold_in(streams_of[5], 71), part),
        "seq_counts": draw_seq_counts(jax.random.fold_in(jax.random.fold_in(streams_of[5], part), 71), part),
    }


def reference(attn_out, out_grad, o_weight, head_counts, seq_counts):
    slot_index = jnp.arange(SLOTS, dtype=jnp.int32)
    slot_owner = slot_index // ROWS
    live_row = slot_index - slot_owner * ROWS < seq_counts[slot_owner] * SEQ
    column_index = jnp.arange(HD_PAD, dtype=jnp.int32)
    column_owner = column_index // CAP_HD
    live_column = column_index - column_owner * CAP_HD < head_counts[column_owner] * HEAD_DIM
    grad_live = jnp.where(live_row[:, None], out_grad, jnp.zeros_like(out_grad))
    back_full = jnp.dot(grad_live, o_weight.T, preferred_element_type=jnp.float32)
    attn_grad = jnp.where(live_column[None, :], back_full, 0.0).astype(jnp.bfloat16)
    weight_full = jnp.dot(attn_out.T, grad_live, preferred_element_type=jnp.float32)
    weight_full = jnp.where(live_column[:, None], weight_full, 0.0)
    square_sum = jnp.sum(weight_full * weight_full)
    factor = jnp.minimum(1.0, 1.0 / jnp.sqrt(square_sum / (HEADS * HEAD_DIM * D) + 1e-06))
    weight_grad = (weight_full * factor).astype(jnp.bfloat16)
    return (attn_grad, weight_grad)
```

```python
import functools

import jax
import jax.numpy as jnp
from jax import lax
from jax.experimental import pallas as pl
from jax.experimental.pallas import tpu as pltpu
from jax.sharding import PartitionSpec as P

HEADS = 64
HEAD_DIM = 128
SEQ = 16
CHUNKS = 4
VMEM_LIMIT = 56 * 1024 * 1024


def params():
    return pltpu.CompilerParams(
        dimension_semantics=("arbitrary",), vmem_limit_bytes=VMEM_LIMIT
    )


def weight_kernel(at_ref, g_ref, before_ref, w_ref, squares_ref):
    @pl.when(pl.program_id(0) == 0)
    def _():
        squares_ref[...] = before_ref[...]

    w = jnp.dot(at_ref[...], g_ref[...], preferred_element_type=jnp.float32)
    w_ref[...] = w
    rows, columns = w.shape
    folded = jnp.sum((w * w).reshape(rows // 8, 8, columns), axis=0)
    total = squares_ref[...]
    for lane in range(0, columns, 128):
        total = total + folded[:, lane : lane + 128]
    squares_ref[...] = total


def weight_chunk(at, g, before):
    capacity, slots = at.shape
    width = g.shape[1]
    tile = min(256, width)
    return pl.pallas_call(
        weight_kernel,
        grid=(width // tile,),
        in_specs=[
            pl.BlockSpec((capacity, slots), lambda j: (0, 0)),
            pl.BlockSpec((slots, tile), lambda j: (0, j)),
            pl.BlockSpec((8, 128), lambda j: (0, 0)),
        ],
        out_specs=[
            pl.BlockSpec((capacity, tile), lambda j: (0, j)),
            pl.BlockSpec((8, 128), lambda j: (0, 0)),
        ],
        out_shape=[
            jax.ShapeDtypeStruct((capacity, width), jnp.float32),
            jax.ShapeDtypeStruct((8, 128), jnp.float32),
        ],
        compiler_params=params(),
        cost_estimate=pl.CostEstimate(
            flops=2 * capacity * slots * width,
            bytes_accessed=2 * slots * (capacity + width) + 4 * capacity * width,
            transcendentals=0,
        ),
        name="weight_chunk",
    )(at, g, before)


def attn_kernel(chunks, width_ref, wt_ref, *refs):
    g_refs, out_ref = refs[:chunks], refs[chunks]
    width = g_refs[0].shape[1]
    total = None
    for i, g_ref in enumerate(g_refs):
        part = lax.dot_general(
            g_ref[...],
            wt_ref[:, i * width : (i + 1) * width],
            (((1,), (1,)), ((), ())),
            preferred_element_type=jnp.float32,
        )
        total = part if total is None else total + part
    column = lax.broadcasted_iota(jnp.int32, total.shape, 1)
    out_ref[...] = jnp.where(column < width_ref[0], total, 0.0).astype(jnp.bfloat16)


def attn_grad_of(gs, o_weight, live_width):
    capacity, features = o_weight.shape
    slots, width = gs[0].shape
    tile = 256
    return pl.pallas_call(
        functools.partial(attn_kernel, len(gs)),
        grid=(slots // tile,),
        in_specs=[
            pl.BlockSpec(memory_space=pltpu.SMEM),
            pl.BlockSpec((capacity, features), lambda j: (0, 0)),
        ]
        + [pl.BlockSpec((tile, width), lambda j: (j, 0)) for _ in gs],
        out_specs=pl.BlockSpec((tile, capacity), lambda j: (j, 0)),
        out_shape=jax.ShapeDtypeStruct((slots, capacity), jnp.bfloat16),
        compiler_params=params(),
        cost_estimate=pl.CostEstimate(
            flops=2 * capacity * slots * features,
            bytes_accessed=2 * (slots * features + capacity * features + capacity * slots),
            transcendentals=0,
        ),
        name="attn_grad",
    )(live_width, o_weight, *gs)


def scale_kernel(chunks, features, *refs):
    w_refs, squares_ref, out_ref = refs[:chunks], refs[chunks], refs[chunks + 1]
    square_sum = jnp.sum(
        jnp.sum(squares_ref[...], axis=0, keepdims=True), axis=1, keepdims=True
    )
    factor = jnp.minimum(
        1.0, 1.0 / jnp.sqrt(square_sum / (HEADS * HEAD_DIM * features) + 1e-06)
    )
    width = w_refs[0].shape[1]
    for i, ref in enumerate(w_refs):
        out_ref[:, i * width : (i + 1) * width] = (ref[...] * factor).astype(jnp.bfloat16)


def scaled(ws, squares):
    capacity, width = ws[0].shape
    features = width * len(ws)
    tile = 64
    return pl.pallas_call(
        functools.partial(scale_kernel, len(ws), features),
        grid=(capacity // tile,),
        in_specs=[pl.BlockSpec((tile, width), lambda j: (j, 0)) for _ in ws]
        + [pl.BlockSpec(squares.shape, lambda j: (0, 0))],
        out_specs=pl.BlockSpec((tile, features), lambda j: (j, 0)),
        out_shape=jax.ShapeDtypeStruct((capacity, features), jnp.bfloat16),
        compiler_params=params(),
        cost_estimate=pl.CostEstimate(
            flops=capacity * features,
            bytes_accessed=6 * capacity * features,
            transcendentals=0,
        ),
        name="scale",
    )(*ws, squares)


def on_device(attn_out, out_grad, o_weight, head_counts, seq_counts):
    row_count, features = out_grad.shape
    capacity = o_weight.shape[0]
    live_width = head_counts * HEAD_DIM
    row_live = lax.broadcasted_iota(jnp.int32, (row_count, 1), 0) < seq_counts[0] * SEQ
    head_live = lax.broadcasted_iota(jnp.int32, (1, capacity), 1) < live_width[0]
    width = features // CHUNKS
    at = jnp.where(head_live, attn_out, jnp.zeros_like(attn_out)).T
    squares = jnp.zeros((8, 128), jnp.float32)
    gs, ws = [], []
    for i in range(CHUNKS):
        piece = out_grad[:, i * width : (i + 1) * width]
        piece = jnp.where(row_live, piece, jnp.zeros_like(piece))
        g = lax.all_gather(piece, "dp", axis=0, tiled=True)
        w, squares = weight_chunk(at, g, squares)
        gs.append(g)
        ws.append(w)
    parts = lax.all_gather(squares, "dp", axis=0, tiled=True)
    attn_grad = attn_grad_of(gs, o_weight, live_width)
    return attn_grad, scaled(ws, parts)


def solution(mesh):
    placed = (
        P("group", "dp"),
        P(("group", "dp"), None),
        P("dp", None),
        P("dp"),
        P(("group", "dp")),
    )
    return jax.shard_map(
        on_device,
        mesh=mesh,
        in_specs=placed,
        out_specs=(P("group", "dp"), P(("group", "dp"), None)),
        check_vma=False,
    )
```

```python
import functools

import jax
import jax.numpy as jnp
from jax import lax
from jax.experimental import pallas as pl
from jax.experimental.pallas import tpu as pltpu
from jax.sharding import PartitionSpec as P

HEADS = 64
HEAD_DIM = 128
SEQ = 16
MIB = 1024 * 1024


def params(mib):
    return pltpu.CompilerParams(vmem_limit_bytes=mib * MIB)


def weight_kernel(at_ref, g_ref, w_ref, squares_ref):
    slots, features = g_ref.shape
    tile = 512
    squares_ref[...] = jnp.zeros_like(squares_ref)

    def body(g_tile):
        start = pl.multiple_of(pl.program_id(0) * tile, tile)
        w = jnp.dot(at_ref[...], g_tile[...], preferred_element_type=jnp.float32)
        w_ref[:, pl.ds(start, tile)] = w
        folded = jnp.sum((w * w).reshape(w.shape[0] // 8, 8, tile), axis=0)
        total = squares_ref[...]
        for lane in range(0, tile, 128):
            total = total + folded[:, lane : lane + 128]
        squares_ref[...] = total

    pltpu.emit_pipeline(
        body,
        grid=(features // tile,),
        in_specs=[pl.BlockSpec((slots, tile), lambda j: (0, j))],
    )(g_ref)


def weight_full(at, g):
    capacity, slots = at.shape
    features = g.shape[1]
    return pl.pallas_call(
        weight_kernel,
        in_specs=[
            pl.BlockSpec(memory_space=pltpu.VMEM),
            pl.BlockSpec(memory_space=pl.ANY),
        ],
        out_specs=[
            pl.BlockSpec(memory_space=pltpu.VMEM),
            pl.BlockSpec(memory_space=pltpu.VMEM),
        ],
        out_shape=[
            pltpu.VMEM((capacity, features), jnp.float32),
            pltpu.VMEM((8, 128), jnp.float32),
        ],
        compiler_params=params(24),
        cost_estimate=pl.CostEstimate(
            flops=2 * capacity * slots * features,
            bytes_accessed=2 * slots * (capacity + features),
            transcendentals=0,
        ),
        name="weight_full",
    )(pltpu.with_memory_space_constraint(at, pltpu.VMEM), g)


def attn_kernel(width_ref, w_ref, g_ref, *refs):
    out_ref = refs[-1]
    total = lax.dot_general(
        g_ref[...], w_ref[...], (((1,), (1,)), ((), ())), preferred_element_type=jnp.float32
    )
    column = lax.broadcasted_iota(jnp.int32, total.shape, 1)
    out_ref[...] = jnp.where(column < width_ref[0], total, 0.0).astype(jnp.bfloat16)


def attn_rows(g, weight, live_width, half, before):
    capacity, features = weight.shape
    slots = g.shape[0]
    tile = slots // 6
    steps = slots // 2 // tile
    first = half * steps
    extra = [] if before is None else [before]
    return pl.pallas_call(
        attn_kernel,
        grid=(steps,),
        in_specs=[
            pl.BlockSpec(memory_space=pltpu.SMEM),
            pl.BlockSpec(memory_space=pltpu.VMEM),
            pl.BlockSpec((tile, features), lambda j: (first + j, 0)),
        ]
        + [pl.BlockSpec(memory_space=pl.ANY) for _ in extra],
        out_specs=pl.BlockSpec((tile, capacity), lambda j: (first + j, 0)),
        out_shape=jax.ShapeDtypeStruct((slots, capacity), jnp.bfloat16),
        input_output_aliases={3: 0} if extra else {},
        compiler_params=params(24),
        cost_estimate=pl.CostEstimate(
            flops=capacity * slots * features,
            bytes_accessed=slots * features + capacity * slots,
            transcendentals=0,
        ),
        name="attn_rows",
    )(live_width, weight, g, *extra)


def scale_kernel(w_ref, squares_ref, out_ref):
    capacity, features = w_ref.shape
    tile = 64
    square_sum = jnp.sum(
        jnp.sum(squares_ref[...], axis=0, keepdims=True), axis=1, keepdims=True
    )
    factor = jnp.minimum(
        1.0, 1.0 / jnp.sqrt(square_sum / (HEADS * HEAD_DIM * features) + 1e-06)
    )

    def body(out_tile):
        start = pl.multiple_of(pl.program_id(0) * tile, tile)
        out_tile[...] = (w_ref[pl.ds(start, tile), :] * factor).astype(jnp.bfloat16)

    pltpu.emit_pipeline(
        body,
        grid=(capacity // tile,),
        out_specs=[pl.BlockSpec((tile, features), lambda j: (j, 0))],
    )(out_ref)


def scaled(w, squares):
    capacity, features = w.shape
    return pl.pallas_call(
        scale_kernel,
        in_specs=[
            pl.BlockSpec(memory_space=pltpu.VMEM),
            pl.BlockSpec(memory_space=pltpu.VMEM),
        ],
        out_specs=pl.BlockSpec(memory_space=pl.ANY),
        out_shape=jax.ShapeDtypeStruct((capacity, features), jnp.bfloat16),
        compiler_params=params(24),
        cost_estimate=pl.CostEstimate(
            flops=capacity * features,
            bytes_accessed=2 * capacity * features,
            transcendentals=0,
        ),
        name="scale",
    )(pltpu.with_memory_space_constraint(w, pltpu.VMEM), squares)


def exchange(x, devices, stride, radix):
    total = x
    for shift in range(1, radix):
        pairs = []
        for d in range(devices):
            digit = d // stride % radix
            pairs.append((d, d + ((digit + shift) % radix - digit) * stride))
        total = total + lax.ppermute(x, "dp", pairs)
    return total


def on_device(devices, attn_out, out_grad, o_weight, head_counts, seq_counts):
    row_count = out_grad.shape[0]
    capacity = o_weight.shape[0]
    live_width = head_counts * HEAD_DIM
    row_live = lax.broadcasted_iota(jnp.int32, (row_count, 1), 0) < seq_counts[0] * SEQ
    head_live = lax.broadcasted_iota(jnp.int32, (1, capacity), 1) < live_width[0]
    grad_live = jnp.where(row_live, out_grad, jnp.zeros_like(out_grad))
    g = lax.all_gather(grad_live, "dp", axis=0, tiled=True)
    g = pltpu.with_memory_space_constraint(g, pltpu.HBM)
    at = jnp.where(head_live, attn_out, jnp.zeros_like(attn_out)).T
    w, squares = weight_full(at, g)
    weight = pltpu.with_memory_space_constraint(o_weight, pltpu.VMEM)
    attn_grad, stride, half = None, 1, 0
    while stride < devices:
        radix = min(4, devices // stride)
        squares = exchange(squares, devices, stride, radix)
        if half < 2:
            attn_grad = attn_rows(g, weight, live_width, half, attn_grad)
        stride, half = stride * radix, half + 1
    return attn_grad, scaled(w, squares)


def solution(mesh):
    placed = (
        P("group", "dp"),
        P(("group", "dp"), None),
        P("dp", None),
        P("dp"),
        P(("group", "dp")),
    )
    return jax.shard_map(
        functools.partial(on_device, mesh.shape["dp"]),
        mesh=mesh,
        in_specs=placed,
        out_specs=(P("group", "dp"), P(("group", "dp"), None)),
        check_vma=False,
    )
```

```python
import functools

import jax
import jax.numpy as jnp
import numpy as np
from jax import lax
from jax.experimental import pallas as pl
from jax.experimental.pallas import tpu as pltpu
from jax.sharding import PartitionSpec as P

HEADS = 64
HEAD_DIM = 128
SEQ = 16
TILE = 512
MIB = 1024 * 1024


class Ring:
    def __init__(self, devices, columns):
        self.devices = devices
        self.length = devices // 2
        rows = self.length // columns
        if columns == 1:
            self.chips = list(range(rows))
        else:
            self.chips = [2 * z for z in range(rows)]
            self.chips += [2 * z + 1 for z in reversed(range(rows))]
        self.position = {chip: p for p, chip in enumerate(self.chips)}

    def device(self, position, core):
        return 2 * self.chips[position % self.length] + core

    def shift(self, step):
        return [
            (self.device(p, core), self.device(p + step, core))
            for p in range(self.length)
            for core in range(2)
        ]

    def swap(self):
        return [(d, d ^ 1) for d in range(self.devices)]

    def owners(self, offsets):
        table = []
        for d in range(self.devices):
            p, core = self.position[d // 2], d % 2
            row = []
            for offset in offsets:
                row += [self.device(p + offset, core), self.device(p + offset, 1 - core)]
            table.append(row)
        return np.array(table, np.int32)


def pick_kernel(owners_ref, width_ref, a_ref, out_ref):
    column = lax.broadcasted_iota(jnp.int32, a_ref.shape, 1)
    out_ref[...] = jnp.where(column < width_ref[0], a_ref[...], jnp.zeros_like(a_ref))


def picked(attn_out, owners, live_width, rows):
    slots, capacity = attn_out.shape
    return pl.pallas_call(
        pick_kernel,
        grid_spec=pltpu.PrefetchScalarGridSpec(
            num_scalar_prefetch=2,
            grid=(slots // rows,),
            in_specs=[pl.BlockSpec((rows, capacity), lambda i, owners, w: (owners[i], 0))],
            out_specs=pl.BlockSpec((rows, capacity), lambda i, owners, w: (i, 0)),
        ),
        out_shape=jax.ShapeDtypeStruct((slots, capacity), attn_out.dtype),
        cost_estimate=pl.CostEstimate(
            flops=0, bytes_accessed=4 * slots * capacity, transcendentals=0
        ),
        name="picked",
    )(owners, live_width, attn_out)


def phase_kernel(spec, *refs):
    do_weight, do_attn, fresh, squares, pieces, halves, rows = spec
    refs = list(refs)
    owners_ref, width_ref = refs.pop(0), refs.pop(0)
    at_ref = refs.pop(0) if do_weight else None
    weight_ref = refs.pop(0) if do_attn else None
    g_refs = [[refs.pop(0) for _ in range(pieces)] for _ in range(halves)]
    if do_weight and not fresh:
        refs.pop(0)
    if do_attn and not fresh:
        refs.pop(0)
    w_ref = refs.pop(0) if do_weight else None
    out_ref = refs.pop(0) if do_attn else None
    squares_ref = refs.pop(0)
    if do_attn:
        total_ref, block_ref, sems = refs
        total_ref[...] = jnp.zeros_like(total_ref)
    squares_ref[...] = jnp.zeros_like(squares_ref)
    span = g_refs[0][0].shape[1]

    def body(half, *tiles):
        start = pl.multiple_of(half * span + pl.program_id(0) * TILE, TILE)
        g = jnp.concatenate([t[...] for t in tiles], axis=0)
        if do_weight:
            w = jnp.dot(at_ref[...], g, preferred_element_type=jnp.float32)
            if not fresh:
                w = w + w_ref[:, pl.ds(start, TILE)]
            w_ref[:, pl.ds(start, TILE)] = w
        if squares:
            folded = jnp.sum((w * w).reshape(w.shape[0] // 8, 8, TILE), axis=0)
            total = squares_ref[...]
            for lane in range(0, TILE, 128):
                total = total + folded[:, lane : lane + 128]
            squares_ref[...] = total
        if do_attn:
            total_ref[...] += lax.dot_general(
                g,
                weight_ref[:, pl.ds(start, TILE)],
                (((1,), (1,)), ((), ())),
                preferred_element_type=jnp.float32,
            )

    for half in range(halves):
        pltpu.emit_pipeline(
            functools.partial(body, half),
            grid=(span // TILE,),
            in_specs=[pl.BlockSpec((rows, TILE), lambda j: (0, j))] * pieces,
        )(*g_refs[half])
    if do_attn:
        total = total_ref[...]
        column = lax.broadcasted_iota(jnp.int32, total.shape, 1)
        block_ref[...] = jnp.where(column < width_ref[0], total, 0.0).astype(jnp.bfloat16)
        copies = [
            pltpu.make_async_copy(
                block_ref.at[pl.ds(i * rows, rows)],
                out_ref.at[pl.ds(pl.multiple_of(owners_ref[i] * rows, rows), rows)],
                sems.at[i],
            )
            for i in range(pieces)
        ]
        for copy in copies:
            copy.start()
        for copy in copies:
            copy.wait()


def phase(owners, live_width, at, weight, gs, w, out, slots, squares=False):
    halves, pieces = len(gs), len(gs[0])
    rows = gs[0][0].shape[0]
    features = gs[0][0].shape[1] * halves
    do_weight, do_attn = at is not None, weight is not None
    capacity = at.shape[0] if do_weight else weight.shape[0]
    fresh = (w is None) if do_weight else (out is None)
    vmem = pl.BlockSpec(memory_space=pltpu.VMEM)
    smem = pl.BlockSpec(memory_space=pltpu.SMEM)
    hbm = pl.BlockSpec(memory_space=pl.ANY)

    args, specs, outs, out_specs, aliases, scratch = [], [], [], [], {}, []

    def add(arg, spec):
        args.append(arg)
        specs.append(spec)

    add(owners, smem)
    add(live_width, smem)
    if do_weight:
        add(pltpu.with_memory_space_constraint(at, pltpu.VMEM), vmem)
    if do_attn:
        add(weight, vmem)
    for group in gs:
        for g in group:
            add(g, hbm)
    if do_weight:
        if not fresh:
            aliases[len(args)] = len(outs)
            add(pltpu.with_memory_space_constraint(w, pltpu.VMEM), vmem)
        outs.append(pltpu.VMEM((capacity, features), jnp.float32))
        out_specs.append(vmem)
    if do_attn:
        if not fresh:
            aliases[len(args)] = len(outs)
            add(out, hbm)
        outs.append(jax.ShapeDtypeStruct((slots, capacity), jnp.bfloat16))
        out_specs.append(hbm)
        scratch = [
            pltpu.VMEM((rows * pieces, capacity), jnp.float32),
            pltpu.VMEM((rows * pieces, capacity), jnp.bfloat16),
            pltpu.SemaphoreType.DMA((pieces,)),
        ]
    outs.append(pltpu.VMEM((8, 128), jnp.float32))
    out_specs.append(vmem)
    dots = do_weight + do_attn
    return pl.pallas_call(
        functools.partial(
            phase_kernel, (do_weight, do_attn, fresh, squares, pieces, halves, rows)
        ),
        in_specs=specs,
        out_specs=out_specs,
        out_shape=outs,
        scratch_shapes=scratch,
        input_output_aliases=aliases,
        compiler_params=pltpu.CompilerParams(vmem_limit_bytes=16 * MIB),
        cost_estimate=pl.CostEstimate(
            flops=dots * capacity * rows * pieces * features // 4,
            bytes_accessed=2 * rows * pieces * features,
            transcendentals=0,
        ),
        name="phase_" + "w" * do_weight + "a" * do_attn,
    )(*args)


def scale_kernel(w_ref, squares_ref, out_ref):
    capacity, features = w_ref.shape
    tile = 64
    square_sum = jnp.sum(
        jnp.sum(squares_ref[...], axis=0, keepdims=True), axis=1, keepdims=True
    )
    factor = jnp.minimum(
        1.0, 1.0 / jnp.sqrt(square_sum / (HEADS * HEAD_DIM * features) + 1e-06)
    )

    def body(out_tile):
        start = pl.multiple_of(pl.program_id(0) * tile, tile)
        out_tile[...] = (w_ref[pl.ds(start, tile), :] * factor).astype(jnp.bfloat16)

    pltpu.emit_pipeline(
        body,
        grid=(capacity // tile,),
        out_specs=[pl.BlockSpec((tile, features), lambda j: (j, 0))],
    )(out_ref)


def scaled(w, squares):
    capacity, features = w.shape
    vmem = pl.BlockSpec(memory_space=pltpu.VMEM)
    return pl.pallas_call(
        scale_kernel,
        in_specs=[vmem, vmem],
        out_specs=pl.BlockSpec(memory_space=pl.ANY),
        out_shape=jax.ShapeDtypeStruct((capacity, features), jnp.bfloat16),
        compiler_params=pltpu.CompilerParams(vmem_limit_bytes=16 * MIB),
        cost_estimate=pl.CostEstimate(
            flops=capacity * features,
            bytes_accessed=2 * capacity * features,
            transcendentals=0,
        ),
        name="scale",
    )(pltpu.with_memory_space_constraint(w, pltpu.VMEM), squares)


def after(done, *arrays):
    hbm = pl.BlockSpec(memory_space=pl.ANY)
    return pl.pallas_call(
        lambda *refs: None,
        in_specs=[hbm] * (len(arrays) + 1),
        out_specs=[hbm] * len(arrays),
        out_shape=[jax.ShapeDtypeStruct(x.shape, x.dtype) for x in arrays],
        input_output_aliases={i: i for i in range(len(arrays))},
        name="after",
    )(*arrays, done)


def exchange(x, devices, stride, radix):
    total = x
    for shift in range(1, radix):
        pairs = []
        for d in range(devices):
            digit = d // stride % radix
            pairs.append((d, d + ((digit + shift) % radix - digit) * stride))
        total = total + lax.ppermute(x, "dp", pairs)
    return total


def on_device(ring, attn_out, out_grad, o_weight, head_counts, seq_counts):
    rows, features = out_grad.shape
    slots = attn_out.shape[0]
    devices, last = ring.devices, ring.length // 2
    live_width = head_counts * HEAD_DIM
    row_live = lax.broadcasted_iota(jnp.int32, (rows, 1), 0) < seq_counts[0] * SEQ
    own = jnp.where(row_live, out_grad, jnp.zeros_like(out_grad))

    offsets = [0] + [s * k for k in range(1, last) for s in (-1, 1)] + [last]
    owners = jnp.asarray(ring.owners(offsets))[lax.axis_index("dp")]
    a = picked(attn_out, owners, live_width, rows)
    weight = pltpu.with_memory_space_constraint(o_weight, pltpu.VMEM)

    def swap(x):
        return lax.ppermute(x, "dp", ring.swap())

    def forward(x):
        return lax.ppermute(x, "dp", ring.shift(1))

    def backward(x):
        return lax.ppermute(x, "dp", ring.shift(-1))

    arrived = [[[own, swap(own)]]]
    ahead, behind = forward(own), backward(own)
    w, out, begin, late = None, None, 0, []
    for k in range(last + 1):
        (gs,) = arrived
        count = len(gs[0])
        ids = owners[begin : begin + count]
        at = a[begin * rows : (begin + count) * rows].T
        begin += count
        if k < last - 1:
            w, out, done = phase(ids, live_width, at, weight, gs, w, out, slots)
        else:
            w, done = phase(ids, live_width, at, None, gs, w, None, slots, k == last)
            late.append((ids, gs))
        if k < last - 1:
            ahead, behind = after(done, ahead, behind)
            arrived = [[[ahead, swap(ahead), behind, swap(behind)]]]
            if k + 2 < last:
                ahead, behind = forward(ahead), backward(behind)
            else:
                ahead = forward(ahead[:, : features // 2])
                behind = backward(behind[:, features // 2 :])
        elif k == last - 1:
            ahead, behind = after(done, ahead, behind)
            arrived = [[[ahead, swap(ahead)], [behind, swap(behind)]]]
    squares = done

    stride = 1
    while stride < devices:
        radix = min(4, devices // stride)
        squares = exchange(squares, devices, stride, radix)
        if late:
            ids, gs = late.pop(0)
            out, done = phase(ids, live_width, None, weight, gs, None, out, slots)
        stride *= radix
    return out, scaled(w, squares)


def solution(mesh):
    placed = (
        P("group", "dp"),
        P(("group", "dp"), None),
        P("dp", None),
        P("dp"),
        P(("group", "dp")),
    )
    ring = Ring(mesh.shape["dp"], 2 if mesh.shape["group"] == 2 else 1)
    return jax.shard_map(
        functools.partial(on_device, ring),
        mesh=mesh,
        in_specs=placed,
        out_specs=(P("group", "dp"), P(("group", "dp"), None)),
        check_vma=False,
    )
```

```python
import functools

import jax
import jax.numpy as jnp
import numpy as np
from jax import lax
from jax.experimental import pallas as pl
from jax.experimental.pallas import tpu as pltpu
from jax.sharding import PartitionSpec as P

HEADS = 64
HEAD_DIM = 128
SEQ = 16
TILE = 512
MIB = 1024 * 1024


class Ring:
    def __init__(self, devices, columns):
        self.devices = devices
        self.length = devices // 2
        rows = self.length // columns
        if columns == 1:
            self.chips = list(range(rows))
        else:
            self.chips = [2 * z for z in range(rows)]
            self.chips += [2 * z + 1 for z in reversed(range(rows))]
        self.position = {chip: p for p, chip in enumerate(self.chips)}

    def device(self, position, core):
        return 2 * self.chips[position % self.length] + core

    def shift(self, step):
        return [
            (self.device(p, core), self.device(p + step, core))
            for p in range(self.length)
            for core in range(2)
        ]

    def swap(self):
        return [(d, d ^ 1) for d in range(self.devices)]

    def owners(self, offsets):
        table = []
        for d in range(self.devices):
            p, core = self.position[d // 2], d % 2
            row = []
            for offset in offsets:
                row += [self.device(p + offset, core), self.device(p + offset, 1 - core)]
            table.append(row)
        return np.array(table, np.int32)


def live_kernel(seqs_ref, me_ref, grad_ref, out_ref, sem):
    copy = pltpu.make_async_copy(grad_ref, out_ref, sem)
    copy.start()
    copy.wait()
    for s in range(out_ref.shape[0] // SEQ):

        @pl.when(s >= seqs_ref[0])
        def _():
            dead = out_ref.at[s * SEQ : (s + 1) * SEQ]
            dead[...] = jnp.zeros_like(dead)


def live_rows(seq_counts, me, out_grad):
    smem = pl.BlockSpec(memory_space=pltpu.SMEM)
    return pl.pallas_call(
        live_kernel,
        in_specs=[smem, smem, pl.BlockSpec(memory_space=pl.ANY)],
        out_specs=pl.BlockSpec(memory_space=pltpu.VMEM),
        out_shape=pltpu.VMEM(out_grad.shape, out_grad.dtype),
        scratch_shapes=[pltpu.SemaphoreType.DMA],
        compiler_params=pltpu.CompilerParams(vmem_limit_bytes=4 * MIB),
        name="live",
    )(seq_counts, me, pltpu.with_memory_space_constraint(out_grad, pltpu.HBM))


def prep_kernel(counts, rows, table_ref, me_ref, heads_ref, a_ref, *refs):
    at_refs, (block_ref, sems) = refs[: len(counts)], refs[len(counts) :]
    width = heads_ref[0] * HEAD_DIM
    copies = []
    for i in range(sum(counts)):
        owner = table_ref[me_ref[0], i]
        copies.append(
            pltpu.make_async_copy(
                a_ref.at[pl.ds(pl.multiple_of(owner * rows, rows), rows)],
                block_ref.at[pl.ds(i * rows, rows)],
                sems.at[i],
            )
        )
        copies[-1].start()
    begin = 0
    for at_ref, count in zip(at_refs, counts):
        for copy in copies[begin : begin + count]:
            copy.wait()
        block = block_ref[begin * rows : (begin + count) * rows, :]
        column = lax.broadcasted_iota(jnp.int32, block.shape, 1)
        at_ref[...] = jnp.where(column < width, block, jnp.zeros_like(block)).T
        begin += count


def prepared(table, me, head_counts, attn_out, counts, rows):
    slots, capacity = attn_out.shape
    vmem = pl.BlockSpec(memory_space=pltpu.VMEM)
    smem = pl.BlockSpec(memory_space=pltpu.SMEM)
    return pl.pallas_call(
        functools.partial(prep_kernel, counts, rows),
        in_specs=[smem, smem, smem, pl.BlockSpec(memory_space=pl.ANY)],
        out_specs=[vmem] * len(counts),
        out_shape=[pltpu.VMEM((capacity, count * rows), jnp.bfloat16) for count in counts],
        scratch_shapes=[
            pltpu.VMEM((slots, capacity), jnp.bfloat16),
            pltpu.SemaphoreType.DMA((sum(counts),)),
        ],
        compiler_params=pltpu.CompilerParams(vmem_limit_bytes=12 * MIB),
        cost_estimate=pl.CostEstimate(
            flops=0, bytes_accessed=4 * slots * capacity, transcendentals=0
        ),
        name="prep",
    )(table, me, head_counts, pltpu.with_memory_space_constraint(attn_out, pltpu.HBM))


def phase_kernel(spec, *refs):
    do_weight, do_attn, fresh, squares, pieces, halves, rows, begin = spec
    refs = list(refs)
    table_ref, me_ref, heads_ref = refs.pop(0), refs.pop(0), refs.pop(0)
    at_ref = refs.pop(0) if do_weight else None
    weight_ref = refs.pop(0) if do_attn else None
    g_refs = [[refs.pop(0) for _ in range(pieces)] for _ in range(halves)]
    if do_weight and not fresh:
        refs.pop(0)
    if do_attn and not fresh:
        refs.pop(0)
    w_ref = refs.pop(0) if do_weight else None
    out_ref = refs.pop(0) if do_attn else None
    squares_ref = refs.pop(0)
    if do_attn:
        total_ref, block_ref, sems = refs
        total_ref[...] = jnp.zeros_like(total_ref)
    squares_ref[...] = jnp.zeros_like(squares_ref)
    span = g_refs[0][0].shape[1]

    def body(half, j, carry):
        here = pl.ds(pl.multiple_of(j * TILE, TILE), TILE)
        there = pl.ds(pl.multiple_of(half * span + j * TILE, TILE), TILE)
        g = jnp.concatenate([t[:, here] for t in g_refs[half]], axis=0)
        if do_weight:
            w = jnp.dot(at_ref[...], g, preferred_element_type=jnp.float32)
            if not fresh:
                w = w + w_ref[:, there]
            w_ref[:, there] = w
        if squares:
            folded = jnp.sum((w * w).reshape(w.shape[0] // 8, 8, TILE), axis=0)
            total = squares_ref[...]
            for lane in range(0, TILE, 128):
                total = total + folded[:, lane : lane + 128]
            squares_ref[...] = total
        if do_attn:
            total_ref[...] += lax.dot_general(
                g,
                weight_ref[:, there],
                (((1,), (1,)), ((), ())),
                preferred_element_type=jnp.float32,
            )
        return carry

    for half in range(halves):
        lax.fori_loop(0, span // TILE, functools.partial(body, half), 0)
    if do_attn:
        total = total_ref[...]
        column = lax.broadcasted_iota(jnp.int32, total.shape, 1)
        block_ref[...] = jnp.where(column < heads_ref[0] * HEAD_DIM, total, 0.0).astype(jnp.bfloat16)
        copies = []
        for i in range(pieces):
            owner = table_ref[me_ref[0], begin + i]
            copies.append(
                pltpu.make_async_copy(
                    block_ref.at[pl.ds(i * rows, rows)],
                    out_ref.at[pl.ds(pl.multiple_of(owner * rows, rows), rows)],
                    sems.at[i],
                )
            )
            copies[-1].start()
        for copy in copies:
            copy.wait()


def phase(where, begin, at, weight, gs, w, out, slots, squares=False):
    halves, pieces = len(gs), len(gs[0])
    rows = gs[0][0].shape[0]
    features = gs[0][0].shape[1] * halves
    do_weight, do_attn = at is not None, weight is not None
    capacity = at.shape[0] if do_weight else weight.shape[0]
    fresh = (w is None) if do_weight else (out is None)
    vmem = pl.BlockSpec(memory_space=pltpu.VMEM)
    smem = pl.BlockSpec(memory_space=pltpu.SMEM)
    hbm = pl.BlockSpec(memory_space=pl.ANY)

    args, specs, outs, out_specs, aliases, scratch = [], [], [], [], {}, []

    def add(arg, spec):
        args.append(arg)
        specs.append(spec)

    def add_vmem(arg):
        add(pltpu.with_memory_space_constraint(arg, pltpu.VMEM), vmem)

    for scalar in where:
        add(scalar, smem)
    if do_weight:
        add_vmem(at)
    if do_attn:
        add_vmem(weight)
    for group in gs:
        for g in group:
            add_vmem(g)
    if do_weight:
        if not fresh:
            aliases[len(args)] = len(outs)
            add_vmem(w)
        outs.append(pltpu.VMEM((capacity, features), jnp.float32))
        out_specs.append(vmem)
    if do_attn:
        if not fresh:
            aliases[len(args)] = len(outs)
            add(out, hbm)
        outs.append(jax.ShapeDtypeStruct((slots, capacity), jnp.bfloat16))
        out_specs.append(hbm)
        scratch = [
            pltpu.VMEM((rows * pieces, capacity), jnp.float32),
            pltpu.VMEM((rows * pieces, capacity), jnp.bfloat16),
            pltpu.SemaphoreType.DMA((pieces,)),
        ]
    outs.append(pltpu.VMEM((8, 128), jnp.float32))
    out_specs.append(vmem)
    dots = do_weight + do_attn
    return pl.pallas_call(
        functools.partial(
            phase_kernel,
            (do_weight, do_attn, fresh, squares, pieces, halves, rows, begin),
        ),
        in_specs=specs,
        out_specs=out_specs,
        out_shape=outs,
        scratch_shapes=scratch,
        input_output_aliases=aliases,
        compiler_params=pltpu.CompilerParams(vmem_limit_bytes=10 * MIB),
        cost_estimate=pl.CostEstimate(
            flops=dots * capacity * rows * pieces * features // 4,
            bytes_accessed=2 * rows * pieces * features,
            transcendentals=0,
        ),
        name="phase_" + "w" * do_weight + "a" * do_attn,
    )(*args)


def scale_kernel(parts, w_ref, squares_ref, out_ref, block_ref, sems):
    capacity, features = w_ref.shape
    square_sum = jnp.sum(
        jnp.sum(squares_ref[...], axis=0, keepdims=True), axis=1, keepdims=True
    )
    factor = jnp.minimum(
        1.0, 1.0 / jnp.sqrt(square_sum / (HEADS * HEAD_DIM * features) + 1e-06)
    )
    copies = []
    height = capacity // parts
    for i in range(parts):
        part = pl.ds(i * height, height)
        block_ref[part, :] = (w_ref[part, :] * factor).astype(jnp.bfloat16)
        copies.append(pltpu.make_async_copy(block_ref.at[part], out_ref.at[part], sems.at[i]))
        copies[-1].start()
    for copy in copies:
        copy.wait()


def scaled(w, squares):
    capacity, features = w.shape
    vmem = pl.BlockSpec(memory_space=pltpu.VMEM)
    parts = 8
    return pl.pallas_call(
        functools.partial(scale_kernel, parts),
        in_specs=[vmem, vmem],
        out_specs=pl.BlockSpec(memory_space=pl.ANY),
        out_shape=jax.ShapeDtypeStruct((capacity, features), jnp.bfloat16),
        scratch_shapes=[
            pltpu.VMEM((capacity, features), jnp.bfloat16),
            pltpu.SemaphoreType.DMA((parts,)),
        ],
        compiler_params=pltpu.CompilerParams(vmem_limit_bytes=10 * MIB),
        cost_estimate=pl.CostEstimate(
            flops=capacity * features,
            bytes_accessed=2 * capacity * features,
            transcendentals=0,
        ),
        name="scale",
    )(pltpu.with_memory_space_constraint(w, pltpu.VMEM), squares)


def after(done, *arrays):
    vmem = pl.BlockSpec(memory_space=pltpu.VMEM)
    return pl.pallas_call(
        lambda *refs: None,
        in_specs=[vmem] * (len(arrays) + 1),
        out_specs=[vmem] * len(arrays),
        out_shape=[pltpu.VMEM(x.shape, x.dtype) for x in arrays],
        input_output_aliases={i: i for i in range(len(arrays))},
        compiler_params=pltpu.CompilerParams(vmem_limit_bytes=MIB),
        name="after",
    )(*[pltpu.with_memory_space_constraint(x, pltpu.VMEM) for x in (*arrays, done)])


def halve_kernel(ahead_ref, behind_ref, left_ref, right_ref, sems):
    half = left_ref.shape[1]
    copies = [
        pltpu.make_async_copy(ahead_ref.at[:, pl.ds(0, half)], left_ref, sems.at[0]),
        pltpu.make_async_copy(behind_ref.at[:, pl.ds(half, half)], right_ref, sems.at[1]),
    ]
    for copy in copies:
        copy.start()
    for copy in copies:
        copy.wait()


def halved(ahead, behind):
    vmem = pl.BlockSpec(memory_space=pltpu.VMEM)
    rows, features = ahead.shape
    return pl.pallas_call(
        halve_kernel,
        in_specs=[vmem] * 2,
        out_specs=[vmem] * 2,
        out_shape=[pltpu.VMEM((rows, features // 2), ahead.dtype)] * 2,
        scratch_shapes=[pltpu.SemaphoreType.DMA((2,))],
        compiler_params=pltpu.CompilerParams(vmem_limit_bytes=MIB),
        name="halved",
    )(*[pltpu.with_memory_space_constraint(x, pltpu.VMEM) for x in (ahead, behind)])


def exchange(x, devices, stride, radix):
    total = x
    for shift in range(1, radix):
        pairs = []
        for d in range(devices):
            digit = d // stride % radix
            pairs.append((d, d + ((digit + shift) % radix - digit) * stride))
        total = total + lax.ppermute(x, "dp", pairs)
    return total


def on_device(ring, attn_out, out_grad, o_weight, head_counts, seq_counts):
    rows, features = out_grad.shape
    slots = attn_out.shape[0]
    devices, last = ring.devices, ring.length // 2
    offsets = [0] + [s * k for k in range(1, last) for s in (-1, 1)] + [last]
    counts = [2] + [4] * (last - 1) + [2]
    table = jnp.asarray(ring.owners(offsets))
    me = lax.axis_index("dp").astype(jnp.int32).reshape(1)
    where = (table, me, head_counts)
    own = live_rows(seq_counts, me, out_grad)
    ats = prepared(*where, attn_out, counts, rows)
    weight = o_weight

    def swap(x):
        return lax.ppermute(x, "dp", ring.swap())

    def forward(x):
        return lax.ppermute(x, "dp", ring.shift(1))

    def backward(x):
        return lax.ppermute(x, "dp", ring.shift(-1))

    arrived = [[own, swap(own)]]
    ahead, behind = forward(own), backward(own)
    w, out, begin = None, None, 0
    for k in range(last):
        w, out, done = phase(where, begin, ats[k], weight, arrived, w, out, slots)
        begin += counts[k]
        ahead, behind = after(done, ahead, behind)
        if k < last - 1:
            arrived = [[ahead, swap(ahead), behind, swap(behind)]]
            if k + 2 == last:
                ahead, behind = halved(ahead, behind)
            ahead, behind = forward(ahead), backward(behind)
        else:
            arrived = [[ahead, swap(ahead)], [behind, swap(behind)]]
    w, squares = phase(where, begin, ats[last], None, arrived, w, None, slots, True)

    stride, late = 1, 0
    while stride < devices:
        radix = min(4, devices // stride)
        squares = exchange(squares, devices, stride, radix)
        if late < 2:
            gs = [group[late : late + 1] for group in arrived]
            out, done = phase(where, begin + late, None, weight, gs, None, out, slots)
        stride, late = stride * radix, late + 1
    return out, scaled(w, squares)


def solution(mesh):
    placed = (
        P("group", "dp"),
        P(("group", "dp"), None),
        P("dp", None),
        P("dp"),
        P(("group", "dp")),
    )
    ring = Ring(mesh.shape["dp"], 2 if mesh.shape["group"] == 2 else 1)
    return jax.shard_map(
        functools.partial(on_device, ring),
        mesh=mesh,
        in_specs=placed,
        out_specs=(P("group", "dp"), P(("group", "dp"), None)),
        check_vma=False,
    )
```

```python
import functools

import jax
import jax.numpy as jnp
import numpy as np
from jax import lax
from jax.experimental import pallas as pl
from jax.experimental.pallas import tpu as pltpu
from jax.sharding import PartitionSpec as P

HEADS = 64
HEAD_DIM = 128
SEQ = 16
TILE = 1024
MIB = 1024 * 1024


class Ring:
    def __init__(self, devices, columns):
        self.devices = devices
        self.length = devices // 2
        rows = self.length // columns
        if columns == 1:
            self.chips = list(range(rows))
        else:
            self.chips = [2 * z for z in range(rows)]
            self.chips += [2 * z + 1 for z in reversed(range(rows))]
        self.position = {chip: p for p, chip in enumerate(self.chips)}

    def device(self, position, core):
        return 2 * self.chips[position % self.length] + core

    def shift(self, step):
        return [
            (self.device(p, core), self.device(p + step, core))
            for p in range(self.length)
            for core in range(2)
        ]

    def swap(self):
        return [(d, d ^ 1) for d in range(self.devices)]

    def owners(self, groups):
        table = []
        for d in range(self.devices):
            p, core = self.position[d // 2], d % 2
            table.append(
                [
                    self.device(p + offset, c)
                    for offsets in groups
                    for c in (core, 1 - core)
                    for offset in offsets
                ]
            )
        return np.array(table, np.int32)


def live_kernel(seqs_ref, me_ref, grad_ref, out_ref, sem):
    load = pltpu.make_async_copy(grad_ref, out_ref, sem)
    load.start()
    load.wait()
    for s in range(out_ref.shape[0] // SEQ):

        @pl.when(s >= seqs_ref[0])
        def _():
            dead = out_ref.at[s * SEQ : (s + 1) * SEQ]
            dead[...] = jnp.zeros_like(dead)


def live_rows(seq_counts, me, out_grad):
    smem = pl.BlockSpec(memory_space=pltpu.SMEM)
    return pl.pallas_call(
        live_kernel,
        in_specs=[smem, smem, pl.BlockSpec(memory_space=pl.ANY)],
        out_specs=pl.BlockSpec(memory_space=pltpu.VMEM),
        out_shape=pltpu.VMEM(out_grad.shape, out_grad.dtype),
        scratch_shapes=[pltpu.SemaphoreType.DMA],
        compiler_params=pltpu.CompilerParams(vmem_limit_bytes=4 * MIB),
        name="live",
    )(seq_counts, me, pltpu.with_memory_space_constraint(out_grad, pltpu.HBM))


def prep_kernel(counts, rows, table_ref, me_ref, heads_ref, a_ref, *refs):
    at_refs, (block_ref, sems) = refs[: len(counts)], refs[len(counts) :]
    width = heads_ref[0] * HEAD_DIM
    copies = []
    for i in range(sum(counts)):
        owner = table_ref[me_ref[0], i]
        copies.append(
            pltpu.make_async_copy(
                a_ref.at[pl.ds(pl.multiple_of(owner * rows, rows), rows)],
                block_ref.at[pl.ds(i * rows, rows)],
                sems.at[i],
            )
        )
        copies[-1].start()
    begin = 0
    for at_ref, count in zip(at_refs, counts):
        for copy in copies[begin : begin + count]:
            copy.wait()
        block = block_ref[begin * rows : (begin + count) * rows, :]
        column = lax.broadcasted_iota(jnp.int32, block.shape, 1)
        at_ref[...] = jnp.where(column < width, block, jnp.zeros_like(block)).T
        begin += count


def prepared(table, me, head_counts, attn_out, counts, rows):
    slots, capacity = attn_out.shape
    vmem = pl.BlockSpec(memory_space=pltpu.VMEM)
    smem = pl.BlockSpec(memory_space=pltpu.SMEM)
    return pl.pallas_call(
        functools.partial(prep_kernel, counts, rows),
        in_specs=[smem, smem, smem, pl.BlockSpec(memory_space=pl.ANY)],
        out_specs=[vmem] * len(counts),
        out_shape=[pltpu.VMEM((capacity, count * rows), jnp.bfloat16) for count in counts],
        scratch_shapes=[
            pltpu.VMEM((slots, capacity), jnp.bfloat16),
            pltpu.SemaphoreType.DMA((sum(counts),)),
        ],
        compiler_params=pltpu.CompilerParams(vmem_limit_bytes=12 * MIB),
        cost_estimate=pl.CostEstimate(
            flops=0, bytes_accessed=4 * slots * capacity, transcendentals=0
        ),
        name="prep",
    )(table, me, head_counts, pltpu.with_memory_space_constraint(attn_out, pltpu.HBM))


def phase_kernel(spec, *refs):
    groups, arrays, w_halves, attn, fresh_w, fresh_out, squares, rows, begin = spec
    refs = list(refs)
    table_ref, me_ref, heads_ref = refs.pop(0), refs.pop(0), refs.pop(0)
    at_ref = refs.pop(0) if w_halves else None
    weight_ref = refs.pop(0) if attn else None
    g_refs = [refs.pop(0) for _ in range(arrays)]
    if w_halves and not fresh_w:
        refs.pop(0)
    before_ref = refs.pop(0) if attn == "last" else None
    if attn in ("whole", "last") and not fresh_out:
        refs.pop(0)
    w_ref = refs.pop(0) if w_halves else None
    total_ref = refs.pop(0) if attn == "first" else None
    out_ref = refs.pop(0) if attn in ("whole", "last") else None
    squares_ref = refs.pop(0)
    if attn in ("whole", "last"):
        total_ref, block_ref, sems = refs
    if attn == "last":
        total_ref[...] = before_ref[...]
    elif attn:
        total_ref[...] = jnp.zeros_like(total_ref)
    squares_ref[...] = jnp.zeros_like(squares_ref)

    def body(half, span, pieces, j, carry):
        here = pl.ds(pl.multiple_of(j * TILE, TILE), TILE)
        there = pl.ds(pl.multiple_of(half * span + j * TILE, TILE), TILE)
        g = [g_refs[i][start : start + count, here] for i, start, count in pieces]
        g = jnp.concatenate(g, axis=0) if len(g) > 1 else g[0]
        if half in w_halves:
            w = jnp.dot(at_ref[...], g, preferred_element_type=jnp.float32)
            if not fresh_w:
                w = w + w_ref[:, there]
            w_ref[:, there] = w
        if squares:
            folded = jnp.sum((w * w).reshape(w.shape[0] // 8, 8, TILE), axis=0)
            total = squares_ref[...]
            for lane in range(0, TILE, 128):
                total = total + folded[:, lane : lane + 128]
            squares_ref[...] = total
        if attn:
            total_ref[...] += lax.dot_general(
                g,
                weight_ref[:, there],
                (((1,), (1,)), ((), ())),
                preferred_element_type=jnp.float32,
            )
        return carry

    for half, span, pieces in groups:
        lax.fori_loop(0, span // TILE, functools.partial(body, half, span, pieces), 0)
    if attn in ("whole", "last"):
        total = total_ref[...]
        column = lax.broadcasted_iota(jnp.int32, total.shape, 1)
        live = column < heads_ref[0] * HEAD_DIM
        block_ref[...] = jnp.where(live, total, 0.0).astype(jnp.bfloat16)
        copies = []
        for i in range(total.shape[0] // rows):
            owner = table_ref[me_ref[0], begin + i]
            copies.append(
                pltpu.make_async_copy(
                    block_ref.at[pl.ds(i * rows, rows)],
                    out_ref.at[pl.ds(pl.multiple_of(owner * rows, rows), rows)],
                    sems.at[i],
                )
            )
            copies[-1].start()
        for copy in copies:
            copy.wait()


def phase(
    where, shapes, begin, groups, at=None, w=None, w_halves=(),
    weight=None, attn=None, before=None, out=None, squares=False,
):
    slots, capacity, features, rows = shapes
    arrays, described = [], []
    for half, pieces in groups:
        placed = []
        for array, start, count in pieces:
            known = [i for i, x in enumerate(arrays) if x is array]
            if not known:
                arrays.append(array)
            placed.append((known[0] if known else len(arrays) - 1, start, count))
        described.append((half, pieces[0][0].shape[1], tuple(placed)))
    height = sum(count for _, _, count in groups[0][1])
    vmem = pl.BlockSpec(memory_space=pltpu.VMEM)
    smem = pl.BlockSpec(memory_space=pltpu.SMEM)
    hbm = pl.BlockSpec(memory_space=pl.ANY)

    args, specs, outs, out_specs, aliases, scratch = [], [], [], [], {}, []

    def add(arg, spec):
        args.append(arg)
        specs.append(spec)

    def add_vmem(arg):
        add(pltpu.with_memory_space_constraint(arg, pltpu.VMEM), vmem)

    for scalar in where:
        add(scalar, smem)
    if w_halves:
        add_vmem(at)
    if attn:
        add_vmem(weight)
    for array in arrays:
        add_vmem(array)
    if w_halves:
        if w is not None:
            aliases[len(args)] = len(outs)
            add_vmem(w)
        outs.append(pltpu.VMEM((capacity, features), jnp.float32))
        out_specs.append(vmem)
    if attn == "last":
        add_vmem(before)
    if attn == "first":
        outs.append(pltpu.VMEM((height, capacity), jnp.float32))
        out_specs.append(vmem)
    elif attn:
        if out is not None:
            aliases[len(args)] = len(outs)
            add(out, hbm)
        outs.append(jax.ShapeDtypeStruct((slots, capacity), jnp.bfloat16))
        out_specs.append(hbm)
        scratch = [
            pltpu.VMEM((height, capacity), jnp.float32),
            pltpu.VMEM((height, capacity), jnp.bfloat16),
            pltpu.SemaphoreType.DMA((height // rows,)),
        ]
    outs.append(pltpu.VMEM((8, 128), jnp.float32))
    out_specs.append(vmem)
    spec = (
        tuple(described), len(arrays), tuple(w_halves), attn, w is None, out is None,
        squares, rows, begin,
    )
    return pl.pallas_call(
        functools.partial(phase_kernel, spec),
        in_specs=specs,
        out_specs=out_specs,
        out_shape=outs,
        scratch_shapes=scratch,
        input_output_aliases=aliases,
        compiler_params=pltpu.CompilerParams(vmem_limit_bytes=12 * MIB),
        cost_estimate=pl.CostEstimate(
            flops=1,
            bytes_accessed=1,
            transcendentals=0,
        ),
        name="phase_" + "w" * len(w_halves) + "_" + str(attn),
    )(*args)


def scale_kernel(parts, w_ref, squares_ref, out_ref, block_ref, sems):
    capacity, features = w_ref.shape
    square_sum = jnp.sum(
        jnp.sum(squares_ref[...], axis=0, keepdims=True), axis=1, keepdims=True
    )
    factor = jnp.minimum(
        1.0, 1.0 / jnp.sqrt(square_sum / (HEADS * HEAD_DIM * features) + 1e-06)
    )
    copies = []
    height = capacity // parts
    for i in range(parts):
        part = pl.ds(i * height, height)
        block_ref[part, :] = (w_ref[part, :] * factor).astype(jnp.bfloat16)
        copies.append(pltpu.make_async_copy(block_ref.at[part], out_ref.at[part], sems.at[i]))
        copies[-1].start()
    for copy in copies:
        copy.wait()


def scaled(w, squares):
    capacity, features = w.shape
    vmem = pl.BlockSpec(memory_space=pltpu.VMEM)
    parts = 8
    return pl.pallas_call(
        functools.partial(scale_kernel, parts),
        in_specs=[vmem, vmem],
        out_specs=pl.BlockSpec(memory_space=pl.ANY),
        out_shape=jax.ShapeDtypeStruct((capacity, features), jnp.bfloat16),
        scratch_shapes=[
            pltpu.VMEM((capacity, features), jnp.bfloat16),
            pltpu.SemaphoreType.DMA((parts,)),
        ],
        compiler_params=pltpu.CompilerParams(vmem_limit_bytes=10 * MIB),
        cost_estimate=pl.CostEstimate(
            flops=capacity * features,
            bytes_accessed=2 * capacity * features,
            transcendentals=0,
        ),
        name="scale",
    )(pltpu.with_memory_space_constraint(w, pltpu.VMEM), squares)


def after(done, *arrays):
    vmem = pl.BlockSpec(memory_space=pltpu.VMEM)
    return pl.pallas_call(
        lambda *refs: None,
        in_specs=[vmem] * (len(arrays) + 1),
        out_specs=[vmem] * len(arrays),
        out_shape=[pltpu.VMEM(x.shape, x.dtype) for x in arrays],
        input_output_aliases={i: i for i in range(len(arrays))},
        compiler_params=pltpu.CompilerParams(vmem_limit_bytes=MIB),
        name="after",
    )(*[pltpu.with_memory_space_constraint(x, pltpu.VMEM) for x in (*arrays, done)])


def split_kernel(plan, first_ref, second_ref, *refs):
    outs, sems = refs[:-1], refs[-1]
    rows, half = first_ref.shape[0], outs[0].shape[1]
    copies = []
    for which, c, out, row in plan:
        source = (first_ref, second_ref)[which].at[:, pl.ds(c * half, half)]
        target = outs[out].at[pl.ds(row * rows, rows)]
        copies.append(pltpu.make_async_copy(source, target, sems.at[len(copies)]))
        copies[-1].start()
    for copy in copies:
        copy.wait()


def split(first, second, join):
    vmem = pl.BlockSpec(memory_space=pltpu.VMEM)
    rows, features = first.shape
    if join:
        plan = [(0, 0, 0, 0), (1, 1, 1, 0)]
        plan += [(which, c, 2 + c, which) for c in range(2) for which in range(2)]
        heights = [rows, rows, 2 * rows, 2 * rows]
    else:
        plan = [(which, c, 2 * which + c, 0) for which in range(2) for c in range(2)]
        heights = [rows] * 4
    return pl.pallas_call(
        functools.partial(split_kernel, plan),
        in_specs=[vmem] * 2,
        out_specs=[vmem] * 4,
        out_shape=[pltpu.VMEM((h, features // 2), first.dtype) for h in heights],
        scratch_shapes=[pltpu.SemaphoreType.DMA((len(plan),))],
        compiler_params=pltpu.CompilerParams(vmem_limit_bytes=MIB),
        name="split",
    )(*[pltpu.with_memory_space_constraint(x, pltpu.VMEM) for x in (first, second)])


def exchange(x, devices, stride, radix):
    total = x
    for shift in range(1, radix):
        pairs = []
        for d in range(devices):
            digit = d // stride % radix
            pairs.append((d, d + ((digit + shift) % radix - digit) * stride))
        total = total + lax.ppermute(x, "dp", pairs)
    return total


def on_device(ring, attn_out, out_grad, o_weight, head_counts, seq_counts):
    rows, features = out_grad.shape
    slots = attn_out.shape[0]
    devices, last = ring.devices, ring.length // 2
    offsets = [[0]] + [[-k, k] for k in range(1, last)] + [[last]]
    counts = [2] + [4] * (last - 1) + [1, 1]
    me = lax.axis_index("dp").astype(jnp.int32).reshape(1)
    where = (jnp.asarray(ring.owners(offsets)), me, head_counts)
    shapes = (slots, o_weight.shape[0], features, rows)
    weight = o_weight

    def swap(x):
        return lax.ppermute(x, "dp", ring.swap())

    def forward(x):
        return lax.ppermute(x, "dp", ring.shift(1))

    def backward(x):
        return lax.ppermute(x, "dp", ring.shift(-1))

    own = live_rows(seq_counts, me, out_grad)
    ahead, behind, other = forward(own), backward(own), swap(own)
    ats = prepared(*where, attn_out, counts, rows)
    w, out, done = phase(
        where, shapes, 0, [(0, [(own, 0, rows), (other, 0, rows)])],
        at=ats[0], w_halves=(0,), weight=weight, attn="whole",
    )
    begin = counts[0]
    for k in range(1, last):
        (ahead,), (behind,) = after(done, ahead), after(done, behind)
        if k < last - 1:
            next_ahead, next_behind = forward(ahead), backward(behind)
        pieces = split(ahead, behind, k == last - 1)
        groups = []
        if k == last - 1:
            next_ahead, next_behind = forward(pieces[0]), backward(pieces[1])
            for c in range(2):
                near = pieces[2 + c]
                groups.append((c, [(x, 0, 2 * rows) for x in (near, swap(near))]))
        else:
            for c in range(2):
                near = [pieces[c], pieces[2 + c]]
                far = [swap(x) for x in near]
                groups.append((c, [(x, 0, rows) for x in near + far]))
        w, done = phase(
            where, shapes, begin, groups[:1], at=ats[k], w=w, w_halves=(0,)
        )
        w, out, done = phase(
            where, shapes, begin, groups, at=ats[k], w=w, w_halves=(1,),
            weight=weight, attn="whole", out=out,
        )
        begin += counts[k]
        ahead, behind = next_ahead, next_behind

    both = after(done, ahead, behind)
    other = [swap(x) for x in both]
    mine = [(c, [(both[c], 0, rows)]) for c in range(2)]
    theirs = [(c, [(other[c], 0, rows)]) for c in range(2)]
    w, done = phase(where, shapes, begin, mine, at=ats[last], w=w, w_halves=(0, 1))
    w, squares = phase(
        where, shapes, begin, theirs, at=ats[last + 1], w=w, w_halves=(0, 1), squares=True
    )

    stride, late = 1, 0
    while stride < devices:
        radix = min(4, devices // stride)
        squares = exchange(squares, devices, stride, radix)
        pieces = [(x[late], 0, rows) for x in (both, other)] if late < 2 else []
        if late == 0:
            before, done = phase(
                where, shapes, begin, [(late, pieces)], weight=weight, attn="first"
            )
            (squares,) = after(done, squares)
        elif late == 1:
            out, done = phase(
                where, shapes, begin, [(late, pieces)], weight=weight, attn="last",
                before=before, out=out,
            )
        stride, late = stride * radix, late + 1
    return out, scaled(w, squares)


def solution(mesh):
    placed = (
        P("group", "dp"),
        P(("group", "dp"), None),
        P("dp", None),
        P("dp"),
        P(("group", "dp")),
    )
    ring = Ring(mesh.shape["dp"], 2 if mesh.shape["group"] == 2 else 1)
    return jax.shard_map(
        functools.partial(on_device, ring),
        mesh=mesh,
        in_specs=placed,
        out_specs=(P("group", "dp"), P(("group", "dp"), None)),
        check_vma=False,
    )
```

```python
import functools

import jax
import jax.numpy as jnp
import numpy as np
from jax import lax
from jax.experimental import pallas as pl
from jax.experimental.pallas import tpu as pltpu
from jax.sharding import PartitionSpec as P

HEADS = 64
HEAD_DIM = 128
SEQ = 16
TILE = 512
CHUNKS = (1024, 1536, 1536)
MIB = 1024 * 1024


class Ring:
    def __init__(self, devices, columns):
        self.devices = devices
        self.length = devices // 2
        rows = self.length // columns
        if columns == 1:
            self.chips = list(range(rows))
        else:
            self.chips = [2 * z for z in range(rows)]
            self.chips += [2 * z + 1 for z in reversed(range(rows))]
        self.position = {chip: p for p, chip in enumerate(self.chips)}

    def device(self, position, core):
        return 2 * self.chips[position % self.length] + core

    def shift(self, step):
        return [
            (self.device(p, core), self.device(p + step, core))
            for p in range(self.length)
            for core in range(2)
        ]

    def across(self):
        return [
            (self.device(p, core), self.device(p + 1 - 2 * core, core))
            for p in range(self.length)
            for core in range(2)
        ]

    def swap(self):
        return [(d, d ^ 1) for d in range(self.devices)]

    def owners(self, groups):
        table = []
        for d in range(self.devices):
            p, core = self.position[d // 2], d % 2
            table.append(
                [
                    self.device(p + offset, c)
                    for offsets in groups
                    for c in (core, 1 - core)
                    for offset in offsets
                ]
            )
        return np.array(table, np.int32)


def live_kernel(seqs_ref, me_ref, grad_ref, out_ref, sem):
    load = pltpu.make_async_copy(grad_ref, out_ref, sem)
    load.start()
    load.wait()
    for s in range(out_ref.shape[0] // SEQ):

        @pl.when(s >= seqs_ref[0])
        def _():
            dead = out_ref.at[s * SEQ : (s + 1) * SEQ]
            dead[...] = jnp.zeros_like(dead)


def live_rows(seq_counts, me, out_grad):
    smem = pl.BlockSpec(memory_space=pltpu.SMEM)
    return pl.pallas_call(
        live_kernel,
        in_specs=[smem, smem, pl.BlockSpec(memory_space=pl.ANY)],
        out_specs=pl.BlockSpec(memory_space=pltpu.VMEM),
        out_shape=pltpu.VMEM(out_grad.shape, out_grad.dtype),
        scratch_shapes=[pltpu.SemaphoreType.DMA],
        compiler_params=pltpu.CompilerParams(vmem_limit_bytes=4 * MIB),
        name="live",
    )(seq_counts, me, pltpu.with_memory_space_constraint(out_grad, pltpu.HBM))


def prep_kernel(core, counts, rows, table_ref, me_ref, heads_ref, own_ref, a_ref, *refs):
    n = len(counts)
    refs = refs[1:] if core else refs[n:]
    at_refs, (block_ref, sems) = refs[-n - 2 : -2], refs[-2:]
    if not core:
        half = refs[0].shape[1]
        copies = [
            pltpu.make_async_copy(own_ref.at[:, pl.ds(i * half, half)], refs[i], sems.at[i])
            for i in range(2)
        ]
        for copy in copies:
            copy.start()
        for copy in copies:
            copy.wait()

    @pl.when(me_ref[0] % 2 == core)
    def _():
        width = heads_ref[0] * HEAD_DIM
        copies = []
        for i in range(sum(counts)):
            owner = table_ref[me_ref[0], i]
            copies.append(
                pltpu.make_async_copy(
                    a_ref.at[pl.ds(pl.multiple_of(owner * rows, rows), rows)],
                    block_ref.at[pl.ds(i * rows, rows)],
                    sems.at[i],
                )
            )
            copies[-1].start()
        begin = 0
        for at_ref, count in zip(at_refs, counts):
            for copy in copies[begin : begin + count]:
                copy.wait()
            block = block_ref[begin * rows : (begin + count) * rows, :]
            column = lax.broadcasted_iota(jnp.int32, block.shape, 1)
            at_ref[...] = jnp.where(column < width, block, jnp.zeros_like(block)).T
            begin += count


def prepared(core, where, own, attn_out, counts, ats=()):
    slots, capacity = attn_out.shape
    rows, features = own.shape
    vmem = pl.BlockSpec(memory_space=pltpu.VMEM)
    smem = pl.BlockSpec(memory_space=pltpu.SMEM)
    owns = [own.shape] if core else [(rows, features // 2)] * 2
    outs = [pltpu.VMEM(shape, own.dtype) for shape in owns]
    outs += [pltpu.VMEM((capacity, count * rows), jnp.bfloat16) for count in counts]
    own, *ats = [pltpu.with_memory_space_constraint(x, pltpu.VMEM) for x in (own, *ats)]
    results = pl.pallas_call(
        functools.partial(prep_kernel, core, counts, rows),
        in_specs=[smem] * 3 + [vmem, pl.BlockSpec(memory_space=pl.ANY)] + [vmem] * len(ats),
        out_specs=[vmem] * len(outs),
        out_shape=outs,
        scratch_shapes=[
            pltpu.VMEM((slots, capacity), jnp.bfloat16),
            pltpu.SemaphoreType.DMA((sum(counts),)),
        ],
        input_output_aliases={3: 0} if core else {5 + i: 2 + i for i in range(len(ats))},
        compiler_params=pltpu.CompilerParams(vmem_limit_bytes=12 * MIB),
        cost_estimate=pl.CostEstimate(flops=1, bytes_accessed=1, transcendentals=0),
        name="prep",
    )(*where, own, pltpu.with_memory_space_constraint(attn_out, pltpu.HBM), *ats)
    return results[: len(owns)], results[len(owns) :]


def phase_kernel(spec, *refs):
    groups, arrays, do_w, attn, fresh_w, fresh_out, squares, rows, begin = spec
    refs = list(refs)
    table_ref, me_ref, heads_ref = refs.pop(0), refs.pop(0), refs.pop(0)
    at_ref = refs.pop(0) if do_w else None
    weight_ref = refs.pop(0) if attn else None
    g_refs = [refs.pop(0) for _ in range(arrays)]
    if do_w and not fresh_w:
        refs.pop(0)
    before_ref = refs.pop(0) if attn == "last" else None
    if attn in ("whole", "last") and not fresh_out:
        refs.pop(0)
    w_ref = refs.pop(0) if do_w else None
    total_ref = refs.pop(0) if attn == "first" else None
    out_ref = refs.pop(0) if attn in ("whole", "last") else None
    squares_ref = refs.pop(0)
    if attn in ("whole", "last"):
        total_ref, block_ref, sems = refs
    if attn == "last":
        total_ref[...] = before_ref[...]
    elif attn:
        total_ref[...] = jnp.zeros_like(total_ref)
    squares_ref[...] = jnp.zeros_like(squares_ref)

    def body(first, column, pieces, j, carry):
        here = pl.ds(pl.multiple_of(column + j * TILE, TILE), TILE)
        there = pl.ds(pl.multiple_of(first + j * TILE, TILE), TILE)
        g = [g_refs[i][start : start + count, here] for i, start, count in pieces]
        g = jnp.concatenate(g, axis=0) if len(g) > 1 else g[0]
        if do_w:
            w = jnp.dot(at_ref[...], g, preferred_element_type=jnp.float32)
            if not fresh_w:
                w = w + w_ref[:, there]
            w_ref[:, there] = w
        if squares:
            folded = jnp.sum((w * w).reshape(w.shape[0] // 8, 8, TILE), axis=0)
            total = squares_ref[...]
            for lane in range(0, TILE, 128):
                total = total + folded[:, lane : lane + 128]
            squares_ref[...] = total
        if attn:
            total_ref[...] += lax.dot_general(
                g,
                weight_ref[:, there],
                (((1,), (1,)), ((), ())),
                preferred_element_type=jnp.float32,
            )
        return carry

    for first, width, column, pieces in groups:
        step = functools.partial(body, first, column, pieces)
        lax.fori_loop(0, width // TILE, step, 0)
    if attn in ("whole", "last"):
        total = total_ref[...]
        column = lax.broadcasted_iota(jnp.int32, total.shape, 1)
        live = column < heads_ref[0] * HEAD_DIM
        block_ref[...] = jnp.where(live, total, 0.0).astype(jnp.bfloat16)
        copies = []
        for i in range(total.shape[0] // rows):
            owner = table_ref[me_ref[0], begin + i]
            copies.append(
                pltpu.make_async_copy(
                    block_ref.at[pl.ds(i * rows, rows)],
                    out_ref.at[pl.ds(pl.multiple_of(owner * rows, rows), rows)],
                    sems.at[i],
                )
            )
            copies[-1].start()
        for copy in copies:
            copy.wait()


def phase(
    where, shapes, begin, groups, at=None, w=None,
    weight=None, attn=None, before=None, out=None, squares=False,
):
    slots, capacity, features, rows = shapes
    do_w = at is not None
    arrays, described = [], []
    for first, width, column, pieces in groups:
        placed = []
        for array, start, count in pieces:
            known = [i for i, x in enumerate(arrays) if x is array]
            if not known:
                arrays.append(array)
            placed.append((known[0] if known else len(arrays) - 1, start, count))
        described.append((first, width, column, tuple(placed)))
    height = sum(count for _, _, count in groups[0][3])
    vmem = pl.BlockSpec(memory_space=pltpu.VMEM)
    smem = pl.BlockSpec(memory_space=pltpu.SMEM)
    hbm = pl.BlockSpec(memory_space=pl.ANY)

    args, specs, outs, out_specs, aliases, scratch = [], [], [], [], {}, []

    def add(arg, spec):
        args.append(arg)
        specs.append(spec)

    def add_vmem(arg):
        add(pltpu.with_memory_space_constraint(arg, pltpu.VMEM), vmem)

    for scalar in where:
        add(scalar, smem)
    if do_w:
        add_vmem(at)
    if attn:
        add_vmem(weight)
    for array in arrays:
        add_vmem(array)
    if do_w:
        if w is not None:
            aliases[len(args)] = len(outs)
            add_vmem(w)
        outs.append(pltpu.VMEM((capacity, features), jnp.float32))
        out_specs.append(vmem)
    if attn == "last":
        add_vmem(before)
    if attn == "first":
        outs.append(pltpu.VMEM((height, capacity), jnp.float32))
        out_specs.append(vmem)
    elif attn:
        if out is not None:
            aliases[len(args)] = len(outs)
            add(out, hbm)
        outs.append(jax.ShapeDtypeStruct((slots, capacity), jnp.bfloat16))
        out_specs.append(hbm)
        scratch = [
            pltpu.VMEM((height, capacity), jnp.float32),
            pltpu.VMEM((height, capacity), jnp.bfloat16),
            pltpu.SemaphoreType.DMA((height // rows,)),
        ]
    outs.append(pltpu.VMEM((8, 128), jnp.float32))
    out_specs.append(vmem)
    spec = (
        tuple(described), len(arrays), do_w, attn, w is None, out is None,
        squares, rows, begin,
    )
    return pl.pallas_call(
        functools.partial(phase_kernel, spec),
        in_specs=specs,
        out_specs=out_specs,
        out_shape=outs,
        scratch_shapes=scratch,
        input_output_aliases=aliases,
        compiler_params=pltpu.CompilerParams(vmem_limit_bytes=12 * MIB),
        cost_estimate=pl.CostEstimate(
            flops=1,
            bytes_accessed=1,
            transcendentals=0,
        ),
        name="phase_" + "w" * do_w + "_" + str(attn),
    )(*args)


def scale_kernel(parts, w_ref, squares_ref, out_ref, block_ref, sems):
    capacity, features = w_ref.shape
    square_sum = jnp.sum(
        jnp.sum(squares_ref[...], axis=0, keepdims=True), axis=1, keepdims=True
    )
    factor = jnp.minimum(
        1.0, 1.0 / jnp.sqrt(square_sum / (HEADS * HEAD_DIM * features) + 1e-06)
    )
    copies = []
    height = capacity // parts
    for i in range(parts):
        part = pl.ds(i * height, height)
        block_ref[part, :] = (w_ref[part, :] * factor).astype(jnp.bfloat16)
        copies.append(pltpu.make_async_copy(block_ref.at[part], out_ref.at[part], sems.at[i]))
        copies[-1].start()
    for copy in copies:
        copy.wait()


def scaled(w, squares):
    capacity, features = w.shape
    vmem = pl.BlockSpec(memory_space=pltpu.VMEM)
    parts = 8
    return pl.pallas_call(
        functools.partial(scale_kernel, parts),
        in_specs=[vmem, vmem],
        out_specs=pl.BlockSpec(memory_space=pl.ANY),
        out_shape=jax.ShapeDtypeStruct((capacity, features), jnp.bfloat16),
        scratch_shapes=[
            pltpu.VMEM((capacity, features), jnp.bfloat16),
            pltpu.SemaphoreType.DMA((parts,)),
        ],
        compiler_params=pltpu.CompilerParams(vmem_limit_bytes=10 * MIB),
        cost_estimate=pl.CostEstimate(
            flops=capacity * features,
            bytes_accessed=2 * capacity * features,
            transcendentals=0,
        ),
        name="scale",
    )(pltpu.with_memory_space_constraint(w, pltpu.VMEM), squares)


def after(done, *arrays):
    vmem = pl.BlockSpec(memory_space=pltpu.VMEM)
    return pl.pallas_call(
        lambda *refs: None,
        in_specs=[vmem] * (len(arrays) + 1),
        out_specs=[vmem] * len(arrays),
        out_shape=[pltpu.VMEM(x.shape, x.dtype) for x in arrays],
        input_output_aliases={i: i for i in range(len(arrays))},
        compiler_params=pltpu.CompilerParams(vmem_limit_bytes=MIB),
        name="after",
    )(*[pltpu.with_memory_space_constraint(x, pltpu.VMEM) for x in (*arrays, done)])


def choose_kernel(me_ref, first_ref, second_ref, done_ref, out_ref, sem):
    for core, ref in enumerate((first_ref, second_ref)):

        @pl.when(me_ref[0] % 2 == core)
        def _():
            copy = pltpu.make_async_copy(ref, out_ref, sem)
            copy.start()
            copy.wait()


def chosen(me, done, first, second):
    vmem = pl.BlockSpec(memory_space=pltpu.VMEM)
    arrays = (first, second, done)
    return pl.pallas_call(
        choose_kernel,
        in_specs=[pl.BlockSpec(memory_space=pltpu.SMEM)] + [vmem] * 3,
        out_specs=vmem,
        out_shape=pltpu.VMEM(first.shape, first.dtype),
        scratch_shapes=[pltpu.SemaphoreType.DMA],
        compiler_params=pltpu.CompilerParams(vmem_limit_bytes=MIB),
        name="chosen",
    )(me, *[pltpu.with_memory_space_constraint(x, pltpu.VMEM) for x in arrays])


def split_kernel(first_ref, second_ref, *refs):
    outs, sems = refs[:-1], refs[-1]
    rows = first_ref.shape[0]
    copies, column = [], 0
    for out in outs:
        width = out.shape[1]
        for i, ref in enumerate((first_ref, second_ref)):
            source = ref.at[:, pl.ds(column, width)]
            target = out.at[pl.ds(i * rows, rows)]
            copies.append(pltpu.make_async_copy(source, target, sems.at[len(copies)]))
            copies[-1].start()
        column += width
    for copy in copies:
        copy.wait()


def split(first, second):
    vmem = pl.BlockSpec(memory_space=pltpu.VMEM)
    rows = first.shape[0]
    return pl.pallas_call(
        split_kernel,
        in_specs=[vmem] * 2,
        out_specs=[vmem] * len(CHUNKS),
        out_shape=[pltpu.VMEM((2 * rows, width), first.dtype) for width in CHUNKS],
        scratch_shapes=[pltpu.SemaphoreType.DMA((2 * len(CHUNKS),))],
        compiler_params=pltpu.CompilerParams(vmem_limit_bytes=MIB),
        name="split",
    )(*[pltpu.with_memory_space_constraint(x, pltpu.VMEM) for x in (first, second)])


def exchange(x, devices, stride, radix):
    total = x
    for shift in range(1, radix):
        pairs = []
        for d in range(devices):
            digit = d // stride % radix
            pairs.append((d, d + ((digit + shift) % radix - digit) * stride))
        total = total + lax.ppermute(x, "dp", pairs)
    return total


def on_device(ring, attn_out, out_grad, o_weight, head_counts, seq_counts):
    rows, features = out_grad.shape
    slots = attn_out.shape[0]
    devices, last = ring.devices, ring.length // 2
    offsets = [[0]] + [[-k, k] for k in range(1, last)] + [[last]]
    counts = [2] + [4] * (last - 1) + [1, 1]
    me = lax.axis_index("dp").astype(jnp.int32).reshape(1)
    where = (jnp.asarray(ring.owners(offsets)), me, head_counts)
    shapes = (slots, o_weight.shape[0], features, rows)
    weight = o_weight

    def send(x, pairs):
        return lax.ppermute(x, "dp", pairs)

    own = live_rows(seq_counts, me, out_grad)
    (own,), ats = prepared(1, where, own, attn_out, counts)
    ahead, behind = send(own, ring.shift(1)), send(own, ring.shift(-1))
    owns, ats = prepared(0, where, own, attn_out, counts, ats)
    half, groups = features // 2, []
    for c, near in enumerate(owns):
        pieces = [(near, 0, rows), (send(near, ring.swap()), 0, rows)]
        groups.append((c * half, half, 0, pieces))
    w, out, done = phase(
        where, shapes, 0, groups, at=ats[0], weight=weight, attn="whole"
    )
    begin = counts[0]
    for k in range(1, last):
        if k < last - 1:
            ahead, behind = after(done, ahead, behind)
            following = send(ahead, ring.shift(1)), send(behind, ring.shift(-1))
        else:
            following = send(chosen(me, done, ahead, behind), ring.across())
        groups, first = [], 0
        for near in split(ahead, behind):
            far = send(near, ring.swap())
            pieces = [(near, 0, 2 * rows), (far, 0, 2 * rows)]
            groups.append((first, near.shape[1], 0, pieces))
            first += near.shape[1]
        w, out, done = phase(
            where, shapes, begin, groups, at=ats[k], w=w,
            weight=weight, attn="whole", out=out,
        )
        begin += counts[k]
        if k < last - 1:
            ahead, behind = following

    (near,) = after(done, following)
    far = send(near, ring.swap())
    w, done = phase(
        where, shapes, begin, [(0, features, 0, [(near, 0, rows)])], at=ats[last], w=w
    )
    w, squares = phase(
        where, shapes, begin, [(0, features, 0, [(far, 0, rows)])], at=ats[last + 1], w=w,
        squares=True,
    )

    stride, late = 1, 0
    while stride < devices:
        radix = min(4, devices // stride)
        squares = exchange(squares, devices, stride, radix)
        groups = [(late * half, half, late * half, [(x, 0, rows) for x in (near, far)])]
        if late == 0:
            before, done = phase(where, shapes, begin, groups, weight=weight, attn="first")
            (squares,) = after(done, squares)
        elif late == 1:
            out, done = phase(
                where, shapes, begin, groups, weight=weight, attn="last",
                before=before, out=out,
            )
        stride, late = stride * radix, late + 1
    return out, scaled(w, squares)


def solution(mesh):
    placed = (
        P("group", "dp"),
        P(("group", "dp"), None),
        P("dp", None),
        P("dp"),
        P(("group", "dp")),
    )
    ring = Ring(mesh.shape["dp"], 2 if mesh.shape["group"] == 2 else 1)
    return jax.shard_map(
        functools.partial(on_device, ring),
        mesh=mesh,
        in_specs=placed,
        out_specs=(P("group", "dp"), P(("group", "dp"), None)),
        check_vma=False,
    )
```

```python
import functools

import jax
import jax.numpy as jnp
import numpy as np
from jax import lax
from jax.experimental import pallas as pl
from jax.experimental.pallas import tpu as pltpu
from jax.sharding import PartitionSpec as P

HEADS = 64
HEAD_DIM = 128
SEQ = 16
TILE = 512
MIB = 1024 * 1024


class Ring:
    def __init__(self, devices, columns):
        self.devices = devices
        self.length = devices // 2
        rows = self.length // columns
        if columns == 1:
            self.chips = list(range(rows))
        else:
            self.chips = [2 * z for z in range(rows)]
            self.chips += [2 * z + 1 for z in reversed(range(rows))]
        self.position = {chip: p for p, chip in enumerate(self.chips)}

    def device(self, position, core):
        return 2 * self.chips[position % self.length] + core

    def along(self):
        return [
            (self.device(p, core), self.device(p + 1 - 2 * core, core))
            for p in range(self.length)
            for core in range(2)
        ]

    def crossing(self):
        return [
            (self.device(p, core), self.device(p - 1 + 2 * core, 1 - core))
            for p in range(self.length)
            for core in range(2)
        ]

    def swap(self):
        return [(d, d ^ 1) for d in range(self.devices)]

    def owners(self):
        table, last = [], self.length // 2
        for d in range(self.devices):
            p, core = self.position[d // 2], d % 2
            row = [d, d ^ 1]
            for k in range(1, last + 1):
                step = k if core else -k
                row += [self.device(p + step, core), self.device(p - step, 1 - core)]
                if k < last:
                    row += [self.device(p + step, 1 - core), self.device(p - step, core)]
            table.append(row)
        return np.array(table, np.int32)


def live_kernel(seqs_ref, me_ref, grad_ref, out_ref, sem):
    load = pltpu.make_async_copy(grad_ref, out_ref, sem)
    load.start()
    load.wait()
    for s in range(out_ref.shape[0] // SEQ):

        @pl.when(s >= seqs_ref[0])
        def _():
            dead = out_ref.at[s * SEQ : (s + 1) * SEQ]
            dead[...] = jnp.zeros_like(dead)


def live_rows(seq_counts, me, out_grad):
    smem = pl.BlockSpec(memory_space=pltpu.SMEM)
    return pl.pallas_call(
        live_kernel,
        in_specs=[smem, smem, pl.BlockSpec(memory_space=pl.ANY)],
        out_specs=pl.BlockSpec(memory_space=pltpu.VMEM),
        out_shape=pltpu.VMEM(out_grad.shape, out_grad.dtype),
        scratch_shapes=[pltpu.SemaphoreType.DMA],
        compiler_params=pltpu.CompilerParams(vmem_limit_bytes=4 * MIB),
        name="live",
    )(seq_counts, me, pltpu.with_memory_space_constraint(out_grad, pltpu.HBM))


def prep_kernel(counts, rows, table_ref, me_ref, heads_ref, own_ref, a_ref, *refs):
    copy_ref, left_ref, right_ref, *at_refs, block_ref, sems, own_sems = refs
    half = left_ref.shape[1]
    owns = [
        pltpu.make_async_copy(own_ref, copy_ref, own_sems.at[0]),
        pltpu.make_async_copy(own_ref.at[:, pl.ds(0, half)], left_ref, own_sems.at[1]),
        pltpu.make_async_copy(own_ref.at[:, pl.ds(half, half)], right_ref, own_sems.at[2]),
    ]
    for copy in owns:
        copy.start()
    width = heads_ref[0] * HEAD_DIM
    copies = []
    for i in range(sum(counts)):
        owner = table_ref[me_ref[0], i]
        copies.append(
            pltpu.make_async_copy(
                a_ref.at[pl.ds(pl.multiple_of(owner * rows, rows), rows)],
                block_ref.at[pl.ds(i * rows, rows)],
                sems.at[i],
            )
        )
        copies[-1].start()
    begin = 0
    for at_ref, count in zip(at_refs, counts):
        for copy in copies[begin : begin + count]:
            copy.wait()
        block = block_ref[begin * rows : (begin + count) * rows, :]
        column = lax.broadcasted_iota(jnp.int32, block.shape, 1)
        at_ref[...] = jnp.where(column < width, block, jnp.zeros_like(block)).T
        begin += count
    for copy in owns:
        copy.wait()


def prepared(where, own, attn_out, counts):
    slots, capacity = attn_out.shape
    rows, features = own.shape
    vmem = pl.BlockSpec(memory_space=pltpu.VMEM)
    smem = pl.BlockSpec(memory_space=pltpu.SMEM)
    outs = [(rows, features), (rows, features // 2), (rows, features // 2)]
    outs += [(capacity, count * rows) for count in counts]
    copy, left, right, *ats = pl.pallas_call(
        functools.partial(prep_kernel, counts, rows),
        in_specs=[smem] * 3 + [vmem, pl.BlockSpec(memory_space=pl.ANY)],
        out_specs=[vmem] * len(outs),
        out_shape=[pltpu.VMEM(shape, jnp.bfloat16) for shape in outs],
        scratch_shapes=[
            pltpu.VMEM((slots, capacity), jnp.bfloat16),
            pltpu.SemaphoreType.DMA((sum(counts),)),
            pltpu.SemaphoreType.DMA((3,)),
        ],
        compiler_params=pltpu.CompilerParams(vmem_limit_bytes=12 * MIB),
        cost_estimate=pl.CostEstimate(flops=1, bytes_accessed=1, transcendentals=0),
        name="prep",
    )(
        *where,
        pltpu.with_memory_space_constraint(own, pltpu.VMEM),
        pltpu.with_memory_space_constraint(attn_out, pltpu.HBM),
    )
    return copy, (left, right), ats


def phase_kernel(spec, *refs):
    groups, arrays, do_w, attn, fresh_w, fresh_out, squares, rows, begin = spec
    refs = list(refs)
    table_ref, me_ref, heads_ref = refs.pop(0), refs.pop(0), refs.pop(0)
    at_ref = refs.pop(0) if do_w else None
    weight_ref = refs.pop(0) if attn else None
    g_refs = [refs.pop(0) for _ in range(arrays)]
    if do_w and not fresh_w:
        refs.pop(0)
    before_ref = refs.pop(0) if attn == "last" else None
    if attn in ("whole", "last") and not fresh_out:
        refs.pop(0)
    w_ref = refs.pop(0) if do_w else None
    total_ref = refs.pop(0) if attn == "first" else None
    out_ref = refs.pop(0) if attn in ("whole", "last") else None
    squares_ref = refs.pop(0)
    if attn in ("whole", "last"):
        total_ref, block_ref, sems = refs
    if attn == "last":
        total_ref[...] = before_ref[...]
    elif attn:
        total_ref[...] = jnp.zeros_like(total_ref)
    squares_ref[...] = jnp.zeros_like(squares_ref)

    def body(first, column, pieces, j, carry):
        here = pl.ds(pl.multiple_of(column + j * TILE, TILE), TILE)
        there = pl.ds(pl.multiple_of(first + j * TILE, TILE), TILE)
        g = [g_refs[i][start : start + count, here] for i, start, count in pieces]
        g = jnp.concatenate(g, axis=0) if len(g) > 1 else g[0]
        if do_w:
            w = jnp.dot(at_ref[...], g, preferred_element_type=jnp.float32)
            if not fresh_w:
                w = w + w_ref[:, there]
            w_ref[:, there] = w
        if squares:
            folded = jnp.sum((w * w).reshape(w.shape[0] // 8, 8, TILE), axis=0)
            total = squares_ref[...]
            for lane in range(0, TILE, 128):
                total = total + folded[:, lane : lane + 128]
            squares_ref[...] = total
        if attn:
            total_ref[...] += lax.dot_general(
                g,
                weight_ref[:, there],
                (((1,), (1,)), ((), ())),
                preferred_element_type=jnp.float32,
            )
        return carry

    for first, width, column, pieces in groups:
        step = functools.partial(body, first, column, pieces)
        lax.fori_loop(0, width // TILE, step, 0)
    if attn in ("whole", "last"):
        total = total_ref[...]
        column = lax.broadcasted_iota(jnp.int32, total.shape, 1)
        live = column < heads_ref[0] * HEAD_DIM
        block_ref[...] = jnp.where(live, total, 0.0).astype(jnp.bfloat16)
        copies = []
        for i in range(total.shape[0] // rows):
            owner = table_ref[me_ref[0], begin + i]
            copies.append(
                pltpu.make_async_copy(
                    block_ref.at[pl.ds(i * rows, rows)],
                    out_ref.at[pl.ds(pl.multiple_of(owner * rows, rows), rows)],
                    sems.at[i],
                )
            )
            copies[-1].start()
        for copy in copies:
            copy.wait()


def phase(
    where, shapes, begin, groups, at=None, w=None,
    weight=None, attn=None, before=None, out=None, squares=False,
):
    slots, capacity, features, rows = shapes
    do_w = at is not None
    arrays, described = [], []
    for first, width, column, pieces in groups:
        placed = []
        for array, start, count in pieces:
            known = [i for i, x in enumerate(arrays) if x is array]
            if not known:
                arrays.append(array)
            placed.append((known[0] if known else len(arrays) - 1, start, count))
        described.append((first, width, column, tuple(placed)))
    height = sum(count for _, _, count in groups[0][3])
    vmem = pl.BlockSpec(memory_space=pltpu.VMEM)
    smem = pl.BlockSpec(memory_space=pltpu.SMEM)
    hbm = pl.BlockSpec(memory_space=pl.ANY)

    args, specs, outs, out_specs, aliases, scratch = [], [], [], [], {}, []

    def add(arg, spec):
        args.append(arg)
        specs.append(spec)

    def add_vmem(arg):
        add(pltpu.with_memory_space_constraint(arg, pltpu.VMEM), vmem)

    for scalar in where:
        add(scalar, smem)
    if do_w:
        add_vmem(at)
    if attn:
        add_vmem(weight)
    for array in arrays:
        add_vmem(array)
    if do_w:
        if w is not None:
            aliases[len(args)] = len(outs)
            add_vmem(w)
        outs.append(pltpu.VMEM((capacity, features), jnp.float32))
        out_specs.append(vmem)
    if attn == "last":
        add_vmem(before)
    if attn == "first":
        outs.append(pltpu.VMEM((height, capacity), jnp.float32))
        out_specs.append(vmem)
    elif attn:
        if out is not None:
            aliases[len(args)] = len(outs)
            add(out, hbm)
        outs.append(jax.ShapeDtypeStruct((slots, capacity), jnp.bfloat16))
        out_specs.append(hbm)
        scratch = [
            pltpu.VMEM((height, capacity), jnp.float32),
            pltpu.VMEM((height, capacity), jnp.bfloat16),
            pltpu.SemaphoreType.DMA((height // rows,)),
        ]
    outs.append(pltpu.VMEM((8, 128), jnp.float32))
    out_specs.append(vmem)
    spec = (
        tuple(described), len(arrays), do_w, attn, w is None, out is None,
        squares, rows, begin,
    )
    return pl.pallas_call(
        functools.partial(phase_kernel, spec),
        in_specs=specs,
        out_specs=out_specs,
        out_shape=outs,
        scratch_shapes=scratch,
        input_output_aliases=aliases,
        compiler_params=pltpu.CompilerParams(vmem_limit_bytes=12 * MIB),
        cost_estimate=pl.CostEstimate(
            flops=1,
            bytes_accessed=1,
            transcendentals=0,
        ),
        name="phase_" + "w" * do_w + "_" + str(attn),
    )(*args)


def scale_kernel(parts, w_ref, squares_ref, out_ref, block_ref, sems):
    capacity, features = w_ref.shape
    square_sum = jnp.sum(
        jnp.sum(squares_ref[...], axis=0, keepdims=True), axis=1, keepdims=True
    )
    factor = jnp.minimum(
        1.0, 1.0 / jnp.sqrt(square_sum / (HEADS * HEAD_DIM * features) + 1e-06)
    )
    copies = []
    height = capacity // parts
    for i in range(parts):
        part = pl.ds(i * height, height)
        block_ref[part, :] = (w_ref[part, :] * factor).astype(jnp.bfloat16)
        copies.append(pltpu.make_async_copy(block_ref.at[part], out_ref.at[part], sems.at[i]))
        copies[-1].start()
    for copy in copies:
        copy.wait()


def scaled(w, squares):
    capacity, features = w.shape
    vmem = pl.BlockSpec(memory_space=pltpu.VMEM)
    parts = 8
    return pl.pallas_call(
        functools.partial(scale_kernel, parts),
        in_specs=[vmem, vmem],
        out_specs=pl.BlockSpec(memory_space=pl.ANY),
        out_shape=jax.ShapeDtypeStruct((capacity, features), jnp.bfloat16),
        scratch_shapes=[
            pltpu.VMEM((capacity, features), jnp.bfloat16),
            pltpu.SemaphoreType.DMA((parts,)),
        ],
        compiler_params=pltpu.CompilerParams(vmem_limit_bytes=10 * MIB),
        cost_estimate=pl.CostEstimate(
            flops=capacity * features,
            bytes_accessed=2 * capacity * features,
            transcendentals=0,
        ),
        name="scale",
    )(pltpu.with_memory_space_constraint(w, pltpu.VMEM), squares)


def after(done, *arrays):
    vmem = pl.BlockSpec(memory_space=pltpu.VMEM)
    return pl.pallas_call(
        lambda *refs: None,
        in_specs=[vmem] * (len(arrays) + 1),
        out_specs=[vmem] * len(arrays),
        out_shape=[pltpu.VMEM(x.shape, x.dtype) for x in arrays],
        input_output_aliases={i: i for i in range(len(arrays))},
        compiler_params=pltpu.CompilerParams(vmem_limit_bytes=MIB),
        name="after",
    )(*[pltpu.with_memory_space_constraint(x, pltpu.VMEM) for x in (*arrays, done)])


def split_kernel(x_ref, left_ref, right_ref, sems):
    half = left_ref.shape[1]
    copies = [
        pltpu.make_async_copy(x_ref.at[:, pl.ds(0, half)], left_ref, sems.at[0]),
        pltpu.make_async_copy(x_ref.at[:, pl.ds(half, half)], right_ref, sems.at[1]),
    ]
    for copy in copies:
        copy.start()
    for copy in copies:
        copy.wait()


def split(x):
    vmem = pl.BlockSpec(memory_space=pltpu.VMEM)
    rows, features = x.shape
    return pl.pallas_call(
        split_kernel,
        in_specs=[vmem],
        out_specs=[vmem] * 2,
        out_shape=[pltpu.VMEM((rows, features // 2), x.dtype)] * 2,
        scratch_shapes=[pltpu.SemaphoreType.DMA((2,))],
        compiler_params=pltpu.CompilerParams(vmem_limit_bytes=MIB),
        name="split",
    )(pltpu.with_memory_space_constraint(x, pltpu.VMEM))


def exchange(x, devices, stride, radix):
    total = x
    for shift in range(1, radix):
        pairs = []
        for d in range(devices):
            digit = d // stride % radix
            pairs.append((d, d + ((digit + shift) % radix - digit) * stride))
        total = total + lax.ppermute(x, "dp", pairs)
    return total


def on_device(ring, attn_out, out_grad, o_weight, head_counts, seq_counts):
    rows, features = out_grad.shape
    slots = attn_out.shape[0]
    devices, last = ring.devices, ring.length // 2
    counts = [2] + [4] * (last - 2) + [2, 2, 1, 1]
    me = lax.axis_index("dp").astype(jnp.int32).reshape(1)
    where = (jnp.asarray(ring.owners()), me, head_counts)
    shapes = (slots, o_weight.shape[0], features, rows)
    weight, half = o_weight, features // 2

    def send(x, pairs):
        return lax.ppermute(x, "dp", pairs)

    def swapped(halves):
        return [send(x, ring.swap()) for x in halves]

    def grouped(*pairs):
        return [(c * half, half, 0, [(x[c], 0, rows) for x in pairs]) for c in range(2)]

    own = live_rows(seq_counts, me, out_grad)
    x = send(own, ring.along())
    own, near, ats = prepared(where, own, attn_out, counts)
    y = send(own, ring.crossing())
    w, out, done = phase(
        where, shapes, 0, grouped(near, swapped(near)), at=ats[0], weight=weight, attn="whole"
    )

    def dots(k, *pairs):
        return phase(
            where, shapes, sum(counts[:k]), grouped(*pairs), at=ats[k], w=w,
            weight=weight, attn="whole", out=out,
        )

    for k in range(1, last):
        (x,) = after(done, x)
        x, near_x = send(x, ring.along()), split(x)
        far_x = swapped(near_x)
        if k == last - 1:
            w, out, done = dots(k, near_x, far_x)
        (y,) = after(done, y)
        y, near_y = send(y, ring.along()) if k < last - 1 else None, split(y)
        far_y = swapped(near_y)
        if k < last - 1:
            w, out, done = dots(k, near_x, far_x, near_y, far_y)
        else:
            w, out, done = dots(k + 1, near_y, far_y)

    (x,) = after(done, x)
    near = split(x)
    far = swapped(near)
    begin = sum(counts[:-2])
    w, done = phase(where, shapes, begin, grouped(near), at=ats[-2], w=w)
    w, squares = phase(where, shapes, begin, grouped(far), at=ats[-1], w=w, squares=True)

    stride, late = 1, 0
    while stride < devices:
        radix = min(4, devices // stride)
        squares = exchange(squares, devices, stride, radix)
        groups = grouped(near, far)[late : late + 1]
        if late == 0:
            before, done = phase(where, shapes, begin, groups, weight=weight, attn="first")
            (squares,) = after(done, squares)
        elif late == 1:
            out, done = phase(
                where, shapes, begin, groups, weight=weight, attn="last",
                before=before, out=out,
            )
        stride, late = stride * radix, late + 1
    return out, scaled(w, squares)


def solution(mesh):
    placed = (
        P("group", "dp"),
        P(("group", "dp"), None),
        P("dp", None),
        P("dp"),
        P(("group", "dp")),
    )
    ring = Ring(mesh.shape["dp"], 2 if mesh.shape["group"] == 2 else 1)
    return jax.shard_map(
        functools.partial(on_device, ring),
        mesh=mesh,
        in_specs=placed,
        out_specs=(P("group", "dp"), P(("group", "dp"), None)),
        check_vma=False,
    )
```

```python
import functools

import jax
import jax.numpy as jnp
import numpy as np
from jax import lax
from jax.experimental import pallas as pl
from jax.experimental.pallas import tpu as pltpu
from jax.sharding import PartitionSpec as P

HEADS = 64
HEAD_DIM = 128
SEQ = 16
TILE = 1024
MIB = 1024 * 1024


class Ring:
    def __init__(self, devices, columns):
        self.devices = devices
        self.length = devices // 2
        rows = self.length // columns
        if columns == 1:
            self.chips = list(range(rows))
        else:
            self.chips = [2 * z for z in range(rows)]
            self.chips += [2 * z + 1 for z in reversed(range(rows))]
        self.position = {chip: p for p, chip in enumerate(self.chips)}

    def device(self, position, core):
        return 2 * self.chips[position % self.length] + core

    def along(self):
        return [
            (self.device(p, core), self.device(p + 1 - 2 * core, core))
            for p in range(self.length)
            for core in range(2)
        ]

    def crossing(self):
        return [
            (self.device(p, core), self.device(p - 1 + 2 * core, 1 - core))
            for p in range(self.length)
            for core in range(2)
        ]

    def swap(self):
        return [(d, d ^ 1) for d in range(self.devices)]

    def owners(self):
        table, last = [], self.length // 2
        for d in range(self.devices):
            p, core = self.position[d // 2], d % 2
            row = [d, d ^ 1]
            for k in range(1, last + 1):
                step = k if core else -k
                row += [self.device(p + step, core), self.device(p - step, 1 - core)]
                if k < last:
                    row += [self.device(p + step, 1 - core), self.device(p - step, core)]
            table.append(row)
        return np.array(table, np.int32)


def live_kernel(seqs_ref, me_ref, grad_ref, out_ref, sem):
    load = pltpu.make_async_copy(grad_ref, out_ref, sem)
    load.start()
    load.wait()
    for s in range(out_ref.shape[0] // SEQ):

        @pl.when(s >= seqs_ref[0])
        def _():
            dead = out_ref.at[s * SEQ : (s + 1) * SEQ]
            dead[...] = jnp.zeros_like(dead)


def live_rows(seq_counts, me, out_grad):
    smem = pl.BlockSpec(memory_space=pltpu.SMEM)
    return pl.pallas_call(
        live_kernel,
        in_specs=[smem, smem, pl.BlockSpec(memory_space=pl.ANY)],
        out_specs=pl.BlockSpec(memory_space=pltpu.VMEM),
        out_shape=pltpu.VMEM(out_grad.shape, out_grad.dtype),
        scratch_shapes=[pltpu.SemaphoreType.DMA],
        compiler_params=pltpu.CompilerParams(vmem_limit_bytes=4 * MIB),
        name="live",
    )(seq_counts, me, pltpu.with_memory_space_constraint(out_grad, pltpu.HBM))


def prep_kernel(spans, rows, table_ref, me_ref, heads_ref, own_ref, a_ref, *refs):
    copy_ref, left_ref, right_ref, *at_refs, block_ref, sems, own_sems = refs
    half = left_ref.shape[1]
    owns = [
        pltpu.make_async_copy(own_ref, copy_ref, own_sems.at[0]),
        pltpu.make_async_copy(own_ref.at[:, pl.ds(0, half)], left_ref, own_sems.at[1]),
        pltpu.make_async_copy(own_ref.at[:, pl.ds(half, half)], right_ref, own_sems.at[2]),
    ]
    for copy in owns:
        copy.start()
    width = heads_ref[0] * HEAD_DIM
    copies = []
    for i in range(block_ref.shape[0] // rows):
        owner = table_ref[me_ref[0], i]
        copies.append(
            pltpu.make_async_copy(
                a_ref.at[pl.ds(pl.multiple_of(owner * rows, rows), rows)],
                block_ref.at[pl.ds(i * rows, rows)],
                sems.at[i],
            )
        )
        copies[-1].start()
    waited = 0
    for at_ref, (begin, count) in zip(at_refs, spans):
        for copy in copies[waited : begin + count]:
            copy.wait()
        waited = max(waited, begin + count)
        block = block_ref[begin * rows : (begin + count) * rows, :]
        column = lax.broadcasted_iota(jnp.int32, block.shape, 1)
        at_ref[...] = jnp.where(column < width, block, jnp.zeros_like(block)).T
    for copy in owns:
        copy.wait()


def prepared(where, own, attn_out, spans):
    slots, capacity = attn_out.shape
    rows, features = own.shape
    vmem = pl.BlockSpec(memory_space=pltpu.VMEM)
    smem = pl.BlockSpec(memory_space=pltpu.SMEM)
    outs = [(rows, features), (rows, features // 2), (rows, features // 2)]
    outs += [(capacity, count * rows) for _, count in spans]
    copy, left, right, *ats = pl.pallas_call(
        functools.partial(prep_kernel, spans, rows),
        in_specs=[smem] * 3 + [vmem, pl.BlockSpec(memory_space=pl.ANY)],
        out_specs=[vmem] * len(outs),
        out_shape=[pltpu.VMEM(shape, jnp.bfloat16) for shape in outs],
        scratch_shapes=[
            pltpu.VMEM((slots, capacity), jnp.bfloat16),
            pltpu.SemaphoreType.DMA((slots // rows,)),
            pltpu.SemaphoreType.DMA((3,)),
        ],
        compiler_params=pltpu.CompilerParams(vmem_limit_bytes=12 * MIB),
        cost_estimate=pl.CostEstimate(flops=1, bytes_accessed=1, transcendentals=0),
        name="prep",
    )(
        *where,
        pltpu.with_memory_space_constraint(own, pltpu.VMEM),
        pltpu.with_memory_space_constraint(attn_out, pltpu.HBM),
    )
    return copy, (left, right), ats


def phase_kernel(spec, *refs):
    groups, arrays, do_w, attn, fresh_w, fresh_out, squares, rows, begin = spec
    refs = list(refs)
    table_ref, me_ref, heads_ref = refs.pop(0), refs.pop(0), refs.pop(0)
    at_ref = refs.pop(0) if do_w else None
    weight_ref = refs.pop(0) if attn else None
    g_refs = [refs.pop(0) for _ in range(arrays)]
    if do_w and not fresh_w:
        refs.pop(0)
    before_ref = refs.pop(0) if attn == "last" else None
    added_ref = refs.pop(0) if squares == "added" else None
    if attn in ("whole", "last") and not fresh_out:
        refs.pop(0)
    w_ref = refs.pop(0) if do_w else None
    total_ref = refs.pop(0) if attn == "first" else None
    out_ref = refs.pop(0) if attn in ("whole", "last") else None
    squares_ref = refs.pop(0)
    if attn in ("whole", "last"):
        total_ref, block_ref, sems = refs
    if attn == "last":
        total_ref[...] = before_ref[...]
    elif attn:
        total_ref[...] = jnp.zeros_like(total_ref)
    if squares == "added":
        squares_ref[...] = added_ref[...]
    else:
        squares_ref[...] = jnp.zeros_like(squares_ref)

    def body(first, column, pieces, j, carry):
        here = pl.ds(pl.multiple_of(column + j * TILE, TILE), TILE)
        there = pl.ds(pl.multiple_of(first + j * TILE, TILE), TILE)
        g = [g_refs[i][start : start + count, here] for i, start, count in pieces]
        g = jnp.concatenate(g, axis=0) if len(g) > 1 else g[0]
        if do_w:
            w = jnp.dot(at_ref[...], g, preferred_element_type=jnp.float32)
            if not fresh_w:
                w = w + w_ref[:, there]
            w_ref[:, there] = w
        if squares:
            folded = jnp.sum((w * w).reshape(w.shape[0] // 8, 8, TILE), axis=0)
            total = squares_ref[...]
            for lane in range(0, TILE, 128):
                total = total + folded[:, lane : lane + 128]
            squares_ref[...] = total
        if attn:
            total_ref[...] += lax.dot_general(
                g,
                weight_ref[:, there],
                (((1,), (1,)), ((), ())),
                preferred_element_type=jnp.float32,
            )
        return carry

    for first, width, column, pieces in groups:
        step = functools.partial(body, first, column, pieces)
        lax.fori_loop(0, width // TILE, step, 0)
    if attn in ("whole", "last"):
        total = total_ref[...]
        column = lax.broadcasted_iota(jnp.int32, total.shape, 1)
        live = column < heads_ref[0] * HEAD_DIM
        block_ref[...] = jnp.where(live, total, 0.0).astype(jnp.bfloat16)
        copies = []
        for i in range(total.shape[0] // rows):
            owner = table_ref[me_ref[0], begin + i]
            copies.append(
                pltpu.make_async_copy(
                    block_ref.at[pl.ds(i * rows, rows)],
                    out_ref.at[pl.ds(pl.multiple_of(owner * rows, rows), rows)],
                    sems.at[i],
                )
            )
            copies[-1].start()
        for copy in copies:
            copy.wait()


def phase(
    where, shapes, begin, groups, at=None, w=None,
    weight=None, attn=None, before=None, out=None, squares=None, added=None,
):
    slots, capacity, features, rows = shapes
    do_w = at is not None
    arrays, described = [], []
    for first, width, column, pieces in groups:
        placed = []
        for array, start, count in pieces:
            known = [i for i, x in enumerate(arrays) if x is array]
            if not known:
                arrays.append(array)
            placed.append((known[0] if known else len(arrays) - 1, start, count))
        described.append((first, width, column, tuple(placed)))
    height = sum(count for _, _, count in groups[0][3])
    vmem = pl.BlockSpec(memory_space=pltpu.VMEM)
    smem = pl.BlockSpec(memory_space=pltpu.SMEM)
    hbm = pl.BlockSpec(memory_space=pl.ANY)

    args, specs, outs, out_specs, aliases, scratch = [], [], [], [], {}, []

    def add(arg, spec):
        args.append(arg)
        specs.append(spec)

    def add_vmem(arg):
        add(pltpu.with_memory_space_constraint(arg, pltpu.VMEM), vmem)

    for scalar in where:
        add(scalar, smem)
    if do_w:
        add_vmem(at)
    if attn:
        add_vmem(weight)
    for array in arrays:
        add_vmem(array)
    if do_w:
        if w is not None:
            aliases[len(args)] = len(outs)
            add_vmem(w)
        outs.append(pltpu.VMEM((capacity, features), jnp.float32))
        out_specs.append(vmem)
    if attn == "last":
        add_vmem(before)
    if squares == "added":
        add_vmem(added)
    if attn == "first":
        outs.append(pltpu.VMEM((height, capacity), jnp.float32))
        out_specs.append(vmem)
    elif attn:
        if out is not None:
            aliases[len(args)] = len(outs)
            add(out, hbm)
        outs.append(jax.ShapeDtypeStruct((slots, capacity), jnp.bfloat16))
        out_specs.append(hbm)
        scratch = [
            pltpu.VMEM((height, capacity), jnp.float32),
            pltpu.VMEM((height, capacity), jnp.bfloat16),
            pltpu.SemaphoreType.DMA((height // rows,)),
        ]
    outs.append(pltpu.VMEM((8, 128), jnp.float32))
    out_specs.append(vmem)
    spec = (
        tuple(described), len(arrays), do_w, attn, w is None, out is None,
        squares, rows, begin,
    )
    return pl.pallas_call(
        functools.partial(phase_kernel, spec),
        in_specs=specs,
        out_specs=out_specs,
        out_shape=outs,
        scratch_shapes=scratch,
        input_output_aliases=aliases,
        compiler_params=pltpu.CompilerParams(vmem_limit_bytes=12 * MIB),
        cost_estimate=pl.CostEstimate(
            flops=1,
            bytes_accessed=1,
            transcendentals=0,
        ),
        name="phase_" + "w" * do_w + "_" + str(attn),
    )(*args)


def scale_kernel(parts, w_ref, squares_ref, out_ref, block_ref, sems):
    capacity, features = w_ref.shape
    square_sum = jnp.sum(
        jnp.sum(squares_ref[...], axis=0, keepdims=True), axis=1, keepdims=True
    )
    factor = jnp.minimum(
        1.0, 1.0 / jnp.sqrt(square_sum / (HEADS * HEAD_DIM * features) + 1e-06)
    )
    copies = []
    height = capacity // parts
    for i in range(parts):
        part = pl.ds(i * height, height)
        block_ref[part, :] = (w_ref[part, :] * factor).astype(jnp.bfloat16)
        copies.append(pltpu.make_async_copy(block_ref.at[part], out_ref.at[part], sems.at[i]))
        copies[-1].start()
    for copy in copies:
        copy.wait()


def scaled(w, squares):
    capacity, features = w.shape
    vmem = pl.BlockSpec(memory_space=pltpu.VMEM)
    parts = 8
    return pl.pallas_call(
        functools.partial(scale_kernel, parts),
        in_specs=[vmem, vmem],
        out_specs=pl.BlockSpec(memory_space=pl.ANY),
        out_shape=jax.ShapeDtypeStruct((capacity, features), jnp.bfloat16),
        scratch_shapes=[
            pltpu.VMEM((capacity, features), jnp.bfloat16),
            pltpu.SemaphoreType.DMA((parts,)),
        ],
        compiler_params=pltpu.CompilerParams(vmem_limit_bytes=10 * MIB),
        cost_estimate=pl.CostEstimate(
            flops=capacity * features,
            bytes_accessed=2 * capacity * features,
            transcendentals=0,
        ),
        name="scale",
    )(pltpu.with_memory_space_constraint(w, pltpu.VMEM), squares)


def after(done, *arrays):
    vmem = pl.BlockSpec(memory_space=pltpu.VMEM)
    return pl.pallas_call(
        lambda *refs: None,
        in_specs=[vmem] * (len(arrays) + 1),
        out_specs=[vmem] * len(arrays),
        out_shape=[pltpu.VMEM(x.shape, x.dtype) for x in arrays],
        input_output_aliases={i: i for i in range(len(arrays))},
        compiler_params=pltpu.CompilerParams(vmem_limit_bytes=MIB),
        name="after",
    )(*[pltpu.with_memory_space_constraint(x, pltpu.VMEM) for x in (*arrays, done)])


def split_kernel(x_ref, left_ref, right_ref, sems):
    half = left_ref.shape[1]
    copies = [
        pltpu.make_async_copy(x_ref.at[:, pl.ds(0, half)], left_ref, sems.at[0]),
        pltpu.make_async_copy(x_ref.at[:, pl.ds(half, half)], right_ref, sems.at[1]),
    ]
    for copy in copies:
        copy.start()
    for copy in copies:
        copy.wait()


def split(x):
    vmem = pl.BlockSpec(memory_space=pltpu.VMEM)
    rows, features = x.shape
    return pl.pallas_call(
        split_kernel,
        in_specs=[vmem],
        out_specs=[vmem] * 2,
        out_shape=[pltpu.VMEM((rows, features // 2), x.dtype)] * 2,
        scratch_shapes=[pltpu.SemaphoreType.DMA((2,))],
        compiler_params=pltpu.CompilerParams(vmem_limit_bytes=MIB),
        name="split",
    )(pltpu.with_memory_space_constraint(x, pltpu.VMEM))


def exchange(x, devices, stride, radix):
    total = x
    for shift in range(1, radix):
        pairs = []
        for d in range(devices):
            digit = d // stride % radix
            pairs.append((d, d + ((digit + shift) % radix - digit) * stride))
        total = total + lax.ppermute(x, "dp", pairs)
    return total


def on_device(ring, attn_out, out_grad, o_weight, head_counts, seq_counts):
    rows, features = out_grad.shape
    slots = attn_out.shape[0]
    devices, last = ring.devices, ring.length // 2
    steps = 2 * last
    spans = [(2 * i, 2) for i in range(steps)]
    me = lax.axis_index("dp").astype(jnp.int32).reshape(1)
    where = (jnp.asarray(ring.owners()), me, head_counts)
    shapes = (slots, o_weight.shape[0], features, rows)
    weight, half = o_weight, features // 2

    def send(x, pairs):
        return lax.ppermute(x, "dp", pairs)

    def swapped(halves):
        return [send(x, ring.swap()) for x in halves]

    def grouped(*pairs):
        return [
            (c * half, half, 0, [(x[c], 0, rows) for x in pairs])
            for c in range(min(len(x) for x in pairs))
        ]

    own = live_rows(seq_counts, me, out_grad)
    x = send(own, ring.along())
    own, near, ats = prepared(where, own, attn_out, spans)
    y = send(own, ring.crossing())
    w, out, done = phase(
        where, shapes, 0, grouped(near, swapped(near)), at=ats[0], weight=weight, attn="whole"
    )

    for k in range(1, last):
        (x,) = after(done, x)
        x, near_x = send(x, ring.along()), split(x)
        far_x = swapped(near_x)
        i, groups = 2 * k - 1, grouped(near_x, far_x)
        w, done = phase(where, shapes, 2 * i, groups, at=ats[i], w=w)
        (y,) = after(done, y)
        y, near_y = send(y, ring.along()) if k < last - 1 else None, split(y)
        far_y = swapped(near_y)
        i, groups = 2 * k, grouped(near_y, far_y)
        w, added = phase(where, shapes, 2 * i, groups, at=ats[i], w=w)
        groups = grouped(near_x, far_x, near_y, far_y)
        out, done = phase(
            where, shapes, 2 * i - 2, groups, weight=weight, attn="whole", out=out
        )

    x, _ = after(done, x, added)
    near = split(x)
    far = swapped(near)
    begin, groups = 2 * steps - 2, grouped(near, far)
    w, squares = phase(where, shapes, begin, groups[:1], at=ats[-1], w=w, squares="new")
    w, squares = phase(
        where, shapes, begin, groups[1:], at=ats[-1], w=w, squares="added", added=squares
    )

    stride, late = 1, 0
    while stride < devices:
        radix = min(4, devices // stride)
        squares = exchange(squares, devices, stride, radix)
        groups = grouped(near, far)[late : late + 1]
        if late == 0:
            before, done = phase(where, shapes, begin, groups, weight=weight, attn="first")
            (squares,) = after(done, squares)
        elif late == 1:
            out, done = phase(
                where, shapes, begin, groups, weight=weight, attn="last",
                before=before, out=out,
            )
        stride, late = stride * radix, late + 1
    return out, scaled(w, squares)


def solution(mesh):
    placed = (
        P("group", "dp"),
        P(("group", "dp"), None),
        P("dp", None),
        P("dp"),
        P(("group", "dp")),
    )
    ring = Ring(mesh.shape["dp"], 2 if mesh.shape["group"] == 2 else 1)
    return jax.shard_map(
        functools.partial(on_device, ring),
        mesh=mesh,
        in_specs=placed,
        out_specs=(P("group", "dp"), P(("group", "dp"), None)),
        check_vma=False,
    )
```

```python
import functools

import jax
import jax.numpy as jnp
import numpy as np
from jax import lax
from jax.experimental import pallas as pl
from jax.experimental.pallas import tpu as pltpu
from jax.sharding import PartitionSpec as P

HEADS = 64
HEAD_DIM = 128
SEQ = 16
TILE = 1024
MIB = 1024 * 1024


class Ring:
    def __init__(self, devices, columns):
        self.devices = devices
        self.length = devices // 2
        rows = self.length // columns
        if columns == 1:
            self.chips = list(range(rows))
        else:
            self.chips = [2 * z for z in range(rows)]
            self.chips += [2 * z + 1 for z in reversed(range(rows))]
        self.position = {chip: p for p, chip in enumerate(self.chips)}

    def device(self, position, core):
        return 2 * self.chips[position % self.length] + core

    def along(self):
        return [
            (self.device(p, core), self.device(p + 1 - 2 * core, core))
            for p in range(self.length)
            for core in range(2)
        ]

    def crossing(self):
        return [
            (self.device(p, core), self.device(p - 1 + 2 * core, 1 - core))
            for p in range(self.length)
            for core in range(2)
        ]

    def swap(self):
        return [(d, d ^ 1) for d in range(self.devices)]

    def owners(self):
        table, last = [], self.length // 2
        for d in range(self.devices):
            p, core = self.position[d // 2], d % 2
            row = [d, d ^ 1]
            for k in range(1, last + 1):
                step = k if core else -k
                row += [self.device(p + step, core), self.device(p - step, 1 - core)]
                if k < last:
                    row += [self.device(p + step, 1 - core), self.device(p - step, core)]
            table.append(row)
        return np.array(table, np.int32)


def live_kernel(seqs_ref, me_ref, grad_ref, out_ref, sem):
    load = pltpu.make_async_copy(grad_ref, out_ref, sem)
    load.start()
    load.wait()
    for s in range(out_ref.shape[0] // SEQ):

        @pl.when(s >= seqs_ref[0])
        def _():
            dead = out_ref.at[s * SEQ : (s + 1) * SEQ]
            dead[...] = jnp.zeros_like(dead)


def live_rows(seq_counts, me, out_grad):
    smem = pl.BlockSpec(memory_space=pltpu.SMEM)
    return pl.pallas_call(
        live_kernel,
        in_specs=[smem, smem, pl.BlockSpec(memory_space=pl.ANY)],
        out_specs=pl.BlockSpec(memory_space=pltpu.VMEM),
        out_shape=pltpu.VMEM(out_grad.shape, out_grad.dtype),
        scratch_shapes=[pltpu.SemaphoreType.DMA],
        compiler_params=pltpu.CompilerParams(vmem_limit_bytes=4 * MIB),
        name="live",
    )(seq_counts, me, pltpu.with_memory_space_constraint(out_grad, pltpu.HBM))


def prep_kernel(spans, rows, table_ref, me_ref, heads_ref, own_ref, a_ref, *refs):
    copy_ref, left_ref, right_ref, *at_refs, block_ref, sems, own_sems = refs
    half = left_ref.shape[1]
    owns = [
        pltpu.make_async_copy(own_ref, copy_ref, own_sems.at[0]),
        pltpu.make_async_copy(own_ref.at[:, pl.ds(0, half)], left_ref, own_sems.at[1]),
        pltpu.make_async_copy(own_ref.at[:, pl.ds(half, half)], right_ref, own_sems.at[2]),
    ]
    for copy in owns:
        copy.start()
    width = heads_ref[0] * HEAD_DIM
    copies = []
    for i in range(block_ref.shape[0] // rows):
        owner = table_ref[me_ref[0], i]
        copies.append(
            pltpu.make_async_copy(
                a_ref.at[pl.ds(pl.multiple_of(owner * rows, rows), rows)],
                block_ref.at[pl.ds(i * rows, rows)],
                sems.at[i],
            )
        )
        copies[-1].start()
    waited = 0
    for at_ref, (begin, count) in zip(at_refs, spans):
        for copy in copies[waited : begin + count]:
            copy.wait()
        waited = max(waited, begin + count)
        block = block_ref[begin * rows : (begin + count) * rows, :]
        column = lax.broadcasted_iota(jnp.int32, block.shape, 1)
        at_ref[...] = jnp.where(column < width, block, jnp.zeros_like(block)).T
    for copy in owns:
        copy.wait()


def prepared(where, own, attn_out, spans):
    slots, capacity = attn_out.shape
    rows, features = own.shape
    vmem = pl.BlockSpec(memory_space=pltpu.VMEM)
    smem = pl.BlockSpec(memory_space=pltpu.SMEM)
    outs = [(rows, features), (rows, features // 2), (rows, features // 2)]
    outs += [(capacity, count * rows) for _, count in spans]
    copy, left, right, *ats = pl.pallas_call(
        functools.partial(prep_kernel, spans, rows),
        in_specs=[smem] * 3 + [vmem, pl.BlockSpec(memory_space=pl.ANY)],
        out_specs=[vmem] * len(outs),
        out_shape=[pltpu.VMEM(shape, jnp.bfloat16) for shape in outs],
        scratch_shapes=[
            pltpu.VMEM((slots, capacity), jnp.bfloat16),
            pltpu.SemaphoreType.DMA((slots // rows,)),
            pltpu.SemaphoreType.DMA((3,)),
        ],
        compiler_params=pltpu.CompilerParams(vmem_limit_bytes=12 * MIB),
        cost_estimate=pl.CostEstimate(flops=1, bytes_accessed=1, transcendentals=0),
        name="prep",
    )(
        *where,
        pltpu.with_memory_space_constraint(own, pltpu.VMEM),
        pltpu.with_memory_space_constraint(attn_out, pltpu.HBM),
    )
    return copy, (left, right), ats


def phase_kernel(spec, *refs):
    groups, arrays, do_w, w_from, attn, fresh_w, fresh_out, squares, rows, begin = spec
    refs = list(refs)
    table_ref, me_ref, heads_ref = refs.pop(0), refs.pop(0), refs.pop(0)
    at_ref = refs.pop(0) if do_w else None
    weight_ref = refs.pop(0) if attn else None
    g_refs = [refs.pop(0) for _ in range(arrays)]
    if do_w and not fresh_w:
        refs.pop(0)
    before_ref = refs.pop(0) if attn == "last" else None
    added_ref = refs.pop(0) if squares == "added" else None
    if attn in ("whole", "last") and not fresh_out:
        refs.pop(0)
    w_ref = refs.pop(0) if do_w else None
    total_ref = refs.pop(0) if attn == "first" else None
    out_ref = refs.pop(0) if attn in ("whole", "last") else None
    squares_ref = refs.pop(0)
    if attn in ("whole", "last"):
        total_ref, block_ref, sems = refs
    if attn == "last":
        total_ref[...] = before_ref[...]
    elif attn:
        total_ref[...] = jnp.zeros_like(total_ref)
    if squares == "added":
        squares_ref[...] = added_ref[...]
    else:
        squares_ref[...] = jnp.zeros_like(squares_ref)

    def body(first, column, pieces, j, carry):
        here = pl.ds(pl.multiple_of(column + j * TILE, TILE), TILE)
        there = pl.ds(pl.multiple_of(first + j * TILE, TILE), TILE)
        g = [g_refs[i][start : start + count, here] for i, start, count in pieces]
        if do_w:
            fresh = jnp.concatenate(g[w_from:], axis=0) if len(g) > w_from + 1 else g[-1]
            w = jnp.dot(at_ref[...], fresh, preferred_element_type=jnp.float32)
            if not fresh_w:
                w = w + w_ref[:, there]
            w_ref[:, there] = w
        if squares:
            folded = jnp.sum((w * w).reshape(w.shape[0] // 8, 8, TILE), axis=0)
            total = squares_ref[...]
            for lane in range(0, TILE, 128):
                total = total + folded[:, lane : lane + 128]
            squares_ref[...] = total
        if attn:
            total_ref[...] += lax.dot_general(
                jnp.concatenate(g, axis=0),
                weight_ref[:, there],
                (((1,), (1,)), ((), ())),
                preferred_element_type=jnp.float32,
            )
        return carry

    for first, width, column, pieces in groups:
        step = functools.partial(body, first, column, pieces)
        lax.fori_loop(0, width // TILE, step, 0)
    if attn in ("whole", "last"):
        total = total_ref[...]
        column = lax.broadcasted_iota(jnp.int32, total.shape, 1)
        live = column < heads_ref[0] * HEAD_DIM
        block_ref[...] = jnp.where(live, total, 0.0).astype(jnp.bfloat16)
        copies = []
        for i in range(total.shape[0] // rows):
            owner = table_ref[me_ref[0], begin + i]
            copies.append(
                pltpu.make_async_copy(
                    block_ref.at[pl.ds(i * rows, rows)],
                    out_ref.at[pl.ds(pl.multiple_of(owner * rows, rows), rows)],
                    sems.at[i],
                )
            )
            copies[-1].start()
        for copy in copies:
            copy.wait()


def phase(
    where, shapes, begin, groups, at=None, w=None,
    weight=None, attn=None, before=None, out=None, squares=None, added=None,
    w_from=0,
):
    slots, capacity, features, rows = shapes
    do_w = at is not None
    arrays, described = [], []
    for first, width, column, pieces in groups:
        placed = []
        for array, start, count in pieces:
            known = [i for i, x in enumerate(arrays) if x is array]
            if not known:
                arrays.append(array)
            placed.append((known[0] if known else len(arrays) - 1, start, count))
        described.append((first, width, column, tuple(placed)))
    height = sum(count for _, _, count in groups[0][3])
    vmem = pl.BlockSpec(memory_space=pltpu.VMEM)
    smem = pl.BlockSpec(memory_space=pltpu.SMEM)
    hbm = pl.BlockSpec(memory_space=pl.ANY)

    args, specs, outs, out_specs, aliases, scratch = [], [], [], [], {}, []

    def add(arg, spec):
        args.append(arg)
        specs.append(spec)

    def add_vmem(arg):
        add(pltpu.with_memory_space_constraint(arg, pltpu.VMEM), vmem)

    for scalar in where:
        add(scalar, smem)
    if do_w:
        add_vmem(at)
    if attn:
        add_vmem(weight)
    for array in arrays:
        add_vmem(array)
    if do_w:
        if w is not None:
            aliases[len(args)] = len(outs)
            add_vmem(w)
        outs.append(pltpu.VMEM((capacity, features), jnp.float32))
        out_specs.append(vmem)
    if attn == "last":
        add_vmem(before)
    if squares == "added":
        add_vmem(added)
    if attn == "first":
        outs.append(pltpu.VMEM((height, capacity), jnp.float32))
        out_specs.append(vmem)
    elif attn:
        if out is not None:
            aliases[len(args)] = len(outs)
            add(out, hbm)
        outs.append(jax.ShapeDtypeStruct((slots, capacity), jnp.bfloat16))
        out_specs.append(hbm)
        scratch = [
            pltpu.VMEM((height, capacity), jnp.float32),
            pltpu.VMEM((height, capacity), jnp.bfloat16),
            pltpu.SemaphoreType.DMA((height // rows,)),
        ]
    outs.append(pltpu.VMEM((8, 128), jnp.float32))
    out_specs.append(vmem)
    spec = (
        tuple(described), len(arrays), do_w, w_from, attn, w is None, out is None,
        squares, rows, begin,
    )
    return pl.pallas_call(
        functools.partial(phase_kernel, spec),
        in_specs=specs,
        out_specs=out_specs,
        out_shape=outs,
        scratch_shapes=scratch,
        input_output_aliases=aliases,
        compiler_params=pltpu.CompilerParams(vmem_limit_bytes=12 * MIB),
        cost_estimate=pl.CostEstimate(
            flops=1,
            bytes_accessed=1,
            transcendentals=0,
        ),
        name="phase_" + "w" * do_w + "_" + str(attn),
    )(*args)


def scale_kernel(parts, w_ref, squares_ref, out_ref, block_ref, sems):
    capacity, features = w_ref.shape
    square_sum = jnp.sum(
        jnp.sum(squares_ref[...], axis=0, keepdims=True), axis=1, keepdims=True
    )
    factor = jnp.minimum(
        1.0, 1.0 / jnp.sqrt(square_sum / (HEADS * HEAD_DIM * features) + 1e-06)
    )
    copies = []
    height = capacity // parts
    for i in range(parts):
        part = pl.ds(i * height, height)
        block_ref[part, :] = (w_ref[part, :] * factor).astype(jnp.bfloat16)
        copies.append(pltpu.make_async_copy(block_ref.at[part], out_ref.at[part], sems.at[i]))
        copies[-1].start()
    for copy in copies:
        copy.wait()


def scaled(w, squares):
    capacity, features = w.shape
    vmem = pl.BlockSpec(memory_space=pltpu.VMEM)
    parts = 8
    return pl.pallas_call(
        functools.partial(scale_kernel, parts),
        in_specs=[vmem, vmem],
        out_specs=pl.BlockSpec(memory_space=pl.ANY),
        out_shape=jax.ShapeDtypeStruct((capacity, features), jnp.bfloat16),
        scratch_shapes=[
            pltpu.VMEM((capacity, features), jnp.bfloat16),
            pltpu.SemaphoreType.DMA((parts,)),
        ],
        compiler_params=pltpu.CompilerParams(vmem_limit_bytes=10 * MIB),
        cost_estimate=pl.CostEstimate(
            flops=capacity * features,
            bytes_accessed=2 * capacity * features,
            transcendentals=0,
        ),
        name="scale",
    )(pltpu.with_memory_space_constraint(w, pltpu.VMEM), squares)


def after(done, *arrays):
    vmem = pl.BlockSpec(memory_space=pltpu.VMEM)
    return pl.pallas_call(
        lambda *refs: None,
        in_specs=[vmem] * (len(arrays) + 1),
        out_specs=[vmem] * len(arrays),
        out_shape=[pltpu.VMEM(x.shape, x.dtype) for x in arrays],
        input_output_aliases={i: i for i in range(len(arrays))},
        compiler_params=pltpu.CompilerParams(vmem_limit_bytes=MIB),
        name="after",
    )(*[pltpu.with_memory_space_constraint(x, pltpu.VMEM) for x in (*arrays, done)])


def split_kernel(x_ref, left_ref, right_ref, sems):
    half = left_ref.shape[1]
    copies = [
        pltpu.make_async_copy(x_ref.at[:, pl.ds(0, half)], left_ref, sems.at[0]),
        pltpu.make_async_copy(x_ref.at[:, pl.ds(half, half)], right_ref, sems.at[1]),
    ]
    for copy in copies:
        copy.start()
    for copy in copies:
        copy.wait()


def split(x):
    vmem = pl.BlockSpec(memory_space=pltpu.VMEM)
    rows, features = x.shape
    return pl.pallas_call(
        split_kernel,
        in_specs=[vmem],
        out_specs=[vmem] * 2,
        out_shape=[pltpu.VMEM((rows, features // 2), x.dtype)] * 2,
        scratch_shapes=[pltpu.SemaphoreType.DMA((2,))],
        compiler_params=pltpu.CompilerParams(vmem_limit_bytes=MIB),
        name="split",
    )(pltpu.with_memory_space_constraint(x, pltpu.VMEM))


def rounds(devices):
    bits = [1 << i for i in range(devices.bit_length() - 1)]
    if len(bits) >= 4:
        bits = bits[1:3] + [bits[0]] + bits[3:]
    masks = []
    while bits:
        pair, bits = bits[:2], bits[2:]
        masks.append(pair + [sum(pair)] if len(pair) == 2 else pair)
    return masks


def exchange(x, devices, masks):
    total = x
    for mask in masks:
        total = total + lax.ppermute(x, "dp", [(d, d ^ mask) for d in range(devices)])
    return total


def on_device(ring, attn_out, out_grad, o_weight, head_counts, seq_counts):
    rows, features = out_grad.shape
    slots = attn_out.shape[0]
    devices, last = ring.devices, ring.length // 2
    steps = 2 * last
    spans = [(0, 2)]
    for k in range(1, last):
        joint = k < last - 1
        spans += [(4 * k - 2, 4), None] if joint else [(4 * k - 2, 2), (4 * k, 2)]
    spans += [(2 * steps - 2, 1), (2 * steps - 1, 1)]
    me = lax.axis_index("dp").astype(jnp.int32).reshape(1)
    where = (jnp.asarray(ring.owners()), me, head_counts)
    shapes = (slots, o_weight.shape[0], features, rows)
    weight, half = o_weight, features // 2

    def send(x, pairs):
        return lax.ppermute(x, "dp", pairs)

    def swapped(halves):
        return [send(x, ring.swap()) for x in halves]

    def grouped(*pairs):
        return [
            (c * half, half, 0, [(x[c], 0, rows) for x in pairs])
            for c in range(min(len(x) for x in pairs))
        ]

    own = live_rows(seq_counts, me, out_grad)
    x = send(own, ring.along())
    own, near, ats = prepared(where, own, attn_out, [x for x in spans if x])
    ats = [ats.pop(0) if x else None for x in spans]
    y = send(own, ring.crossing())
    w, out, done = phase(
        where, shapes, 0, grouped(near, swapped(near)), at=ats[0], weight=weight, attn="whole"
    )

    for k in range(1, last):
        (x,) = after(done, x)
        x, near_x = send(x, ring.along()), split(x)
        far_x = swapped(near_x)
        i = 2 * k - 1
        if k == last - 1:
            held = held + [near_x, far_x]
            w, out, done = phase(
                where, shapes, 2 * (i + 1) - len(held), grouped(*held), at=ats[i], w=w,
                w_from=len(held) - 2, weight=weight, attn="whole", out=out,
            )
        (y,) = after(done, y)
        y, near_y = send(y, ring.along()) if k < last - 1 else None, split(y)
        far_y = swapped(near_y)
        groups = grouped(near_x, far_x, near_y, far_y)
        if k == last - 1:
            w, out, done = phase(
                where, shapes, 2 * (i + 1), grouped(near_y, far_y), at=ats[i + 1], w=w,
                weight=weight, attn="whole", out=out,
            )
        elif k == last - 2:
            held = [near_x, far_x, near_y, far_y]
            w, done = phase(where, shapes, 2 * i, groups, at=ats[i], w=w)
        else:
            w, out, done = phase(
                where, shapes, 2 * i, groups, at=ats[i], w=w,
                weight=weight, attn="whole", out=out,
            )

    (x,) = after(done, x)
    near = split(x)
    far = swapped(near)
    begin = 2 * steps - 2
    w, done = phase(where, shapes, begin, grouped(near), at=ats[-2], w=w)
    w, squares = phase(where, shapes, begin, grouped(far), at=ats[-1], w=w, squares="new")

    pieces = [group[3] for group in grouped(near, far)]
    parts = [
        [(0, half, 0, pieces[0]), (half, half // 2, 0, pieces[1])],
        [(half + half // 2, half // 2, half // 2, pieces[1])],
    ]
    for late, masks in enumerate(rounds(devices)):
        squares = exchange(squares, devices, masks)
        if late == 0:
            before, done = phase(
                where, shapes, begin, parts[0], weight=weight, attn="first"
            )
            (squares,) = after(done, squares)
        elif late == 1:
            out, done = phase(
                where, shapes, begin, parts[1], weight=weight, attn="last",
                before=before, out=out,
            )
    return out, scaled(w, squares)


def solution(mesh):
    placed = (
        P("group", "dp"),
        P(("group", "dp"), None),
        P("dp", None),
        P("dp"),
        P(("group", "dp")),
    )
    ring = Ring(mesh.shape["dp"], 2 if mesh.shape["group"] == 2 else 1)
    return jax.shard_map(
        functools.partial(on_device, ring),
        mesh=mesh,
        in_specs=placed,
        out_specs=(P("group", "dp"), P(("group", "dp"), None)),
        check_vma=False,
    )
```

```python
import functools

import jax
import jax.numpy as jnp
import numpy as np
from jax import lax
from jax.experimental import pallas as pl
from jax.experimental.pallas import tpu as pltpu
from jax.sharding import PartitionSpec as P

HEADS = 64
HEAD_DIM = 128
SEQ = 16
TILE = 1024
MIB = 1024 * 1024


class Ring:
    def __init__(self, devices, columns):
        self.devices = devices
        self.length = devices // 2
        rows = self.length // columns
        if columns == 1:
            self.chips = list(range(rows))
        else:
            self.chips = [2 * z for z in range(rows)]
            self.chips += [2 * z + 1 for z in reversed(range(rows))]
        self.position = {chip: p for p, chip in enumerate(self.chips)}

    def device(self, position, core):
        return 2 * self.chips[position % self.length] + core

    def along(self):
        return [
            (self.device(p, core), self.device(p + 1 - 2 * core, core))
            for p in range(self.length)
            for core in range(2)
        ]

    def crossing(self):
        return [
            (self.device(p, core), self.device(p - 1 + 2 * core, 1 - core))
            for p in range(self.length)
            for core in range(2)
        ]

    def swap(self):
        return [(d, d ^ 1) for d in range(self.devices)]

    def owners(self):
        table, last = [], self.length // 2
        for d in range(self.devices):
            p, core = self.position[d // 2], d % 2
            row = [d, d ^ 1]
            for k in range(1, last + 1):
                step = k if core else -k
                row += [self.device(p + step, core), self.device(p - step, 1 - core)]
                if k < last:
                    row += [self.device(p + step, 1 - core), self.device(p - step, core)]
            table.append(row)
        return np.array(table, np.int32)


def zero_dead(count, ref):
    for s in range(ref.shape[0] // SEQ):

        @pl.when(s >= count)
        def _():
            dead = ref.at[s * SEQ : (s + 1) * SEQ]
            dead[...] = jnp.zeros_like(dead)


def prep_kernel(
    spans, rows, table_ref, me_ref, heads_ref, seqs_ref, grad_ref, a_ref, *refs
):
    copy_ref, left_ref, right_ref, count_ref, *at_refs, block_ref, sems, own_sems = refs
    half = left_ref.shape[1]
    owns = [
        pltpu.make_async_copy(grad_ref, copy_ref, own_sems.at[0]),
        pltpu.make_async_copy(grad_ref.at[:, pl.ds(0, half)], left_ref, own_sems.at[1]),
        pltpu.make_async_copy(grad_ref.at[:, pl.ds(half, half)], right_ref, own_sems.at[2]),
    ]
    for copy in owns:
        copy.start()
    count_ref[...] = jnp.full(count_ref.shape, seqs_ref[0], jnp.int32)
    width = heads_ref[0] * HEAD_DIM
    copies = []
    for i in range(block_ref.shape[0] // rows):
        owner = table_ref[me_ref[0], i]
        copies.append(
            pltpu.make_async_copy(
                a_ref.at[pl.ds(pl.multiple_of(owner * rows, rows), rows)],
                block_ref.at[pl.ds(i * rows, rows)],
                sems.at[i],
            )
        )
        copies[-1].start()
    waited = 0
    for at_ref, (begin, count) in zip(at_refs, spans):
        for copy in copies[waited : begin + count]:
            copy.wait()
        waited = max(waited, begin + count)
        block = block_ref[begin * rows : (begin + count) * rows, :]
        column = lax.broadcasted_iota(jnp.int32, block.shape, 1)
        at_ref[...] = jnp.where(column < width, block, jnp.zeros_like(block)).T
    for copy in owns:
        copy.wait()
    zero_dead(seqs_ref[0], left_ref)
    zero_dead(seqs_ref[0], right_ref)


def prepared(where, seq_counts, out_grad, attn_out, spans):
    slots, capacity = attn_out.shape
    rows, features = out_grad.shape
    vmem = pl.BlockSpec(memory_space=pltpu.VMEM)
    smem = pl.BlockSpec(memory_space=pltpu.SMEM)
    outs = [(rows, features), (rows, features // 2), (rows, features // 2)]
    outs += [(capacity, count * rows) for _, count in spans]
    shapes = [pltpu.VMEM(shape, jnp.bfloat16) for shape in outs]
    shapes.insert(3, pltpu.VMEM((8, 128), jnp.int32))
    copy, left, right, count, *ats = pl.pallas_call(
        functools.partial(prep_kernel, spans, rows),
        in_specs=[smem] * 4 + [pl.BlockSpec(memory_space=pl.ANY)] * 2,
        out_specs=[vmem] * len(shapes),
        out_shape=shapes,
        scratch_shapes=[
            pltpu.VMEM((slots, capacity), jnp.bfloat16),
            pltpu.SemaphoreType.DMA((slots // rows,)),
            pltpu.SemaphoreType.DMA((3,)),
        ],
        compiler_params=pltpu.CompilerParams(vmem_limit_bytes=12 * MIB),
        cost_estimate=pl.CostEstimate(flops=1, bytes_accessed=1, transcendentals=0),
        name="prep",
    )(
        *where,
        seq_counts,
        pltpu.with_memory_space_constraint(out_grad, pltpu.HBM),
        pltpu.with_memory_space_constraint(attn_out, pltpu.HBM),
    )
    return copy, (left, right), count, ats


def flip_kernel(x_ref, out_ref):
    width = 512
    for i in range(x_ref.shape[1] // width):
        part = slice(i * width, (i + 1) * width)
        out_ref[part, :] = x_ref[:, part].T


def flipped(x):
    vmem = pl.BlockSpec(memory_space=pltpu.VMEM)
    return pl.pallas_call(
        flip_kernel,
        in_specs=[vmem],
        out_specs=vmem,
        out_shape=pltpu.VMEM(x.shape[::-1], x.dtype),
        compiler_params=pltpu.CompilerParams(vmem_limit_bytes=8 * MIB),
        cost_estimate=pl.CostEstimate(flops=1, bytes_accessed=1, transcendentals=0),
        name="flipped",
    )(pltpu.with_memory_space_constraint(x, pltpu.VMEM))


def arrive_kernel(count_ref, x_ref, done_ref, out_ref):
    zero_dead(count_ref[0, 0], out_ref)


def arrived(done, count, x):
    vmem = pl.BlockSpec(memory_space=pltpu.VMEM)
    return pl.pallas_call(
        arrive_kernel,
        in_specs=[pl.BlockSpec(memory_space=pltpu.SMEM), vmem, vmem],
        out_specs=vmem,
        out_shape=pltpu.VMEM(x.shape, x.dtype),
        input_output_aliases={1: 0},
        compiler_params=pltpu.CompilerParams(vmem_limit_bytes=MIB),
        name="arrived",
    )(count, *[pltpu.with_memory_space_constraint(x, pltpu.VMEM) for x in (x, done)])


def phase_kernel(spec, *refs):
    groups, arrays, do_w, w_from, attn, fresh_w, fresh_out, squares, rows, begin = spec
    refs = list(refs)
    table_ref, me_ref, heads_ref = refs.pop(0), refs.pop(0), refs.pop(0)
    at_ref = refs.pop(0) if do_w else None
    weight_ref = refs.pop(0) if attn else None
    g_refs = [refs.pop(0) for _ in range(arrays)]
    if do_w and not fresh_w:
        refs.pop(0)
    before_ref = refs.pop(0) if attn == "last" else None
    added_ref = refs.pop(0) if squares == "added" else None
    if attn in ("whole", "last") and not fresh_out:
        refs.pop(0)
    w_ref = refs.pop(0) if do_w else None
    total_ref = refs.pop(0) if attn == "first" else None
    out_ref = refs.pop(0) if attn in ("whole", "last") else None
    squares_ref = refs.pop(0)
    if attn in ("whole", "last"):
        total_ref, block_ref, sems = refs
    if attn == "last":
        total_ref[...] = before_ref[...]
    elif attn:
        total_ref[...] = jnp.zeros_like(total_ref)
    if squares == "added":
        squares_ref[...] = added_ref[...]
    else:
        squares_ref[...] = jnp.zeros_like(squares_ref)

    def body(first, column, pieces, j, carry):
        here = pl.ds(pl.multiple_of(column + j * TILE, TILE), TILE)
        there = pl.ds(pl.multiple_of(first + j * TILE, TILE), TILE)
        g = [g_refs[i][start : start + count, here] for i, start, count in pieces]
        if do_w:
            fresh = jnp.concatenate(g[w_from:], axis=0) if len(g) > w_from + 1 else g[-1]
            w = jnp.dot(at_ref[...], fresh, preferred_element_type=jnp.float32)
            if not fresh_w:
                w = w + w_ref[:, there]
            w_ref[:, there] = w
        if squares:
            folded = jnp.sum((w * w).reshape(w.shape[0] // 8, 8, TILE), axis=0)
            total = squares_ref[...]
            for lane in range(0, TILE, 128):
                total = total + folded[:, lane : lane + 128]
            squares_ref[...] = total
        if attn:
            total_ref[...] += lax.dot_general(
                jnp.concatenate(g, axis=0),
                weight_ref[there, :],
                (((1,), (0,)), ((), ())),
                preferred_element_type=jnp.float32,
            )
        return carry

    for first, width, column, pieces in groups:
        step = functools.partial(body, first, column, pieces)
        lax.fori_loop(0, width // TILE, step, 0)
    if attn in ("whole", "last"):
        total = total_ref[...]
        column = lax.broadcasted_iota(jnp.int32, total.shape, 1)
        live = column < heads_ref[0] * HEAD_DIM
        block_ref[...] = jnp.where(live, total, 0.0).astype(jnp.bfloat16)
        copies = []
        for i in range(total.shape[0] // rows):
            owner = table_ref[me_ref[0], begin + i]
            copies.append(
                pltpu.make_async_copy(
                    block_ref.at[pl.ds(i * rows, rows)],
                    out_ref.at[pl.ds(pl.multiple_of(owner * rows, rows), rows)],
                    sems.at[i],
                )
            )
            copies[-1].start()
        for copy in copies:
            copy.wait()


def phase(
    where, shapes, begin, groups, at=None, w=None,
    weight=None, attn=None, before=None, out=None, squares=None, added=None,
    w_from=0,
):
    slots, capacity, features, rows = shapes
    do_w = at is not None
    arrays, described = [], []
    for first, width, column, pieces in groups:
        placed = []
        for array, start, count in pieces:
            known = [i for i, x in enumerate(arrays) if x is array]
            if not known:
                arrays.append(array)
            placed.append((known[0] if known else len(arrays) - 1, start, count))
        described.append((first, width, column, tuple(placed)))
    height = sum(count for _, _, count in groups[0][3])
    vmem = pl.BlockSpec(memory_space=pltpu.VMEM)
    smem = pl.BlockSpec(memory_space=pltpu.SMEM)
    hbm = pl.BlockSpec(memory_space=pl.ANY)

    args, specs, outs, out_specs, aliases, scratch = [], [], [], [], {}, []

    def add(arg, spec):
        args.append(arg)
        specs.append(spec)

    def add_vmem(arg):
        add(pltpu.with_memory_space_constraint(arg, pltpu.VMEM), vmem)

    for scalar in where:
        add(scalar, smem)
    if do_w:
        add_vmem(at)
    if attn:
        add_vmem(weight)
    for array in arrays:
        add_vmem(array)
    if do_w:
        if w is not None:
            aliases[len(args)] = len(outs)
            add_vmem(w)
        outs.append(pltpu.VMEM((capacity, features), jnp.float32))
        out_specs.append(vmem)
    if attn == "last":
        add_vmem(before)
    if squares == "added":
        add_vmem(added)
    if attn == "first":
        outs.append(pltpu.VMEM((height, capacity), jnp.float32))
        out_specs.append(vmem)
    elif attn:
        if out is not None:
            aliases[len(args)] = len(outs)
            add(out, hbm)
        outs.append(jax.ShapeDtypeStruct((slots, capacity), jnp.bfloat16))
        out_specs.append(hbm)
        scratch = [
            pltpu.VMEM((height, capacity), jnp.float32),
            pltpu.VMEM((height, capacity), jnp.bfloat16),
            pltpu.SemaphoreType.DMA((height // rows,)),
        ]
    outs.append(pltpu.VMEM((8, 128), jnp.float32))
    out_specs.append(vmem)
    spec = (
        tuple(described), len(arrays), do_w, w_from, attn, w is None, out is None,
        squares, rows, begin,
    )
    return pl.pallas_call(
        functools.partial(phase_kernel, spec),
        in_specs=specs,
        out_specs=out_specs,
        out_shape=outs,
        scratch_shapes=scratch,
        input_output_aliases=aliases,
        compiler_params=pltpu.CompilerParams(vmem_limit_bytes=12 * MIB),
        cost_estimate=pl.CostEstimate(
            flops=1,
            bytes_accessed=1,
            transcendentals=0,
        ),
        name="phase_" + "w" * do_w + "_" + str(attn),
    )(*args)


def scale_kernel(parts, w_ref, squares_ref, out_ref, block_ref, sems):
    capacity, features = w_ref.shape
    square_sum = jnp.sum(
        jnp.sum(squares_ref[...], axis=0, keepdims=True), axis=1, keepdims=True
    )
    factor = jnp.minimum(
        1.0, 1.0 / jnp.sqrt(square_sum / (HEADS * HEAD_DIM * features) + 1e-06)
    )
    copies = []
    height = capacity // parts
    for i in range(parts):
        part = pl.ds(i * height, height)
        block_ref[part, :] = (w_ref[part, :] * factor).astype(jnp.bfloat16)
        copies.append(pltpu.make_async_copy(block_ref.at[part], out_ref.at[part], sems.at[i]))
        copies[-1].start()
    for copy in copies:
        copy.wait()


def scaled(w, squares):
    capacity, features = w.shape
    vmem = pl.BlockSpec(memory_space=pltpu.VMEM)
    parts = 8
    return pl.pallas_call(
        functools.partial(scale_kernel, parts),
        in_specs=[vmem, vmem],
        out_specs=pl.BlockSpec(memory_space=pl.ANY),
        out_shape=jax.ShapeDtypeStruct((capacity, features), jnp.bfloat16),
        scratch_shapes=[
            pltpu.VMEM((capacity, features), jnp.bfloat16),
            pltpu.SemaphoreType.DMA((parts,)),
        ],
        compiler_params=pltpu.CompilerParams(vmem_limit_bytes=10 * MIB),
        cost_estimate=pl.CostEstimate(
            flops=capacity * features,
            bytes_accessed=2 * capacity * features,
            transcendentals=0,
        ),
        name="scale",
    )(pltpu.with_memory_space_constraint(w, pltpu.VMEM), squares)


def after(done, *arrays):
    vmem = pl.BlockSpec(memory_space=pltpu.VMEM)
    return pl.pallas_call(
        lambda *refs: None,
        in_specs=[vmem] * (len(arrays) + 1),
        out_specs=[vmem] * len(arrays),
        out_shape=[pltpu.VMEM(x.shape, x.dtype) for x in arrays],
        input_output_aliases={i: i for i in range(len(arrays))},
        compiler_params=pltpu.CompilerParams(vmem_limit_bytes=MIB),
        name="after",
    )(*[pltpu.with_memory_space_constraint(x, pltpu.VMEM) for x in (*arrays, done)])


def split_kernel(x_ref, left_ref, right_ref, sems):
    half = left_ref.shape[1]
    copies = [
        pltpu.make_async_copy(x_ref.at[:, pl.ds(0, half)], left_ref, sems.at[0]),
        pltpu.make_async_copy(x_ref.at[:, pl.ds(half, half)], right_ref, sems.at[1]),
    ]
    for copy in copies:
        copy.start()
    for copy in copies:
        copy.wait()


def split(x):
    vmem = pl.BlockSpec(memory_space=pltpu.VMEM)
    rows, features = x.shape
    return pl.pallas_call(
        split_kernel,
        in_specs=[vmem],
        out_specs=[vmem] * 2,
        out_shape=[pltpu.VMEM((rows, features // 2), x.dtype)] * 2,
        scratch_shapes=[pltpu.SemaphoreType.DMA((2,))],
        compiler_params=pltpu.CompilerParams(vmem_limit_bytes=MIB),
        name="split",
    )(pltpu.with_memory_space_constraint(x, pltpu.VMEM))


def rounds(devices):
    bits = [1 << i for i in range(devices.bit_length() - 1)]
    if len(bits) >= 4:
        bits = bits[1:3] + [bits[0]] + bits[3:]
    masks = []
    while bits:
        pair, bits = bits[:2], bits[2:]
        masks.append(pair + [sum(pair)] if len(pair) == 2 else pair)
    return masks


def exchange(x, devices, masks):
    total = x
    for mask in masks:
        total = total + lax.ppermute(x, "dp", [(d, d ^ mask) for d in range(devices)])
    return total


def on_device(ring, attn_out, out_grad, o_weight, head_counts, seq_counts):
    rows, features = out_grad.shape
    slots = attn_out.shape[0]
    devices, last = ring.devices, ring.length // 2
    steps = 2 * last
    spans = [(0, 2)]
    for k in range(1, last):
        joint = k < last - 1
        spans += [(4 * k - 2, 4), None] if joint else [(4 * k - 2, 2), (4 * k, 2)]
    spans += [(2 * steps - 2, 1), (2 * steps - 1, 1)]
    me = lax.axis_index("dp").astype(jnp.int32).reshape(1)
    where = (jnp.asarray(ring.owners()), me, head_counts)
    shapes = (slots, o_weight.shape[0], features, rows)
    half = features // 2

    def send(x, pairs):
        return lax.ppermute(x, "dp", pairs)

    def swapped(halves):
        return [send(x, ring.swap()) for x in halves]

    def grouped(*pairs):
        return [
            (c * half, half, 0, [(x[c], 0, rows) for x in pairs])
            for c in range(min(len(x) for x in pairs))
        ]

    x = send(out_grad, ring.along())
    own, near, count, ats = prepared(
        where, seq_counts, out_grad, attn_out, [x for x in spans if x]
    )
    ats = [ats.pop(0) if x else None for x in spans]
    y = send(own, ring.crossing())
    counts = send(count, ring.along()), send(count, ring.crossing())
    first = [near, swapped(near)]
    w, done = phase(where, shapes, 0, grouped(*first), at=ats[0])
    weight, out = flipped(o_weight), None

    for k in range(1, last):
        x = arrived(done, counts[0], x) if k == 1 else after(done, x)[0]
        x, near_x = send(x, ring.along()), split(x)
        far_x = swapped(near_x)
        i = 2 * k - 1
        if k == last - 1:
            held = held + [near_x, far_x]
            w, out, done = phase(
                where, shapes, 2 * (i + 1) - len(held), grouped(*held), at=ats[i], w=w,
                w_from=len(held) - 2, weight=weight, attn="whole", out=out,
            )
        y = arrived(weight, counts[1], y) if k == 1 else after(done, y)[0]
        y, near_y = send(y, ring.along()) if k < last - 1 else None, split(y)
        far_y = swapped(near_y)
        groups = grouped(near_x, far_x, near_y, far_y)
        if k == last - 1:
            w, out, done = phase(
                where, shapes, 2 * (i + 1), grouped(near_y, far_y), at=ats[i + 1], w=w,
                weight=weight, attn="whole", out=out,
            )
        elif k == last - 2:
            held = [near_x, far_x, near_y, far_y]
            w, done = phase(where, shapes, 2 * i, groups, at=ats[i], w=w)
        else:
            groups = grouped(*first, near_x, far_x, near_y, far_y)
            w, out, done = phase(
                where, shapes, 2 * i - len(first), groups, at=ats[i], w=w,
                w_from=len(first), weight=weight, attn="whole", out=out,
            )
            first = []

    (x,) = after(done, x)
    near = split(x)
    far = swapped(near)
    begin = 2 * steps - 2
    w, done = phase(where, shapes, begin, grouped(near), at=ats[-2], w=w)
    w, squares = phase(where, shapes, begin, grouped(far), at=ats[-1], w=w, squares="new")

    pieces = [group[3] for group in grouped(near, far)]
    parts = [
        [(0, half, 0, pieces[0]), (half, half // 2, 0, pieces[1])],
        [(half + half // 2, half // 2, half // 2, pieces[1])],
    ]
    for late, masks in enumerate(rounds(devices)):
        squares = exchange(squares, devices, masks)
        if late == 0:
            before, done = phase(
                where, shapes, begin, parts[0], weight=weight, attn="first"
            )
            (squares,) = after(done, squares)
        elif late == 1:
            out, done = phase(
                where, shapes, begin, parts[1], weight=weight, attn="last",
                before=before, out=out,
            )
    return out, scaled(w, squares)


def solution(mesh):
    placed = (
        P("group", "dp"),
        P(("group", "dp"), None),
        P("dp", None),
        P("dp"),
        P(("group", "dp")),
    )
    ring = Ring(mesh.shape["dp"], 2 if mesh.shape["group"] == 2 else 1)
    return jax.shard_map(
        functools.partial(on_device, ring),
        mesh=mesh,
        in_specs=placed,
        out_specs=(P("group", "dp"), P(("group", "dp"), None)),
        check_vma=False,
    )
```

```python
import functools

import jax
import jax.numpy as jnp
import numpy as np
from jax import lax
from jax.experimental import pallas as pl
from jax.experimental.pallas import tpu as pltpu
from jax.sharding import PartitionSpec as P

HEADS = 64
HEAD_DIM = 128
SEQ = 16
TILE = 1024
MIB = 1024 * 1024


class Ring:
    def __init__(self, devices, columns):
        self.devices = devices
        self.length = devices // 2
        rows = self.length // columns
        if columns == 1:
            self.chips = list(range(rows))
        else:
            self.chips = [2 * z for z in range(rows)]
            self.chips += [2 * z + 1 for z in reversed(range(rows))]
        self.position = {chip: p for p, chip in enumerate(self.chips)}

    def device(self, position, core):
        return 2 * self.chips[position % self.length] + core

    def along(self):
        return [
            (self.device(p, core), self.device(p + 1 - 2 * core, core))
            for p in range(self.length)
            for core in range(2)
        ]

    def crossing(self):
        return [
            (self.device(p, core), self.device(p - 1 + 2 * core, 1 - core))
            for p in range(self.length)
            for core in range(2)
        ]

    def swap(self):
        return [(d, d ^ 1) for d in range(self.devices)]

    def owners(self):
        table, last = [], self.length // 2
        for d in range(self.devices):
            p, core = self.position[d // 2], d % 2
            row = [d, d ^ 1]
            for k in range(1, last + 1):
                step = k if core else -k
                row += [self.device(p + step, core), self.device(p - step, 1 - core)]
                if k < last:
                    row += [self.device(p + step, 1 - core), self.device(p - step, core)]
            table.append(row)
        return np.array(table, np.int32)


def zero_dead(count, ref):
    for s in range(ref.shape[0] // SEQ):

        @pl.when(s >= count)
        def _():
            dead = ref.at[s * SEQ : (s + 1) * SEQ]
            dead[...] = jnp.zeros_like(dead)


def prep_kernel(
    spans, rows, table_ref, me_ref, heads_ref, seqs_ref, grad_ref, a_ref, *refs
):
    copy_ref, left_ref, right_ref, count_ref, *at_refs, block_ref, sems, own_sems = refs
    half = left_ref.shape[1]
    owns = [
        pltpu.make_async_copy(grad_ref, copy_ref, own_sems.at[0]),
        pltpu.make_async_copy(grad_ref.at[:, pl.ds(0, half)], left_ref, own_sems.at[1]),
        pltpu.make_async_copy(grad_ref.at[:, pl.ds(half, half)], right_ref, own_sems.at[2]),
    ]
    for copy in owns:
        copy.start()
    count_ref[...] = jnp.full(count_ref.shape, seqs_ref[0], jnp.int32)
    width = heads_ref[0] * HEAD_DIM
    copies = []
    for i in range(block_ref.shape[0] // rows):
        owner = table_ref[me_ref[0], i]
        copies.append(
            pltpu.make_async_copy(
                a_ref.at[pl.ds(pl.multiple_of(owner * rows, rows), rows)],
                block_ref.at[pl.ds(i * rows, rows)],
                sems.at[i],
            )
        )
        copies[-1].start()
    waited = 0
    for at_ref, (begin, count) in zip(at_refs, spans):
        for copy in copies[waited : begin + count]:
            copy.wait()
        waited = max(waited, begin + count)
        block = block_ref[begin * rows : (begin + count) * rows, :]
        column = lax.broadcasted_iota(jnp.int32, block.shape, 1)
        at_ref[...] = jnp.where(column < width, block, jnp.zeros_like(block)).T
    for copy in owns:
        copy.wait()
    zero_dead(seqs_ref[0], left_ref)
    zero_dead(seqs_ref[0], right_ref)


def prepared(where, seq_counts, out_grad, attn_out, spans):
    slots, capacity = attn_out.shape
    rows, features = out_grad.shape
    vmem = pl.BlockSpec(memory_space=pltpu.VMEM)
    smem = pl.BlockSpec(memory_space=pltpu.SMEM)
    outs = [(rows, features), (rows, features // 2), (rows, features // 2)]
    outs += [(capacity, count * rows) for _, count in spans]
    shapes = [pltpu.VMEM(shape, jnp.bfloat16) for shape in outs]
    shapes.insert(3, pltpu.VMEM((8, 128), jnp.int32))
    copy, left, right, count, *ats = pl.pallas_call(
        functools.partial(prep_kernel, spans, rows),
        in_specs=[smem] * 4 + [pl.BlockSpec(memory_space=pl.ANY)] * 2,
        out_specs=[vmem] * len(shapes),
        out_shape=shapes,
        scratch_shapes=[
            pltpu.VMEM((slots, capacity), jnp.bfloat16),
            pltpu.SemaphoreType.DMA((slots // rows,)),
            pltpu.SemaphoreType.DMA((3,)),
        ],
        compiler_params=pltpu.CompilerParams(vmem_limit_bytes=12 * MIB),
        cost_estimate=pl.CostEstimate(flops=1, bytes_accessed=1, transcendentals=0),
        name="prep",
    )(
        *where,
        seq_counts,
        pltpu.with_memory_space_constraint(out_grad, pltpu.HBM),
        pltpu.with_memory_space_constraint(attn_out, pltpu.HBM),
    )
    return copy, (left, right), count, ats


def arrive_kernel(count_ref, x_ref, done_ref, out_ref):
    zero_dead(count_ref[0, 0], out_ref)


def arrived(done, count, x):
    vmem = pl.BlockSpec(memory_space=pltpu.VMEM)
    return pl.pallas_call(
        arrive_kernel,
        in_specs=[pl.BlockSpec(memory_space=pltpu.SMEM), vmem, vmem],
        out_specs=vmem,
        out_shape=pltpu.VMEM(x.shape, x.dtype),
        input_output_aliases={1: 0},
        compiler_params=pltpu.CompilerParams(vmem_limit_bytes=MIB),
        name="arrived",
    )(count, *[pltpu.with_memory_space_constraint(x, pltpu.VMEM) for x in (x, done)])


def phase_kernel(spec, *refs):
    groups, arrays, do_w, w_from, attn, fresh_w, fresh_out, squares, rows, begin = spec
    refs = list(refs)
    table_ref, me_ref, heads_ref = refs.pop(0), refs.pop(0), refs.pop(0)
    at_ref = refs.pop(0) if do_w else None
    weight_ref = refs.pop(0) if attn else None
    g_refs = [refs.pop(0) for _ in range(arrays)]
    if do_w and not fresh_w:
        refs.pop(0)
    before_ref = refs.pop(0) if attn == "last" else None
    added_ref = refs.pop(0) if squares == "added" else None
    if attn in ("whole", "last") and not fresh_out:
        refs.pop(0)
    w_ref = refs.pop(0) if do_w else None
    total_ref = refs.pop(0) if attn == "first" else None
    out_ref = refs.pop(0) if attn in ("whole", "last") else None
    squares_ref = refs.pop(0)
    if attn in ("whole", "last"):
        total_ref, block_ref, sems = refs
    if attn == "last":
        total_ref[...] = before_ref[...]
    elif attn:
        total_ref[...] = jnp.zeros_like(total_ref)
    if squares == "added":
        squares_ref[...] = added_ref[...]
    else:
        squares_ref[...] = jnp.zeros_like(squares_ref)

    def body(first, column, pieces, j, carry):
        here = pl.ds(pl.multiple_of(column + j * TILE, TILE), TILE)
        there = pl.ds(pl.multiple_of(first + j * TILE, TILE), TILE)
        g = [g_refs[i][start : start + count, here] for i, start, count in pieces]
        if do_w:
            fresh = jnp.concatenate(g[w_from:], axis=0) if len(g) > w_from + 1 else g[-1]
            w = jnp.dot(at_ref[...], fresh, preferred_element_type=jnp.float32)
            if not fresh_w:
                w = w + w_ref[:, there]
            w_ref[:, there] = w
        if squares:
            folded = jnp.sum((w * w).reshape(w.shape[0] // 8, 8, TILE), axis=0)
            total = squares_ref[...]
            for lane in range(0, TILE, 128):
                total = total + folded[:, lane : lane + 128]
            squares_ref[...] = total
        if attn:
            total_ref[...] += lax.dot_general(
                jnp.concatenate(g, axis=0),
                weight_ref[:, there],
                (((1,), (1,)), ((), ())),
                preferred_element_type=jnp.float32,
            )
        return carry

    for first, width, column, pieces in groups:
        step = functools.partial(body, first, column, pieces)
        lax.fori_loop(0, width // TILE, step, 0)
    if attn in ("whole", "last"):
        total = total_ref[...]
        column = lax.broadcasted_iota(jnp.int32, total.shape, 1)
        live = column < heads_ref[0] * HEAD_DIM
        block_ref[...] = jnp.where(live, total, 0.0).astype(jnp.bfloat16)
        copies = []
        for i in range(total.shape[0] // rows):
            owner = table_ref[me_ref[0], begin + i]
            copies.append(
                pltpu.make_async_copy(
                    block_ref.at[pl.ds(i * rows, rows)],
                    out_ref.at[pl.ds(pl.multiple_of(owner * rows, rows), rows)],
                    sems.at[i],
                )
            )
            copies[-1].start()
        for copy in copies:
            copy.wait()


def phase(
    where, shapes, begin, groups, at=None, w=None,
    weight=None, attn=None, before=None, out=None, squares=None, added=None,
    w_from=0,
):
    slots, capacity, features, rows = shapes
    do_w = at is not None
    arrays, described = [], []
    for first, width, column, pieces in groups:
        placed = []
        for array, start, count in pieces:
            known = [i for i, x in enumerate(arrays) if x is array]
            if not known:
                arrays.append(array)
            placed.append((known[0] if known else len(arrays) - 1, start, count))
        described.append((first, width, column, tuple(placed)))
    height = sum(count for _, _, count in groups[0][3])
    vmem = pl.BlockSpec(memory_space=pltpu.VMEM)
    smem = pl.BlockSpec(memory_space=pltpu.SMEM)
    hbm = pl.BlockSpec(memory_space=pl.ANY)

    args, specs, outs, out_specs, aliases, scratch = [], [], [], [], {}, []

    def add(arg, spec):
        args.append(arg)
        specs.append(spec)

    def add_vmem(arg):
        add(pltpu.with_memory_space_constraint(arg, pltpu.VMEM), vmem)

    for scalar in where:
        add(scalar, smem)
    if do_w:
        add_vmem(at)
    if attn:
        add_vmem(weight)
    for array in arrays:
        add_vmem(array)
    if do_w:
        if w is not None:
            aliases[len(args)] = len(outs)
            add_vmem(w)
        outs.append(pltpu.VMEM((capacity, features), jnp.float32))
        out_specs.append(vmem)
    if attn == "last":
        add_vmem(before)
    if squares == "added":
        add_vmem(added)
    if attn == "first":
        outs.append(pltpu.VMEM((height, capacity), jnp.float32))
        out_specs.append(vmem)
    elif attn:
        if out is not None:
            aliases[len(args)] = len(outs)
            add(out, hbm)
        outs.append(jax.ShapeDtypeStruct((slots, capacity), jnp.bfloat16))
        out_specs.append(hbm)
        scratch = [
            pltpu.VMEM((height, capacity), jnp.float32),
            pltpu.VMEM((height, capacity), jnp.bfloat16),
            pltpu.SemaphoreType.DMA((height // rows,)),
        ]
    outs.append(pltpu.VMEM((8, 128), jnp.float32))
    out_specs.append(vmem)
    spec = (
        tuple(described), len(arrays), do_w, w_from, attn, w is None, out is None,
        squares, rows, begin,
    )
    return pl.pallas_call(
        functools.partial(phase_kernel, spec),
        in_specs=specs,
        out_specs=out_specs,
        out_shape=outs,
        scratch_shapes=scratch,
        input_output_aliases=aliases,
        compiler_params=pltpu.CompilerParams(vmem_limit_bytes=12 * MIB),
        cost_estimate=pl.CostEstimate(
            flops=1,
            bytes_accessed=1,
            transcendentals=0,
        ),
        name="phase_" + "w" * do_w + "_" + str(attn),
    )(*args)


def scale_kernel(parts, w_ref, squares_ref, out_ref, block_ref, sems):
    capacity, features = w_ref.shape
    square_sum = jnp.sum(
        jnp.sum(squares_ref[...], axis=0, keepdims=True), axis=1, keepdims=True
    )
    factor = jnp.minimum(
        1.0, 1.0 / jnp.sqrt(square_sum / (HEADS * HEAD_DIM * features) + 1e-06)
    )
    copies = []
    height = capacity // parts
    for i in range(parts):
        part = pl.ds(i * height, height)
        block_ref[part, :] = (w_ref[part, :] * factor).astype(jnp.bfloat16)
        copies.append(pltpu.make_async_copy(block_ref.at[part], out_ref.at[part], sems.at[i]))
        copies[-1].start()
    for copy in copies:
        copy.wait()


def scaled(w, squares):
    capacity, features = w.shape
    vmem = pl.BlockSpec(memory_space=pltpu.VMEM)
    parts = 8
    return pl.pallas_call(
        functools.partial(scale_kernel, parts),
        in_specs=[vmem, vmem],
        out_specs=pl.BlockSpec(memory_space=pl.ANY),
        out_shape=jax.ShapeDtypeStruct((capacity, features), jnp.bfloat16),
        scratch_shapes=[
            pltpu.VMEM((capacity, features), jnp.bfloat16),
            pltpu.SemaphoreType.DMA((parts,)),
        ],
        compiler_params=pltpu.CompilerParams(vmem_limit_bytes=10 * MIB),
        cost_estimate=pl.CostEstimate(
            flops=capacity * features,
            bytes_accessed=2 * capacity * features,
            transcendentals=0,
        ),
        name="scale",
    )(pltpu.with_memory_space_constraint(w, pltpu.VMEM), squares)


def after(done, *arrays):
    vmem = pl.BlockSpec(memory_space=pltpu.VMEM)
    return pl.pallas_call(
        lambda *refs: None,
        in_specs=[vmem] * (len(arrays) + 1),
        out_specs=[vmem] * len(arrays),
        out_shape=[pltpu.VMEM(x.shape, x.dtype) for x in arrays],
        input_output_aliases={i: i for i in range(len(arrays))},
        compiler_params=pltpu.CompilerParams(vmem_limit_bytes=MIB),
        name="after",
    )(*[pltpu.with_memory_space_constraint(x, pltpu.VMEM) for x in (*arrays, done)])


def split_kernel(x_ref, left_ref, right_ref, sems):
    half = left_ref.shape[1]
    copies = [
        pltpu.make_async_copy(x_ref.at[:, pl.ds(0, half)], left_ref, sems.at[0]),
        pltpu.make_async_copy(x_ref.at[:, pl.ds(half, half)], right_ref, sems.at[1]),
    ]
    for copy in copies:
        copy.start()
    for copy in copies:
        copy.wait()


def split(x):
    vmem = pl.BlockSpec(memory_space=pltpu.VMEM)
    rows, features = x.shape
    return pl.pallas_call(
        split_kernel,
        in_specs=[vmem],
        out_specs=[vmem] * 2,
        out_shape=[pltpu.VMEM((rows, features // 2), x.dtype)] * 2,
        scratch_shapes=[pltpu.SemaphoreType.DMA((2,))],
        compiler_params=pltpu.CompilerParams(vmem_limit_bytes=MIB),
        name="split",
    )(pltpu.with_memory_space_constraint(x, pltpu.VMEM))


def rounds(devices):
    bits = [1 << i for i in range(devices.bit_length() - 1)]
    if len(bits) >= 4:
        bits = bits[1:3] + [bits[0]] + bits[3:]
    masks = []
    while bits:
        pair, bits = bits[:2], bits[2:]
        masks.append(pair + [sum(pair)] if len(pair) == 2 else pair)
    return masks


def exchange(x, devices, masks):
    total = x
    for mask in masks:
        total = total + lax.ppermute(x, "dp", [(d, d ^ mask) for d in range(devices)])
    return total


def on_device(ring, attn_out, out_grad, o_weight, head_counts, seq_counts):
    rows, features = out_grad.shape
    slots = attn_out.shape[0]
    devices, last = ring.devices, ring.length // 2
    steps = 2 * last
    spans = [(0, 2)]
    for k in range(1, last):
        joint = k < last - 1
        spans += [(4 * k - 2, 4), None] if joint else [(4 * k - 2, 2), (4 * k, 2)]
    spans += [(2 * steps - 2, 1), (2 * steps - 1, 1)]
    me = lax.axis_index("dp").astype(jnp.int32).reshape(1)
    where = (jnp.asarray(ring.owners()), me, head_counts)
    shapes = (slots, o_weight.shape[0], features, rows)
    weight, half = o_weight, features // 2

    def send(x, pairs):
        return lax.ppermute(x, "dp", pairs)

    def swapped(halves):
        return [send(x, ring.swap()) for x in halves]

    def grouped(*pairs):
        return [
            (c * half, half, 0, [(x[c], 0, rows) for x in pairs])
            for c in range(min(len(x) for x in pairs))
        ]

    x = send(out_grad, ring.along())
    own, near, count, ats = prepared(
        where, seq_counts, out_grad, attn_out, [x for x in spans if x]
    )
    ats = [ats.pop(0) if x else None for x in spans]
    y = send(own, ring.crossing())
    counts = send(count, ring.along()), send(count, ring.crossing())
    w, out, done = phase(
        where, shapes, 0, grouped(near, swapped(near)), at=ats[0], weight=weight, attn="whole"
    )

    for k in range(1, last):
        x = arrived(done, counts[0], x) if k == 1 else after(done, x)[0]
        x, near_x = send(x, ring.along()), split(x)
        far_x = swapped(near_x)
        i = 2 * k - 1
        if k == last - 1:
            held = held + [near_x, far_x]
            w, out, done = phase(
                where, shapes, 2 * (i + 1) - len(held), grouped(*held), at=ats[i], w=w,
                w_from=len(held) - 2, weight=weight, attn="whole", out=out,
            )
        y = arrived(done, counts[1], y) if k == 1 else after(done, y)[0]
        y, near_y = send(y, ring.along()) if k < last - 1 else None, split(y)
        far_y = swapped(near_y)
        groups = grouped(near_x, far_x, near_y, far_y)
        if k == last - 1:
            w, out, done = phase(
                where, shapes, 2 * (i + 1), grouped(near_y, far_y), at=ats[i + 1], w=w,
                weight=weight, attn="whole", out=out,
            )
        elif k == last - 2:
            held = [near_x, far_x, near_y, far_y]
            w, done = phase(where, shapes, 2 * i, groups, at=ats[i], w=w)
        else:
            w, out, done = phase(
                where, shapes, 2 * i, groups, at=ats[i], w=w,
                weight=weight, attn="whole", out=out,
            )

    (x,) = after(done, x)
    near = split(x)
    far = swapped(near)
    begin = 2 * steps - 2
    w, done = phase(where, shapes, begin, grouped(near), at=ats[-2], w=w)
    w, squares = phase(where, shapes, begin, grouped(far), at=ats[-1], w=w, squares="new")

    pieces = [group[3] for group in grouped(near, far)]
    parts = [
        [(0, half, 0, pieces[0]), (half, half // 2, 0, pieces[1])],
        [(half + half // 2, half // 2, half // 2, pieces[1])],
    ]
    for late, masks in enumerate(rounds(devices)):
        squares = exchange(squares, devices, masks)
        if late == 0:
            before, done = phase(
                where, shapes, begin, parts[0], weight=weight, attn="first"
            )
            (squares,) = after(done, squares)
        elif late == 1:
            out, done = phase(
                where, shapes, begin, parts[1], weight=weight, attn="last",
                before=before, out=out,
            )
    return out, scaled(w, squares)


def solution(mesh):
    placed = (
        P("group", "dp"),
        P(("group", "dp"), None),
        P("dp", None),
        P("dp"),
        P(("group", "dp")),
    )
    ring = Ring(mesh.shape["dp"], 2 if mesh.shape["group"] == 2 else 1)
    return jax.shard_map(
        functools.partial(on_device, ring),
        mesh=mesh,
        in_specs=placed,
        out_specs=(P("group", "dp"), P(("group", "dp"), None)),
        check_vma=False,
    )
```

```python
import functools

import jax
import jax.numpy as jnp
import numpy as np
from jax import lax
from jax.experimental import pallas as pl
from jax.experimental.pallas import tpu as pltpu
from jax.sharding import PartitionSpec as P

HEADS = 64
HEAD_DIM = 128
SEQ = 16
TILE = 1024
MIB = 1024 * 1024


class Ring:
    def __init__(self, devices, columns):
        self.devices = devices
        self.length = devices // 2
        rows = self.length // columns
        if columns == 1:
            self.chips = list(range(rows))
        else:
            self.chips = [2 * z for z in range(rows)]
            self.chips += [2 * z + 1 for z in reversed(range(rows))]
        self.position = {chip: p for p, chip in enumerate(self.chips)}

    def device(self, position, core):
        return 2 * self.chips[position % self.length] + core

    def along(self):
        return [
            (self.device(p, core), self.device(p + 1 - 2 * core, core))
            for p in range(self.length)
            for core in range(2)
        ]

    def crossing(self):
        return [
            (self.device(p, core), self.device(p - 1 + 2 * core, 1 - core))
            for p in range(self.length)
            for core in range(2)
        ]

    def swap(self):
        return [(d, d ^ 1) for d in range(self.devices)]

    def owners(self):
        table, last = [], self.length // 2
        for d in range(self.devices):
            p, core = self.position[d // 2], d % 2
            row = [d, d ^ 1]
            for k in range(1, last + 1):
                step = k if core else -k
                row += [self.device(p + step, core), self.device(p - step, 1 - core)]
                if k < last:
                    row += [self.device(p + step, 1 - core), self.device(p - step, core)]
            table.append(row)
        return np.array(table, np.int32)


def zero_dead(count, ref):
    for s in range(ref.shape[0] // SEQ):

        @pl.when(s >= count)
        def _():
            dead = ref.at[s * SEQ : (s + 1) * SEQ]
            dead[...] = jnp.zeros_like(dead)


def prep_kernel(
    spans, rows, table_ref, me_ref, heads_ref, seqs_ref, grad_ref, a_ref, *refs
):
    copy_ref, left_ref, right_ref, count_ref, *at_refs, block_ref, sems, own_sems = refs
    half = left_ref.shape[1]
    owns = [
        pltpu.make_async_copy(grad_ref, copy_ref, own_sems.at[0]),
        pltpu.make_async_copy(grad_ref.at[:, pl.ds(0, half)], left_ref, own_sems.at[1]),
        pltpu.make_async_copy(grad_ref.at[:, pl.ds(half, half)], right_ref, own_sems.at[2]),
    ]
    for copy in owns:
        copy.start()
    count_ref[...] = jnp.full(count_ref.shape, seqs_ref[0], jnp.int32)
    width = heads_ref[0] * HEAD_DIM
    copies = []
    for i in range(block_ref.shape[0] // rows):
        owner = table_ref[me_ref[0], i]
        copies.append(
            pltpu.make_async_copy(
                a_ref.at[pl.ds(pl.multiple_of(owner * rows, rows), rows)],
                block_ref.at[pl.ds(i * rows, rows)],
                sems.at[i],
            )
        )
        copies[-1].start()
    waited = 0
    for at_ref, (begin, count) in zip(at_refs, spans):
        for copy in copies[waited : begin + count]:
            copy.wait()
        waited = max(waited, begin + count)
        block = block_ref[begin * rows : (begin + count) * rows, :]
        column = lax.broadcasted_iota(jnp.int32, block.shape, 1)
        at_ref[...] = jnp.where(column < width, block, jnp.zeros_like(block)).T
    for copy in owns:
        copy.wait()
    zero_dead(seqs_ref[0], left_ref)
    zero_dead(seqs_ref[0], right_ref)


def prepared(where, seq_counts, out_grad, attn_out, spans):
    slots, capacity = attn_out.shape
    rows, features = out_grad.shape
    vmem = pl.BlockSpec(memory_space=pltpu.VMEM)
    smem = pl.BlockSpec(memory_space=pltpu.SMEM)
    outs = [(rows, features), (rows, features // 2), (rows, features // 2)]
    outs += [(capacity, count * rows) for _, count in spans]
    shapes = [pltpu.VMEM(shape, jnp.bfloat16) for shape in outs]
    shapes.insert(3, pltpu.VMEM((8, 128), jnp.int32))
    copy, left, right, count, *ats = pl.pallas_call(
        functools.partial(prep_kernel, spans, rows),
        in_specs=[smem] * 4 + [pl.BlockSpec(memory_space=pl.ANY)] * 2,
        out_specs=[vmem] * len(shapes),
        out_shape=shapes,
        scratch_shapes=[
            pltpu.VMEM((slots, capacity), jnp.bfloat16),
            pltpu.SemaphoreType.DMA((slots // rows,)),
            pltpu.SemaphoreType.DMA((3,)),
        ],
        compiler_params=pltpu.CompilerParams(vmem_limit_bytes=12 * MIB),
        cost_estimate=pl.CostEstimate(flops=1, bytes_accessed=1, transcendentals=0),
        name="prep",
    )(
        *where,
        seq_counts,
        pltpu.with_memory_space_constraint(out_grad, pltpu.HBM),
        pltpu.with_memory_space_constraint(attn_out, pltpu.HBM),
    )
    return copy, (left, right), count, ats


def arrive_kernel(count_ref, x_ref, done_ref, out_ref):
    zero_dead(count_ref[0, 0], out_ref)


def arrived(done, count, x):
    vmem = pl.BlockSpec(memory_space=pltpu.VMEM)
    return pl.pallas_call(
        arrive_kernel,
        in_specs=[pl.BlockSpec(memory_space=pltpu.SMEM), vmem, vmem],
        out_specs=vmem,
        out_shape=pltpu.VMEM(x.shape, x.dtype),
        input_output_aliases={1: 0},
        compiler_params=pltpu.CompilerParams(vmem_limit_bytes=MIB),
        name="arrived",
    )(count, *[pltpu.with_memory_space_constraint(x, pltpu.VMEM) for x in (x, done)])


def phase_kernel(spec, *refs):
    groups, arrays, do_w, w_from, attn, has_before, fresh_w, fresh_out, squares = spec[:9]
    rows, begin = spec[9:]
    refs = list(refs)
    table_ref, me_ref, heads_ref = refs.pop(0), refs.pop(0), refs.pop(0)
    at_ref = refs.pop(0) if do_w else None
    weight_ref = refs.pop(0) if attn else None
    g_refs = [refs.pop(0) for _ in range(arrays)]
    if do_w and not fresh_w:
        refs.pop(0)
    before_ref = refs.pop(0) if has_before else None
    added_ref = refs.pop(0) if squares == "added" else None
    if attn in ("whole", "last") and not fresh_out:
        refs.pop(0)
    w_ref = refs.pop(0) if do_w else None
    total_ref = refs.pop(0) if attn == "part" else None
    out_ref = refs.pop(0) if attn in ("whole", "last") else None
    squares_ref = refs.pop(0)
    if attn in ("whole", "last"):
        total_ref, block_ref, sems = refs
    if has_before:
        if attn == "last":
            total_ref[...] = before_ref[...]
    elif attn:
        total_ref[...] = jnp.zeros_like(total_ref)
    if squares == "added":
        squares_ref[...] = added_ref[...]
    else:
        squares_ref[...] = jnp.zeros_like(squares_ref)

    def body(first, column, pieces, j, carry):
        here = pl.ds(pl.multiple_of(column + j * TILE, TILE), TILE)
        there = pl.ds(pl.multiple_of(first + j * TILE, TILE), TILE)
        g = [g_refs[i][start : start + count, here] for i, start, count in pieces]
        if do_w:
            fresh = jnp.concatenate(g[w_from:], axis=0) if len(g) > w_from + 1 else g[-1]
            w = jnp.dot(at_ref[...], fresh, preferred_element_type=jnp.float32)
            if not fresh_w:
                w = w + w_ref[:, there]
            w_ref[:, there] = w
        if squares:
            folded = jnp.sum((w * w).reshape(w.shape[0] // 8, 8, TILE), axis=0)
            total = squares_ref[...]
            for lane in range(0, TILE, 128):
                total = total + folded[:, lane : lane + 128]
            squares_ref[...] = total
        if attn:
            total_ref[...] += lax.dot_general(
                jnp.concatenate(g, axis=0),
                weight_ref[:, there],
                (((1,), (1,)), ((), ())),
                preferred_element_type=jnp.float32,
            )
        return carry

    for first, width, column, pieces in groups:
        step = functools.partial(body, first, column, pieces)
        lax.fori_loop(0, width // TILE, step, 0)
    if attn in ("whole", "last"):
        total = total_ref[...]
        column = lax.broadcasted_iota(jnp.int32, total.shape, 1)
        live = column < heads_ref[0] * HEAD_DIM
        block_ref[...] = jnp.where(live, total, 0.0).astype(jnp.bfloat16)
        copies = []
        for i in range(total.shape[0] // rows):
            owner = table_ref[me_ref[0], begin + i]
            copies.append(
                pltpu.make_async_copy(
                    block_ref.at[pl.ds(i * rows, rows)],
                    out_ref.at[pl.ds(pl.multiple_of(owner * rows, rows), rows)],
                    sems.at[i],
                )
            )
            copies[-1].start()
        for copy in copies:
            copy.wait()


def phase(
    where, shapes, begin, groups, at=None, w=None,
    weight=None, attn=None, before=None, out=None, squares=None, added=None,
    w_from=0,
):
    slots, capacity, features, rows = shapes
    do_w = at is not None
    arrays, described = [], []
    for first, width, column, pieces in groups:
        placed = []
        for array, start, count in pieces:
            known = [i for i, x in enumerate(arrays) if x is array]
            if not known:
                arrays.append(array)
            placed.append((known[0] if known else len(arrays) - 1, start, count))
        described.append((first, width, column, tuple(placed)))
    height = sum(count for _, _, count in groups[0][3])
    vmem = pl.BlockSpec(memory_space=pltpu.VMEM)
    smem = pl.BlockSpec(memory_space=pltpu.SMEM)
    hbm = pl.BlockSpec(memory_space=pl.ANY)

    args, specs, outs, out_specs, aliases, scratch = [], [], [], [], {}, []

    def add(arg, spec):
        args.append(arg)
        specs.append(spec)

    def add_vmem(arg):
        add(pltpu.with_memory_space_constraint(arg, pltpu.VMEM), vmem)

    for scalar in where:
        add(scalar, smem)
    if do_w:
        add_vmem(at)
    if attn:
        add_vmem(weight)
    for array in arrays:
        add_vmem(array)
    if do_w:
        if w is not None:
            aliases[len(args)] = len(outs)
            add_vmem(w)
        outs.append(pltpu.VMEM((capacity, features), jnp.float32))
        out_specs.append(vmem)
    if before is not None:
        if attn == "part":
            aliases[len(args)] = len(outs)
        add_vmem(before)
    if squares == "added":
        add_vmem(added)
    if attn == "part":
        outs.append(pltpu.VMEM((height, capacity), jnp.float32))
        out_specs.append(vmem)
    elif attn:
        if out is not None:
            aliases[len(args)] = len(outs)
            add(out, hbm)
        outs.append(jax.ShapeDtypeStruct((slots, capacity), jnp.bfloat16))
        out_specs.append(hbm)
        scratch = [
            pltpu.VMEM((height, capacity), jnp.float32),
            pltpu.VMEM((height, capacity), jnp.bfloat16),
            pltpu.SemaphoreType.DMA((height // rows,)),
        ]
    outs.append(pltpu.VMEM((8, 128), jnp.float32))
    out_specs.append(vmem)
    spec = (
        tuple(described), len(arrays), do_w, w_from, attn, before is not None, w is None,
        out is None, squares, rows, begin,
    )
    return pl.pallas_call(
        functools.partial(phase_kernel, spec),
        in_specs=specs,
        out_specs=out_specs,
        out_shape=outs,
        scratch_shapes=scratch,
        input_output_aliases=aliases,
        compiler_params=pltpu.CompilerParams(vmem_limit_bytes=12 * MIB),
        cost_estimate=pl.CostEstimate(
            flops=1,
            bytes_accessed=1,
            transcendentals=0,
        ),
        name="phase_" + "w" * do_w + "_" + str(attn),
    )(*args)


def scale_kernel(parts, w_ref, squares_ref, other_ref, out_ref, block_ref, sems):
    capacity, features = w_ref.shape
    square_sum = jnp.sum(
        jnp.sum(squares_ref[...] + other_ref[...], axis=0, keepdims=True),
        axis=1,
        keepdims=True,
    )
    factor = jnp.minimum(
        1.0, 1.0 / jnp.sqrt(square_sum / (HEADS * HEAD_DIM * features) + 1e-06)
    )
    copies = []
    height = capacity // parts
    for i in range(parts):
        part = pl.ds(i * height, height)
        block_ref[part, :] = (w_ref[part, :] * factor).astype(jnp.bfloat16)
        copies.append(pltpu.make_async_copy(block_ref.at[part], out_ref.at[part], sems.at[i]))
        copies[-1].start()
    for copy in copies:
        copy.wait()


def scaled(w, squares, other):
    capacity, features = w.shape
    vmem = pl.BlockSpec(memory_space=pltpu.VMEM)
    parts = 8
    return pl.pallas_call(
        functools.partial(scale_kernel, parts),
        in_specs=[vmem] * 3,
        out_specs=pl.BlockSpec(memory_space=pl.ANY),
        out_shape=jax.ShapeDtypeStruct((capacity, features), jnp.bfloat16),
        scratch_shapes=[
            pltpu.VMEM((capacity, features), jnp.bfloat16),
            pltpu.SemaphoreType.DMA((parts,)),
        ],
        compiler_params=pltpu.CompilerParams(vmem_limit_bytes=10 * MIB),
        cost_estimate=pl.CostEstimate(
            flops=capacity * features,
            bytes_accessed=2 * capacity * features,
            transcendentals=0,
        ),
        name="scale",
    )(*[pltpu.with_memory_space_constraint(x, pltpu.VMEM) for x in (w, squares, other)])


def after(done, *arrays):
    vmem = pl.BlockSpec(memory_space=pltpu.VMEM)
    return pl.pallas_call(
        lambda *refs: None,
        in_specs=[vmem] * (len(arrays) + 1),
        out_specs=[vmem] * len(arrays),
        out_shape=[pltpu.VMEM(x.shape, x.dtype) for x in arrays],
        input_output_aliases={i: i for i in range(len(arrays))},
        compiler_params=pltpu.CompilerParams(vmem_limit_bytes=MIB),
        name="after",
    )(*[pltpu.with_memory_space_constraint(x, pltpu.VMEM) for x in (*arrays, done)])


def split_kernel(x_ref, left_ref, right_ref, sems):
    half = left_ref.shape[1]
    copies = [
        pltpu.make_async_copy(x_ref.at[:, pl.ds(0, half)], left_ref, sems.at[0]),
        pltpu.make_async_copy(x_ref.at[:, pl.ds(half, half)], right_ref, sems.at[1]),
    ]
    for copy in copies:
        copy.start()
    for copy in copies:
        copy.wait()


def split(x):
    vmem = pl.BlockSpec(memory_space=pltpu.VMEM)
    rows, features = x.shape
    return pl.pallas_call(
        split_kernel,
        in_specs=[vmem],
        out_specs=[vmem] * 2,
        out_shape=[pltpu.VMEM((rows, features // 2), x.dtype)] * 2,
        scratch_shapes=[pltpu.SemaphoreType.DMA((2,))],
        compiler_params=pltpu.CompilerParams(vmem_limit_bytes=MIB),
        name="split",
    )(pltpu.with_memory_space_constraint(x, pltpu.VMEM))


def rounds(devices):
    bits = [1 << i for i in range(devices.bit_length() - 1)]
    if len(bits) >= 4:
        bits = bits[1:3] + [bits[0]] + bits[3:]
    return bits


def sum_kernel(x_ref, y_ref, done_ref, out_ref):
    out_ref[...] = x_ref[...] + y_ref[...]


def summed(done, x, y):
    vmem = pl.BlockSpec(memory_space=pltpu.VMEM)
    return pl.pallas_call(
        sum_kernel,
        in_specs=[vmem] * 3,
        out_specs=vmem,
        out_shape=pltpu.VMEM(x.shape, x.dtype),
        compiler_params=pltpu.CompilerParams(vmem_limit_bytes=MIB),
        name="summed",
    )(*[pltpu.with_memory_space_constraint(x, pltpu.VMEM) for x in (x, y, done)])


def on_device(ring, attn_out, out_grad, o_weight, head_counts, seq_counts):
    rows, features = out_grad.shape
    slots = attn_out.shape[0]
    devices, last = ring.devices, ring.length // 2
    steps = 2 * last
    spans = [(0, 2)]
    for k in range(1, last):
        joint = k < last - 1
        spans += [(4 * k - 2, 4), None] if joint else [(4 * k - 2, 2), (4 * k, 2)]
    spans += [(2 * steps - 2, 1), (2 * steps - 1, 1)]
    me = lax.axis_index("dp").astype(jnp.int32).reshape(1)
    where = (jnp.asarray(ring.owners()), me, head_counts)
    shapes = (slots, o_weight.shape[0], features, rows)
    weight, half = o_weight, features // 2

    def send(x, pairs):
        return lax.ppermute(x, "dp", pairs)

    def swapped(halves):
        return [send(x, ring.swap()) for x in halves]

    def grouped(*pairs):
        return [
            (c * half, half, 0, [(x[c], 0, rows) for x in pairs])
            for c in range(min(len(x) for x in pairs))
        ]

    x = send(out_grad, ring.along())
    own, near, count, ats = prepared(
        where, seq_counts, out_grad, attn_out, [x for x in spans if x]
    )
    ats = [ats.pop(0) if x else None for x in spans]
    y = send(own, ring.crossing())
    counts = send(count, ring.along()), send(count, ring.crossing())
    w, out, done = phase(
        where, shapes, 0, grouped(near, swapped(near)), at=ats[0], weight=weight, attn="whole"
    )

    for k in range(1, last):
        x = arrived(done, counts[0], x) if k == 1 else after(done, x)[0]
        x, near_x = send(x, ring.along()), split(x)
        far_x = swapped(near_x)
        i = 2 * k - 1
        if k == last - 1:
            w, out, done = phase(
                where, shapes, 2 * i, grouped(near_x, far_x), at=ats[i], w=w,
                weight=weight, attn="whole", out=out,
            )
        y = arrived(done, counts[1], y) if k == 1 else after(done, y)[0]
        y, near_y = send(y, ring.along()) if k < last - 1 else None, split(y)
        far_y = swapped(near_y)
        groups = grouped(near_x, far_x, near_y, far_y)
        if k == last - 1:
            w, out, done = phase(
                where, shapes, 2 * (i + 1), grouped(near_y, far_y), at=ats[i + 1], w=w,
                weight=weight, attn="whole", out=out,
            )
        else:
            w, out, done = phase(
                where, shapes, 2 * i, groups, at=ats[i], w=w,
                weight=weight, attn="whole", out=out,
            )

    (x,) = after(done, x)
    near = split(x)
    far = swapped(near)
    begin = 2 * steps - 2
    w, done = phase(where, shapes, begin, grouped(near), at=ats[-2], w=w)
    w, squares = phase(where, shapes, begin, grouped(far), at=ats[-1], w=w, squares="new")

    bits = rounds(devices)
    parts = 4 if len(bits) >= 4 else 1
    width = features // parts
    before = None
    for late, bit in enumerate(bits):
        other = send(squares, [(d, d ^ bit) for d in range(devices)])
        done = squares
        if late < parts:
            first = late * width
            pieces = grouped(near, far)[first // half][3]
            groups = [(first, width, first % half, pieces)]
            if late < parts - 1:
                before, done = phase(
                    where, shapes, begin, groups, weight=weight, attn="part", before=before
                )
            else:
                out, done = phase(
                    where, shapes, begin, groups, weight=weight, attn="last",
                    before=before, out=out,
                )
        if late < len(bits) - 1:
            squares = summed(done, squares, other)
    return out, scaled(w, squares, other)


def solution(mesh):
    placed = (
        P("group", "dp"),
        P(("group", "dp"), None),
        P("dp", None),
        P("dp"),
        P(("group", "dp")),
    )
    ring = Ring(mesh.shape["dp"], 2 if mesh.shape["group"] == 2 else 1)
    return jax.shard_map(
        functools.partial(on_device, ring),
        mesh=mesh,
        in_specs=placed,
        out_specs=(P("group", "dp"), P(("group", "dp"), None)),
        check_vma=False,
    )
```

```python
import functools

import jax
import jax.numpy as jnp
import numpy as np
from jax import lax
from jax.experimental import pallas as pl
from jax.experimental.pallas import tpu as pltpu
from jax.sharding import PartitionSpec as P

HEADS = 64
HEAD_DIM = 128
SEQ = 16
TILE = 1024
MIB = 1024 * 1024


class Ring:
    def __init__(self, devices, columns):
        self.devices = devices
        self.length = devices // 2
        rows = self.length // columns
        if columns == 1:
            self.chips = list(range(rows))
        else:
            self.chips = [2 * z for z in range(rows)]
            self.chips += [2 * z + 1 for z in reversed(range(rows))]
        self.position = {chip: p for p, chip in enumerate(self.chips)}

    def device(self, position, core):
        return 2 * self.chips[position % self.length] + core

    def along(self):
        return [
            (self.device(p, core), self.device(p + 1 - 2 * core, core))
            for p in range(self.length)
            for core in range(2)
        ]

    def crossing(self):
        return [
            (self.device(p, core), self.device(p - 1 + 2 * core, 1 - core))
            for p in range(self.length)
            for core in range(2)
        ]

    def swap(self):
        return [(d, d ^ 1) for d in range(self.devices)]

    def owners(self):
        table, last = [], self.length // 2
        for d in range(self.devices):
            p, core = self.position[d // 2], d % 2
            row = [d, d ^ 1]
            for k in range(1, last + 1):
                step = k if core else -k
                row += [self.device(p + step, core), self.device(p - step, 1 - core)]
                if k < last:
                    row += [self.device(p + step, 1 - core), self.device(p - step, core)]
            table.append(row)
        return np.array(table, np.int32)


def zero_dead(count, ref):
    for s in range(ref.shape[0] // SEQ):

        @pl.when(s >= count)
        def _():
            dead = ref.at[s * SEQ : (s + 1) * SEQ]
            dead[...] = jnp.zeros_like(dead)


def prep_kernel(
    spans, rows, table_ref, me_ref, heads_ref, seqs_ref, grad_ref, a_ref, *refs
):
    copy_ref, left_ref, right_ref, count_ref, *at_refs, block_ref, sems, own_sems = refs
    half = left_ref.shape[1]
    owns = [
        pltpu.make_async_copy(grad_ref, copy_ref, own_sems.at[0]),
        pltpu.make_async_copy(grad_ref.at[:, pl.ds(0, half)], left_ref, own_sems.at[1]),
        pltpu.make_async_copy(grad_ref.at[:, pl.ds(half, half)], right_ref, own_sems.at[2]),
    ]
    for copy in owns:
        copy.start()
    count_ref[...] = jnp.full(count_ref.shape, seqs_ref[0], jnp.int32)
    width = heads_ref[0] * HEAD_DIM
    copies = []
    for i in range(block_ref.shape[0] // rows):
        owner = table_ref[me_ref[0], i]
        copies.append(
            pltpu.make_async_copy(
                a_ref.at[pl.ds(pl.multiple_of(owner * rows, rows), rows)],
                block_ref.at[pl.ds(i * rows, rows)],
                sems.at[i],
            )
        )
        copies[-1].start()
    waited = 0
    for at_ref, (begin, count) in zip(at_refs, spans):
        for copy in copies[waited : begin + count]:
            copy.wait()
        waited = max(waited, begin + count)
        block = block_ref[begin * rows : (begin + count) * rows, :]
        column = lax.broadcasted_iota(jnp.int32, block.shape, 1)
        at_ref[...] = jnp.where(column < width, block, jnp.zeros_like(block)).T
    for copy in owns:
        copy.wait()
    zero_dead(seqs_ref[0], left_ref)
    zero_dead(seqs_ref[0], right_ref)


def prepared(where, seq_counts, out_grad, attn_out, spans):
    slots, capacity = attn_out.shape
    rows, features = out_grad.shape
    vmem = pl.BlockSpec(memory_space=pltpu.VMEM)
    smem = pl.BlockSpec(memory_space=pltpu.SMEM)
    outs = [(rows, features), (rows, features // 2), (rows, features // 2)]
    outs += [(capacity, count * rows) for _, count in spans]
    shapes = [pltpu.VMEM(shape, jnp.bfloat16) for shape in outs]
    shapes.insert(3, pltpu.VMEM((8, 128), jnp.int32))
    copy, left, right, count, *ats = pl.pallas_call(
        functools.partial(prep_kernel, spans, rows),
        in_specs=[smem] * 4 + [pl.BlockSpec(memory_space=pl.ANY)] * 2,
        out_specs=[vmem] * len(shapes),
        out_shape=shapes,
        scratch_shapes=[
            pltpu.VMEM((slots, capacity), jnp.bfloat16),
            pltpu.SemaphoreType.DMA((slots // rows,)),
            pltpu.SemaphoreType.DMA((3,)),
        ],
        compiler_params=pltpu.CompilerParams(vmem_limit_bytes=12 * MIB),
        cost_estimate=pl.CostEstimate(flops=1, bytes_accessed=1, transcendentals=0),
        name="prep",
    )(
        *where,
        seq_counts,
        pltpu.with_memory_space_constraint(out_grad, pltpu.HBM),
        pltpu.with_memory_space_constraint(attn_out, pltpu.HBM),
    )
    return copy, (left, right), count, ats


def arrive_kernel(count_ref, x_ref, done_ref, out_ref):
    zero_dead(count_ref[0, 0], out_ref)


def arrived(done, count, x):
    vmem = pl.BlockSpec(memory_space=pltpu.VMEM)
    return pl.pallas_call(
        arrive_kernel,
        in_specs=[pl.BlockSpec(memory_space=pltpu.SMEM), vmem, vmem],
        out_specs=vmem,
        out_shape=pltpu.VMEM(x.shape, x.dtype),
        input_output_aliases={1: 0},
        compiler_params=pltpu.CompilerParams(vmem_limit_bytes=MIB),
        name="arrived",
    )(count, *[pltpu.with_memory_space_constraint(x, pltpu.VMEM) for x in (x, done)])


def phase_kernel(spec, *refs):
    groups, arrays, do_w, w_from, attn, has_before, fresh_w, fresh_out, squares = spec[:9]
    rows, begin = spec[9:]
    refs = list(refs)
    table_ref, me_ref, heads_ref = refs.pop(0), refs.pop(0), refs.pop(0)
    at_ref = refs.pop(0) if do_w else None
    weight_ref = refs.pop(0) if attn else None
    g_refs = [refs.pop(0) for _ in range(arrays)]
    if do_w and not fresh_w:
        refs.pop(0)
    before_ref = refs.pop(0) if has_before else None
    added_ref = refs.pop(0) if squares == "added" else None
    if attn in ("whole", "last") and not fresh_out:
        refs.pop(0)
    w_ref = refs.pop(0) if do_w else None
    total_ref = refs.pop(0) if attn == "part" else None
    out_ref = refs.pop(0) if attn in ("whole", "last") else None
    squares_ref = refs.pop(0)
    if attn in ("whole", "last"):
        total_ref, block_ref, sems = refs
    if has_before:
        if attn == "last":
            total_ref[...] = before_ref[...]
    elif attn:
        total_ref[...] = jnp.zeros_like(total_ref)
    if squares == "added":
        squares_ref[...] = added_ref[...]
    else:
        squares_ref[...] = jnp.zeros_like(squares_ref)

    def body(first, column, pieces, j, carry):
        here = pl.ds(pl.multiple_of(column + j * TILE, TILE), TILE)
        there = pl.ds(pl.multiple_of(first + j * TILE, TILE), TILE)
        g = [g_refs[i][start : start + count, here] for i, start, count in pieces]
        if do_w:
            fresh = jnp.concatenate(g[w_from:], axis=0) if len(g) > w_from + 1 else g[-1]
            w = jnp.dot(at_ref[...], fresh, preferred_element_type=jnp.float32)
            if not fresh_w:
                w = w + w_ref[:, there]
            w_ref[:, there] = w
        if squares:
            folded = jnp.sum((w * w).reshape(w.shape[0] // 8, 8, TILE), axis=0)
            total = squares_ref[...]
            for lane in range(0, TILE, 128):
                total = total + folded[:, lane : lane + 128]
            squares_ref[...] = total
        if attn:
            total_ref[...] += lax.dot_general(
                jnp.concatenate(g, axis=0),
                weight_ref[:, there],
                (((1,), (1,)), ((), ())),
                preferred_element_type=jnp.float32,
            )
        return carry

    for first, width, column, pieces in groups:
        step = functools.partial(body, first, column, pieces)
        lax.fori_loop(0, width // TILE, step, 0)
    if attn in ("whole", "last"):
        total = total_ref[...]
        column = lax.broadcasted_iota(jnp.int32, total.shape, 1)
        live = column < heads_ref[0] * HEAD_DIM
        block_ref[...] = jnp.where(live, total, 0.0).astype(jnp.bfloat16)
        copies = []
        for i in range(total.shape[0] // rows):
            owner = table_ref[me_ref[0], begin + i]
            copies.append(
                pltpu.make_async_copy(
                    block_ref.at[pl.ds(i * rows, rows)],
                    out_ref.at[pl.ds(pl.multiple_of(owner * rows, rows), rows)],
                    sems.at[i],
                )
            )
            copies[-1].start()
        for copy in copies:
            copy.wait()


def phase(
    where, shapes, begin, groups, at=None, w=None,
    weight=None, attn=None, before=None, out=None, squares=None, added=None,
    w_from=0,
):
    slots, capacity, features, rows = shapes
    do_w = at is not None
    arrays, described = [], []
    for first, width, column, pieces in groups:
        placed = []
        for array, start, count in pieces:
            known = [i for i, x in enumerate(arrays) if x is array]
            if not known:
                arrays.append(array)
            placed.append((known[0] if known else len(arrays) - 1, start, count))
        described.append((first, width, column, tuple(placed)))
    height = sum(count for _, _, count in groups[0][3])
    vmem = pl.BlockSpec(memory_space=pltpu.VMEM)
    smem = pl.BlockSpec(memory_space=pltpu.SMEM)
    hbm = pl.BlockSpec(memory_space=pl.ANY)

    args, specs, outs, out_specs, aliases, scratch = [], [], [], [], {}, []

    def add(arg, spec):
        args.append(arg)
        specs.append(spec)

    def add_vmem(arg):
        add(pltpu.with_memory_space_constraint(arg, pltpu.VMEM), vmem)

    for scalar in where:
        add(scalar, smem)
    if do_w:
        add_vmem(at)
    if attn:
        add_vmem(weight)
    for array in arrays:
        add_vmem(array)
    if do_w:
        if w is not None:
            aliases[len(args)] = len(outs)
            add_vmem(w)
        outs.append(pltpu.VMEM((capacity, features), jnp.float32))
        out_specs.append(vmem)
    if before is not None:
        if attn == "part":
            aliases[len(args)] = len(outs)
        add_vmem(before)
    if squares == "added":
        add_vmem(added)
    if attn == "part":
        outs.append(pltpu.VMEM((height, capacity), jnp.float32))
        out_specs.append(vmem)
    elif attn:
        if out is not None:
            aliases[len(args)] = len(outs)
            add(out, hbm)
        outs.append(jax.ShapeDtypeStruct((slots, capacity), jnp.bfloat16))
        out_specs.append(hbm)
        scratch = [
            pltpu.VMEM((height, capacity), jnp.float32),
            pltpu.VMEM((height, capacity), jnp.bfloat16),
            pltpu.SemaphoreType.DMA((height // rows,)),
        ]
    outs.append(pltpu.VMEM((8, 128), jnp.float32))
    out_specs.append(vmem)
    spec = (
        tuple(described), len(arrays), do_w, w_from, attn, before is not None, w is None,
        out is None, squares, rows, begin,
    )
    return pl.pallas_call(
        functools.partial(phase_kernel, spec),
        in_specs=specs,
        out_specs=out_specs,
        out_shape=outs,
        scratch_shapes=scratch,
        input_output_aliases=aliases,
        compiler_params=pltpu.CompilerParams(vmem_limit_bytes=12 * MIB),
        cost_estimate=pl.CostEstimate(
            flops=1,
            bytes_accessed=1,
            transcendentals=0,
        ),
        name="phase_" + "w" * do_w + "_" + str(attn),
    )(*args)


def finish_kernel(
    parts, begin, table_ref, me_ref, heads_ref, w_ref, squares_ref, weight_ref,
    near_ref, far_ref, before_ref, _, out_ref, grad_ref, scaled_ref, rows_ref, sems, row_sems,
):
    capacity, features = w_ref.shape
    square_sum = jnp.sum(
        jnp.sum(squares_ref[...], axis=0, keepdims=True), axis=1, keepdims=True
    )
    factor = jnp.minimum(
        1.0, 1.0 / jnp.sqrt(square_sum / (HEADS * HEAD_DIM * features) + 1e-06)
    )
    copies = []
    height = capacity // parts
    for i in range(parts):
        part = pl.ds(i * height, height)
        scaled_ref[part, :] = (w_ref[part, :] * factor).astype(jnp.bfloat16)
        copies.append(pltpu.make_async_copy(scaled_ref.at[part], grad_ref.at[part], sems.at[i]))
        copies[-1].start()
    rows, half = near_ref.shape
    total = before_ref[...]
    for start in range(0, half, TILE):
        here = slice(start, start + TILE)
        there = slice(features - half + start, features - half + start + TILE)
        total = total + lax.dot_general(
            jnp.concatenate([near_ref[:, here], far_ref[:, here]], axis=0),
            weight_ref[:, there],
            (((1,), (1,)), ((), ())),
            preferred_element_type=jnp.float32,
        )
    column = lax.broadcasted_iota(jnp.int32, total.shape, 1)
    live = column < heads_ref[0] * HEAD_DIM
    rows_ref[...] = jnp.where(live, total, 0.0).astype(jnp.bfloat16)
    for i in range(2):
        owner = table_ref[me_ref[0], begin + i]
        target = out_ref.at[pl.ds(pl.multiple_of(owner * rows, rows), rows)]
        copies.append(
            pltpu.make_async_copy(rows_ref.at[pl.ds(i * rows, rows)], target, row_sems.at[i])
        )
        copies[-1].start()
    for copy in copies:
        copy.wait()


def finished(where, begin, w, squares, weight, near, far, before, out):
    capacity, features = w.shape
    rows = near.shape[0]
    vmem = pl.BlockSpec(memory_space=pltpu.VMEM)
    smem = pl.BlockSpec(memory_space=pltpu.SMEM)
    hbm = pl.BlockSpec(memory_space=pl.ANY)
    parts = 8
    arrays = (w, squares, weight, near, far, before)
    return pl.pallas_call(
        functools.partial(finish_kernel, parts, begin),
        in_specs=[smem] * 3 + [vmem] * len(arrays) + [hbm],
        out_specs=[hbm] * 2,
        out_shape=[
            jax.ShapeDtypeStruct(out.shape, out.dtype),
            jax.ShapeDtypeStruct((capacity, features), jnp.bfloat16),
        ],
        scratch_shapes=[
            pltpu.VMEM((capacity, features), jnp.bfloat16),
            pltpu.VMEM((2 * rows, capacity), jnp.bfloat16),
            pltpu.SemaphoreType.DMA((parts,)),
            pltpu.SemaphoreType.DMA((2,)),
        ],
        input_output_aliases={3 + len(arrays): 0},
        compiler_params=pltpu.CompilerParams(vmem_limit_bytes=14 * MIB),
        cost_estimate=pl.CostEstimate(
            flops=capacity * features,
            bytes_accessed=2 * capacity * features,
            transcendentals=0,
        ),
        name="finish",
    )(*where, *[pltpu.with_memory_space_constraint(x, pltpu.VMEM) for x in arrays], out)


def after(done, *arrays):
    vmem = pl.BlockSpec(memory_space=pltpu.VMEM)
    return pl.pallas_call(
        lambda *refs: None,
        in_specs=[vmem] * (len(arrays) + 1),
        out_specs=[vmem] * len(arrays),
        out_shape=[pltpu.VMEM(x.shape, x.dtype) for x in arrays],
        input_output_aliases={i: i for i in range(len(arrays))},
        compiler_params=pltpu.CompilerParams(vmem_limit_bytes=MIB),
        name="after",
    )(*[pltpu.with_memory_space_constraint(x, pltpu.VMEM) for x in (*arrays, done)])


def split_kernel(x_ref, left_ref, right_ref, sems):
    half = left_ref.shape[1]
    copies = [
        pltpu.make_async_copy(x_ref.at[:, pl.ds(0, half)], left_ref, sems.at[0]),
        pltpu.make_async_copy(x_ref.at[:, pl.ds(half, half)], right_ref, sems.at[1]),
    ]
    for copy in copies:
        copy.start()
    for copy in copies:
        copy.wait()


def split(x):
    vmem = pl.BlockSpec(memory_space=pltpu.VMEM)
    rows, features = x.shape
    return pl.pallas_call(
        split_kernel,
        in_specs=[vmem],
        out_specs=[vmem] * 2,
        out_shape=[pltpu.VMEM((rows, features // 2), x.dtype)] * 2,
        scratch_shapes=[pltpu.SemaphoreType.DMA((2,))],
        compiler_params=pltpu.CompilerParams(vmem_limit_bytes=MIB),
        name="split",
    )(pltpu.with_memory_space_constraint(x, pltpu.VMEM))


def rounds(devices):
    bits = [1 << i for i in range(devices.bit_length() - 1)]
    if len(bits) >= 4:
        bits = bits[1:3] + [bits[0]] + bits[3:]
    masks = []
    while bits:
        pair, bits = bits[:2], bits[2:]
        masks.append(pair + [sum(pair)] if len(pair) == 2 else pair)
    return masks


def exchange(x, devices, masks):
    total = x
    for mask in masks:
        total = total + lax.ppermute(x, "dp", [(d, d ^ mask) for d in range(devices)])
    return total


def on_device(ring, attn_out, out_grad, o_weight, head_counts, seq_counts):
    rows, features = out_grad.shape
    slots = attn_out.shape[0]
    devices, last = ring.devices, ring.length // 2
    steps = 2 * last
    spans = [(0, 2)]
    for k in range(1, last):
        joint = k < last - 1
        spans += [(4 * k - 2, 4), None] if joint else [(4 * k - 2, 2), (4 * k, 2)]
    spans += [(2 * steps - 2, 1), (2 * steps - 1, 1)]
    me = lax.axis_index("dp").astype(jnp.int32).reshape(1)
    where = (jnp.asarray(ring.owners()), me, head_counts)
    shapes = (slots, o_weight.shape[0], features, rows)
    weight, half = o_weight, features // 2

    def send(x, pairs):
        return lax.ppermute(x, "dp", pairs)

    def swapped(halves):
        return [send(x, ring.swap()) for x in halves]

    def grouped(*pairs):
        return [
            (c * half, half, 0, [(x[c], 0, rows) for x in pairs])
            for c in range(min(len(x) for x in pairs))
        ]

    x = send(out_grad, ring.along())
    own, near, count, ats = prepared(
        where, seq_counts, out_grad, attn_out, [x for x in spans if x]
    )
    ats = [ats.pop(0) if x else None for x in spans]
    y = send(own, ring.crossing())
    counts = send(count, ring.along()), send(count, ring.crossing())
    w, out, done = phase(
        where, shapes, 0, grouped(near, swapped(near)), at=ats[0], weight=weight, attn="whole"
    )

    for k in range(1, last):
        x = arrived(done, counts[0], x) if k == 1 else after(done, x)[0]
        x, near_x = send(x, ring.along()), split(x)
        far_x = swapped(near_x)
        i = 2 * k - 1
        if k == last - 1:
            w, out, done = phase(
                where, shapes, 2 * i, grouped(near_x, far_x), at=ats[i], w=w,
                weight=weight, attn="whole", out=out,
            )
        y = arrived(done, counts[1], y) if k == 1 else after(done, y)[0]
        y, near_y = send(y, ring.along()) if k < last - 1 else None, split(y)
        far_y = swapped(near_y)
        groups = grouped(near_x, far_x, near_y, far_y)
        if k == last - 1:
            w, out, done = phase(
                where, shapes, 2 * (i + 1), grouped(near_y, far_y), at=ats[i + 1], w=w,
                weight=weight, attn="whole", out=out,
            )
        else:
            w, out, done = phase(
                where, shapes, 2 * i, groups, at=ats[i], w=w,
                weight=weight, attn="whole", out=out,
            )

    (x,) = after(done, x)
    near = split(x)
    far = swapped(near)
    begin = 2 * steps - 2
    w, done = phase(where, shapes, begin, grouped(near), at=ats[-2], w=w)
    w, squares = phase(where, shapes, begin, grouped(far), at=ats[-1], w=w, squares="new")

    before, part = None, half // 2
    for late, masks in enumerate(rounds(devices)):
        squares = exchange(squares, devices, masks)
        if late < 2:
            groups = [(late * part, part, late * part, grouped(near, far)[0][3])]
            before, done = phase(
                where, shapes, begin, groups, weight=weight, attn="part", before=before
            )
            (squares,) = after(done, squares)
    return finished(
        where, begin, w, squares, weight, near[1], far[1], before, out
    )


def solution(mesh):
    placed = (
        P("group", "dp"),
        P(("group", "dp"), None),
        P("dp", None),
        P("dp"),
        P(("group", "dp")),
    )
    ring = Ring(mesh.shape["dp"], 2 if mesh.shape["group"] == 2 else 1)
    return jax.shard_map(
        functools.partial(on_device, ring),
        mesh=mesh,
        in_specs=placed,
        out_specs=(P("group", "dp"), P(("group", "dp"), None)),
        check_vma=False,
    )
```

```python
import functools

import jax
import jax.numpy as jnp
import numpy as np
from jax import lax
from jax.experimental import pallas as pl
from jax.experimental.pallas import tpu as pltpu
from jax.sharding import PartitionSpec as P

HEADS = 64
HEAD_DIM = 128
SEQ = 16
TILE = 1024
MIB = 1024 * 1024


class Ring:
    def __init__(self, devices, columns):
        self.devices = devices
        self.length = devices // 2
        rows = self.length // columns
        if columns == 1:
            self.chips = list(range(rows))
        else:
            self.chips = [2 * z for z in range(rows)]
            self.chips += [2 * z + 1 for z in reversed(range(rows))]
        self.position = {chip: p for p, chip in enumerate(self.chips)}

    def device(self, position, core):
        return 2 * self.chips[position % self.length] + core

    def along(self):
        return [
            (self.device(p, core), self.device(p + 1 - 2 * core, core))
            for p in range(self.length)
            for core in range(2)
        ]

    def crossing(self):
        return [
            (self.device(p, core), self.device(p - 1 + 2 * core, 1 - core))
            for p in range(self.length)
            for core in range(2)
        ]

    def swap(self):
        return [(d, d ^ 1) for d in range(self.devices)]

    def owners(self):
        table, last = [], self.length // 2
        for d in range(self.devices):
            p, core = self.position[d // 2], d % 2
            row = [d, d ^ 1]
            for k in range(1, last + 1):
                step = k if core else -k
                row += [self.device(p + step, core), self.device(p - step, 1 - core)]
                if k < last:
                    row += [self.device(p + step, 1 - core), self.device(p - step, core)]
            table.append(row)
        return np.array(table, np.int32)


def zero_dead(count, ref):
    for s in range(ref.shape[0] // SEQ):

        @pl.when(s >= count)
        def _():
            dead = ref.at[s * SEQ : (s + 1) * SEQ]
            dead[...] = jnp.zeros_like(dead)


def prep_kernel(
    spans, rows, table_ref, me_ref, heads_ref, seqs_ref, grad_ref, a_ref, *refs
):
    copy_ref, left_ref, right_ref, count_ref, *at_refs, block_ref, sems, own_sems = refs
    half = left_ref.shape[1]
    owns = [
        pltpu.make_async_copy(grad_ref, copy_ref, own_sems.at[0]),
        pltpu.make_async_copy(grad_ref.at[:, pl.ds(0, half)], left_ref, own_sems.at[1]),
        pltpu.make_async_copy(grad_ref.at[:, pl.ds(half, half)], right_ref, own_sems.at[2]),
    ]
    for copy in owns:
        copy.start()
    count_ref[...] = jnp.full(count_ref.shape, seqs_ref[0], jnp.int32)
    width = heads_ref[0] * HEAD_DIM
    copies = []
    for i in range(block_ref.shape[0] // rows):
        owner = table_ref[me_ref[0], i]
        copies.append(
            pltpu.make_async_copy(
                a_ref.at[pl.ds(pl.multiple_of(owner * rows, rows), rows)],
                block_ref.at[pl.ds(i * rows, rows)],
                sems.at[i],
            )
        )
        copies[-1].start()
    waited = 0
    for at_ref, (begin, count) in zip(at_refs, spans):
        for copy in copies[waited : begin + count]:
            copy.wait()
        waited = max(waited, begin + count)
        block = block_ref[begin * rows : (begin + count) * rows, :]
        column = lax.broadcasted_iota(jnp.int32, block.shape, 1)
        at_ref[...] = jnp.where(column < width, block, jnp.zeros_like(block)).T
    for copy in owns:
        copy.wait()
    zero_dead(seqs_ref[0], left_ref)
    zero_dead(seqs_ref[0], right_ref)


def prepared(where, seq_counts, out_grad, attn_out, spans):
    slots, capacity = attn_out.shape
    rows, features = out_grad.shape
    vmem = pl.BlockSpec(memory_space=pltpu.VMEM)
    smem = pl.BlockSpec(memory_space=pltpu.SMEM)
    outs = [(rows, features), (rows, features // 2), (rows, features // 2)]
    outs += [(capacity, count * rows) for _, count in spans]
    shapes = [pltpu.VMEM(shape, jnp.bfloat16) for shape in outs]
    shapes.insert(3, pltpu.VMEM((8, 128), jnp.int32))
    copy, left, right, count, *ats = pl.pallas_call(
        functools.partial(prep_kernel, spans, rows),
        in_specs=[smem] * 4 + [pl.BlockSpec(memory_space=pl.ANY)] * 2,
        out_specs=[vmem] * len(shapes),
        out_shape=shapes,
        scratch_shapes=[
            pltpu.VMEM((slots, capacity), jnp.bfloat16),
            pltpu.SemaphoreType.DMA((slots // rows,)),
            pltpu.SemaphoreType.DMA((3,)),
        ],
        compiler_params=pltpu.CompilerParams(vmem_limit_bytes=12 * MIB),
        cost_estimate=pl.CostEstimate(flops=1, bytes_accessed=1, transcendentals=0),
        name="prep",
    )(
        *where,
        seq_counts,
        pltpu.with_memory_space_constraint(out_grad, pltpu.HBM),
        pltpu.with_memory_space_constraint(attn_out, pltpu.HBM),
    )
    return copy, (left, right), count, ats


def arrive_kernel(count_ref, x_ref, done_ref, out_ref):
    zero_dead(count_ref[0, 0], out_ref)


def arrived(done, count, x):
    vmem = pl.BlockSpec(memory_space=pltpu.VMEM)
    return pl.pallas_call(
        arrive_kernel,
        in_specs=[pl.BlockSpec(memory_space=pltpu.SMEM), vmem, vmem],
        out_specs=vmem,
        out_shape=pltpu.VMEM(x.shape, x.dtype),
        input_output_aliases={1: 0},
        compiler_params=pltpu.CompilerParams(vmem_limit_bytes=MIB),
        name="arrived",
    )(count, *[pltpu.with_memory_space_constraint(x, pltpu.VMEM) for x in (x, done)])


def phase_kernel(spec, *refs):
    groups, arrays, do_w, w_from, attn, fresh_w, fresh_out, squares, rows, begin = spec
    refs = list(refs)
    table_ref, me_ref, heads_ref = refs.pop(0), refs.pop(0), refs.pop(0)
    at_ref = refs.pop(0) if do_w else None
    weight_ref = refs.pop(0) if attn else None
    g_refs = [refs.pop(0) for _ in range(arrays)]
    if do_w and not fresh_w:
        refs.pop(0)
    before_ref = refs.pop(0) if attn == "last" else None
    added_ref = refs.pop(0) if squares == "added" else None
    if attn in ("whole", "last") and not fresh_out:
        refs.pop(0)
    w_ref = refs.pop(0) if do_w else None
    total_ref = refs.pop(0) if attn == "first" else None
    out_ref = refs.pop(0) if attn in ("whole", "last") else None
    squares_ref = refs.pop(0)
    if attn in ("whole", "last"):
        total_ref, block_ref, sems = refs
    if attn == "last":
        total_ref[...] = before_ref[...]
    elif attn:
        total_ref[...] = jnp.zeros_like(total_ref)
    if squares == "added":
        squares_ref[...] = added_ref[...]
    else:
        squares_ref[...] = jnp.zeros_like(squares_ref)

    def body(first, column, pieces, j, carry):
        here = pl.ds(pl.multiple_of(column + j * TILE, TILE), TILE)
        there = pl.ds(pl.multiple_of(first + j * TILE, TILE), TILE)
        g = [g_refs[i][start : start + count, here] for i, start, count in pieces]
        if do_w:
            fresh = jnp.concatenate(g[w_from:], axis=0) if len(g) > w_from + 1 else g[-1]
            w = jnp.dot(at_ref[...], fresh, preferred_element_type=jnp.float32)
            if not fresh_w:
                w = w + w_ref[:, there]
            w_ref[:, there] = w
        if squares:
            folded = jnp.sum((w * w).reshape(w.shape[0] // 8, 8, TILE), axis=0)
            total = squares_ref[...]
            for lane in range(0, TILE, 128):
                total = total + folded[:, lane : lane + 128]
            squares_ref[...] = total
        if attn:
            total_ref[...] += lax.dot_general(
                jnp.concatenate(g, axis=0),
                weight_ref[:, there],
                (((1,), (1,)), ((), ())),
                preferred_element_type=jnp.float32,
            )
        return carry

    for first, width, column, pieces in groups:
        step = functools.partial(body, first, column, pieces)
        lax.fori_loop(0, width // TILE, step, 0)
    if attn in ("whole", "last"):
        total = total_ref[...]
        column = lax.broadcasted_iota(jnp.int32, total.shape, 1)
        live = column < heads_ref[0] * HEAD_DIM
        block_ref[...] = jnp.where(live, total, 0.0).astype(jnp.bfloat16)
        copies = []
        for i in range(total.shape[0] // rows):
            owner = table_ref[me_ref[0], begin + i]
            copies.append(
                pltpu.make_async_copy(
                    block_ref.at[pl.ds(i * rows, rows)],
                    out_ref.at[pl.ds(pl.multiple_of(owner * rows, rows), rows)],
                    sems.at[i],
                )
            )
            copies[-1].start()
        for copy in copies:
            copy.wait()


def phase(
    where, shapes, begin, groups, at=None, w=None,
    weight=None, attn=None, before=None, out=None, squares=None, added=None,
    w_from=0,
):
    slots, capacity, features, rows = shapes
    do_w = at is not None
    arrays, described = [], []
    for first, width, column, pieces in groups:
        placed = []
        for array, start, count in pieces:
            known = [i for i, x in enumerate(arrays) if x is array]
            if not known:
                arrays.append(array)
            placed.append((known[0] if known else len(arrays) - 1, start, count))
        described.append((first, width, column, tuple(placed)))
    height = sum(count for _, _, count in groups[0][3])
    vmem = pl.BlockSpec(memory_space=pltpu.VMEM)
    smem = pl.BlockSpec(memory_space=pltpu.SMEM)
    hbm = pl.BlockSpec(memory_space=pl.ANY)

    args, specs, outs, out_specs, aliases, scratch = [], [], [], [], {}, []

    def add(arg, spec):
        args.append(arg)
        specs.append(spec)

    def add_vmem(arg):
        add(pltpu.with_memory_space_constraint(arg, pltpu.VMEM), vmem)

    for scalar in where:
        add(scalar, smem)
    if do_w:
        add_vmem(at)
    if attn:
        add_vmem(weight)
    for array in arrays:
        add_vmem(array)
    if do_w:
        if w is not None:
            aliases[len(args)] = len(outs)
            add_vmem(w)
        outs.append(pltpu.VMEM((capacity, features), jnp.float32))
        out_specs.append(vmem)
    if attn == "last":
        add_vmem(before)
    if squares == "added":
        add_vmem(added)
    if attn == "first":
        outs.append(pltpu.VMEM((height, capacity), jnp.float32))
        out_specs.append(vmem)
    elif attn:
        if out is not None:
            aliases[len(args)] = len(outs)
            add(out, hbm)
        outs.append(jax.ShapeDtypeStruct((slots, capacity), jnp.bfloat16))
        out_specs.append(hbm)
        scratch = [
            pltpu.VMEM((height, capacity), jnp.float32),
            pltpu.VMEM((height, capacity), jnp.bfloat16),
            pltpu.SemaphoreType.DMA((height // rows,)),
        ]
    outs.append(pltpu.VMEM((8, 128), jnp.float32))
    out_specs.append(vmem)
    spec = (
        tuple(described), len(arrays), do_w, w_from, attn, w is None, out is None,
        squares, rows, begin,
    )
    return pl.pallas_call(
        functools.partial(phase_kernel, spec),
        in_specs=specs,
        out_specs=out_specs,
        out_shape=outs,
        scratch_shapes=scratch,
        input_output_aliases=aliases,
        compiler_params=pltpu.CompilerParams(vmem_limit_bytes=12 * MIB),
        cost_estimate=pl.CostEstimate(
            flops=1,
            bytes_accessed=1,
            transcendentals=0,
        ),
        name="phase_" + "w" * do_w + "_" + str(attn),
    )(*args)


def scale_kernel(parts, w_ref, squares_ref, out_ref, block_ref, sems):
    capacity, features = w_ref.shape
    square_sum = jnp.sum(
        jnp.sum(squares_ref[...], axis=0, keepdims=True), axis=1, keepdims=True
    )
    factor = jnp.minimum(
        1.0, 1.0 / jnp.sqrt(square_sum / (HEADS * HEAD_DIM * features) + 1e-06)
    )
    copies = []
    height = capacity // parts
    for i in range(parts):
        part = pl.ds(i * height, height)
        block_ref[part, :] = (w_ref[part, :] * factor).astype(jnp.bfloat16)
        copies.append(pltpu.make_async_copy(block_ref.at[part], out_ref.at[part], sems.at[i]))
        copies[-1].start()
    for copy in copies:
        copy.wait()


def scaled(w, squares):
    capacity, features = w.shape
    vmem = pl.BlockSpec(memory_space=pltpu.VMEM)
    parts = capacity // 48
    return pl.pallas_call(
        functools.partial(scale_kernel, parts),
        in_specs=[vmem, vmem],
        out_specs=pl.BlockSpec(memory_space=pl.ANY),
        out_shape=jax.ShapeDtypeStruct((capacity, features), jnp.bfloat16),
        scratch_shapes=[
            pltpu.VMEM((capacity, features), jnp.bfloat16),
            pltpu.SemaphoreType.DMA((parts,)),
        ],
        compiler_params=pltpu.CompilerParams(vmem_limit_bytes=10 * MIB),
        cost_estimate=pl.CostEstimate(
            flops=capacity * features,
            bytes_accessed=2 * capacity * features,
            transcendentals=0,
        ),
        name="scale",
    )(pltpu.with_memory_space_constraint(w, pltpu.VMEM), squares)


def after(done, *arrays):
    vmem = pl.BlockSpec(memory_space=pltpu.VMEM)
    return pl.pallas_call(
        lambda *refs: None,
        in_specs=[vmem] * (len(arrays) + 1),
        out_specs=[vmem] * len(arrays),
        out_shape=[pltpu.VMEM(x.shape, x.dtype) for x in arrays],
        input_output_aliases={i: i for i in range(len(arrays))},
        compiler_params=pltpu.CompilerParams(vmem_limit_bytes=MIB),
        name="after",
    )(*[pltpu.with_memory_space_constraint(x, pltpu.VMEM) for x in (*arrays, done)])


def split_kernel(x_ref, left_ref, right_ref, sems):
    half = left_ref.shape[1]
    copies = [
        pltpu.make_async_copy(x_ref.at[:, pl.ds(0, half)], left_ref, sems.at[0]),
        pltpu.make_async_copy(x_ref.at[:, pl.ds(half, half)], right_ref, sems.at[1]),
    ]
    for copy in copies:
        copy.start()
    for copy in copies:
        copy.wait()


def split(x):
    vmem = pl.BlockSpec(memory_space=pltpu.VMEM)
    rows, features = x.shape
    return pl.pallas_call(
        split_kernel,
        in_specs=[vmem],
        out_specs=[vmem] * 2,
        out_shape=[pltpu.VMEM((rows, features // 2), x.dtype)] * 2,
        scratch_shapes=[pltpu.SemaphoreType.DMA((2,))],
        compiler_params=pltpu.CompilerParams(vmem_limit_bytes=MIB),
        name="split",
    )(pltpu.with_memory_space_constraint(x, pltpu.VMEM))


def rounds(devices):
    bits = [1 << i for i in range(devices.bit_length() - 1)]
    if len(bits) >= 4:
        bits = bits[1:3] + [bits[0]] + bits[3:]
    masks = []
    while bits:
        pair, bits = bits[:2], bits[2:]
        masks.append(pair + [sum(pair)] if len(pair) == 2 else pair)
    return masks


def exchange(x, devices, masks):
    total = x
    for mask in masks:
        total = total + lax.ppermute(x, "dp", [(d, d ^ mask) for d in range(devices)])
    return total


def on_device(ring, attn_out, out_grad, o_weight, head_counts, seq_counts):
    rows, features = out_grad.shape
    slots = attn_out.shape[0]
    devices, last = ring.devices, ring.length // 2
    steps = 2 * last
    spans = [(0, 2)]
    for k in range(1, last):
        joint = k < last - 1
        spans += [(4 * k - 2, 4), None] if joint else [(4 * k - 2, 2), (4 * k, 2)]
    spans += [(2 * steps - 2, 1), (2 * steps - 1, 1)]
    me = lax.axis_index("dp").astype(jnp.int32).reshape(1)
    where = (jnp.asarray(ring.owners()), me, head_counts)
    shapes = (slots, o_weight.shape[0], features, rows)
    weight, half = o_weight, features // 2

    def send(x, pairs):
        return lax.ppermute(x, "dp", pairs)

    def swapped(halves):
        return [send(x, ring.swap()) for x in halves]

    def grouped(*pairs):
        return [
            (c * half, half, 0, [(x[c], 0, rows) for x in pairs])
            for c in range(min(len(x) for x in pairs))
        ]

    x = send(out_grad, ring.along())
    own, near, count, ats = prepared(
        where, seq_counts, out_grad, attn_out, [x for x in spans if x]
    )
    ats = [ats.pop(0) if x else None for x in spans]
    y = send(own, ring.crossing())
    counts = send(count, ring.along()), send(count, ring.crossing())
    w, out, done = phase(
        where, shapes, 0, grouped(near, swapped(near)), at=ats[0], weight=weight, attn="whole"
    )

    for k in range(1, last):
        x = arrived(done, counts[0], x) if k == 1 else after(done, x)[0]
        x, near_x = send(x, ring.along()), split(x)
        far_x = swapped(near_x)
        i = 2 * k - 1
        if k == last - 1:
            w, out, done = phase(
                where, shapes, 2 * i, grouped(near_x, far_x), at=ats[i], w=w,
                weight=weight, attn="whole", out=out,
            )
        y = arrived(done, counts[1], y) if k == 1 else after(done, y)[0]
        y, near_y = send(y, ring.along()) if k < last - 1 else None, split(y)
        far_y = swapped(near_y)
        groups = grouped(near_x, far_x, near_y, far_y)
        if k == last - 1:
            w, out, done = phase(
                where, shapes, 2 * (i + 1), grouped(near_y, far_y), at=ats[i + 1], w=w,
                weight=weight, attn="whole", out=out,
            )
        else:
            w, out, done = phase(
                where, shapes, 2 * i, groups, at=ats[i], w=w,
                weight=weight, attn="whole", out=out,
            )

    (x,) = after(done, x)
    near = split(x)
    far = swapped(near)
    begin = 2 * steps - 2
    w, done = phase(where, shapes, begin, grouped(near), at=ats[-2], w=w)
    w, squares = phase(where, shapes, begin, grouped(far), at=ats[-1], w=w, squares="new")

    pieces = [group[3] for group in grouped(near, far)]
    parts = [
        [(0, half, 0, pieces[0]), (half, half // 2, 0, pieces[1])],
        [(half + half // 2, half // 2, half // 2, pieces[1])],
    ]
    for late, masks in enumerate(rounds(devices)):
        squares = exchange(squares, devices, masks)
        if late == 0:
            before, done = phase(
                where, shapes, begin, parts[0], weight=weight, attn="first"
            )
            (squares,) = after(done, squares)
        elif late == 1:
            out, done = phase(
                where, shapes, begin, parts[1], weight=weight, attn="last",
                before=before, out=out,
            )
    return out, scaled(w, squares)


def solution(mesh):
    placed = (
        P("group", "dp"),
        P(("group", "dp"), None),
        P("dp", None),
        P("dp"),
        P(("group", "dp")),
    )
    ring = Ring(mesh.shape["dp"], 2 if mesh.shape["group"] == 2 else 1)
    return jax.shard_map(
        functools.partial(on_device, ring),
        mesh=mesh,
        in_specs=placed,
        out_specs=(P("group", "dp"), P(("group", "dp"), None)),
        check_vma=False,
    )
```

```python
import functools

import jax
import jax.numpy as jnp
import numpy as np
from jax import lax
from jax.experimental import pallas as pl
from jax.experimental.pallas import tpu as pltpu
from jax.sharding import PartitionSpec as P

HEADS = 64
HEAD_DIM = 128
SEQ = 16
TILE = 1024
MIB = 1024 * 1024


class Ring:
    def __init__(self, devices, columns):
        self.devices = devices
        self.length = devices // 2
        rows = self.length // columns
        if columns == 1:
            self.chips = list(range(rows))
        else:
            self.chips = [2 * z for z in range(rows)]
            self.chips += [2 * z + 1 for z in reversed(range(rows))]
        self.position = {chip: p for p, chip in enumerate(self.chips)}

    def device(self, position, core):
        return 2 * self.chips[position % self.length] + core

    def along(self):
        return [
            (self.device(p, core), self.device(p + 1 - 2 * core, core))
            for p in range(self.length)
            for core in range(2)
        ]

    def crossing(self):
        return [
            (self.device(p, core), self.device(p - 1 + 2 * core, 1 - core))
            for p in range(self.length)
            for core in range(2)
        ]

    def swap(self):
        return [(d, d ^ 1) for d in range(self.devices)]

    def owners(self):
        table, last = [], self.length // 2
        for d in range(self.devices):
            p, core = self.position[d // 2], d % 2
            row = [d, d ^ 1]
            for k in range(1, last + 1):
                step = k if core else -k
                row += [self.device(p + step, core), self.device(p - step, 1 - core)]
                if k < last:
                    row += [self.device(p + step, 1 - core), self.device(p - step, core)]
            table.append(row)
        return np.array(table, np.int32)


def zero_dead(count, ref):
    for s in range(ref.shape[0] // SEQ):

        @pl.when(s >= count)
        def _():
            dead = ref.at[s * SEQ : (s + 1) * SEQ]
            dead[...] = jnp.zeros_like(dead)


def prep_kernel(
    spans, rows, table_ref, me_ref, heads_ref, seqs_ref, grad_ref, a_ref, *refs
):
    copy_ref, left_ref, right_ref, count_ref, *at_refs, block_ref, sems, own_sems = refs
    half = left_ref.shape[1]
    owns = [
        pltpu.make_async_copy(grad_ref, copy_ref, own_sems.at[0]),
        pltpu.make_async_copy(grad_ref.at[:, pl.ds(0, half)], left_ref, own_sems.at[1]),
        pltpu.make_async_copy(grad_ref.at[:, pl.ds(half, half)], right_ref, own_sems.at[2]),
    ]
    for copy in owns:
        copy.start()
    count_ref[...] = jnp.full(count_ref.shape, seqs_ref[0], jnp.int32)
    width = heads_ref[0] * HEAD_DIM
    copies = []
    for i in range(block_ref.shape[0] // rows):
        owner = table_ref[me_ref[0], i]
        copies.append(
            pltpu.make_async_copy(
                a_ref.at[pl.ds(pl.multiple_of(owner * rows, rows), rows)],
                block_ref.at[pl.ds(i * rows, rows)],
                sems.at[i],
            )
        )
        copies[-1].start()
    waited = 0
    for at_ref, (begin, count) in zip(at_refs, spans):
        for copy in copies[waited : begin + count]:
            copy.wait()
        waited = max(waited, begin + count)
        block = block_ref[begin * rows : (begin + count) * rows, :]
        column = lax.broadcasted_iota(jnp.int32, block.shape, 1)
        at_ref[...] = jnp.where(column < width, block, jnp.zeros_like(block)).T
    for copy in owns:
        copy.wait()
    zero_dead(seqs_ref[0], left_ref)
    zero_dead(seqs_ref[0], right_ref)


def prepared(where, seq_counts, out_grad, attn_out, spans):
    slots, capacity = attn_out.shape
    rows, features = out_grad.shape
    vmem = pl.BlockSpec(memory_space=pltpu.VMEM)
    smem = pl.BlockSpec(memory_space=pltpu.SMEM)
    outs = [(rows, features), (rows, features // 2), (rows, features // 2)]
    outs += [(capacity, count * rows) for _, count in spans]
    shapes = [pltpu.VMEM(shape, jnp.bfloat16) for shape in outs]
    shapes.insert(3, pltpu.VMEM((8, 128), jnp.int32))
    copy, left, right, count, *ats = pl.pallas_call(
        functools.partial(prep_kernel, spans, rows),
        in_specs=[smem] * 4 + [pl.BlockSpec(memory_space=pl.ANY)] * 2,
        out_specs=[vmem] * len(shapes),
        out_shape=shapes,
        scratch_shapes=[
            pltpu.VMEM((slots, capacity), jnp.bfloat16),
            pltpu.SemaphoreType.DMA((slots // rows,)),
            pltpu.SemaphoreType.DMA((3,)),
        ],
        compiler_params=pltpu.CompilerParams(vmem_limit_bytes=12 * MIB),
        cost_estimate=pl.CostEstimate(flops=1, bytes_accessed=1, transcendentals=0),
        name="prep",
    )(
        *where,
        seq_counts,
        pltpu.with_memory_space_constraint(out_grad, pltpu.HBM),
        pltpu.with_memory_space_constraint(attn_out, pltpu.HBM),
    )
    return copy, (left, right), count, ats


def arrive_kernel(count_ref, x_ref, done_ref, out_ref):
    zero_dead(count_ref[0, 0], out_ref)


def arrived(done, count, x):
    vmem = pl.BlockSpec(memory_space=pltpu.VMEM)
    return pl.pallas_call(
        arrive_kernel,
        in_specs=[pl.BlockSpec(memory_space=pltpu.SMEM), vmem, vmem],
        out_specs=vmem,
        out_shape=pltpu.VMEM(x.shape, x.dtype),
        input_output_aliases={1: 0},
        compiler_params=pltpu.CompilerParams(vmem_limit_bytes=MIB),
        name="arrived",
    )(count, *[pltpu.with_memory_space_constraint(x, pltpu.VMEM) for x in (x, done)])


def phase_kernel(spec, *refs):
    groups, arrays, do_w, w_from, attn, fresh_w, fresh_out, squares, rows, begin = spec
    refs = list(refs)
    table_ref, me_ref, heads_ref = refs.pop(0), refs.pop(0), refs.pop(0)
    at_ref = refs.pop(0) if do_w else None
    weight_ref = refs.pop(0) if attn else None
    g_refs = [refs.pop(0) for _ in range(arrays)]
    if do_w and not fresh_w:
        refs.pop(0)
    before_ref = refs.pop(0) if attn == "last" else None
    added_ref = refs.pop(0) if squares == "added" else None
    if attn in ("whole", "last") and not fresh_out:
        refs.pop(0)
    w_ref = refs.pop(0) if do_w else None
    total_ref = refs.pop(0) if attn == "first" else None
    out_ref = refs.pop(0) if attn in ("whole", "last") else None
    squares_ref = refs.pop(0)
    if attn in ("whole", "last"):
        total_ref, block_ref, sems = refs
    if attn == "last":
        total_ref[...] = before_ref[...]
    elif attn:
        total_ref[...] = jnp.zeros_like(total_ref)
    if squares == "added":
        squares_ref[...] = added_ref[...]
    else:
        squares_ref[...] = jnp.zeros_like(squares_ref)

    def body(first, column, pieces, j, carry):
        here = pl.ds(pl.multiple_of(column + j * TILE, TILE), TILE)
        there = pl.ds(pl.multiple_of(first + j * TILE, TILE), TILE)
        g = [g_refs[i][start : start + count, here] for i, start, count in pieces]
        if do_w:
            fresh = jnp.concatenate(g[w_from:], axis=0) if len(g) > w_from + 1 else g[-1]
            w = jnp.dot(at_ref[...], fresh, preferred_element_type=jnp.float32)
            if not fresh_w:
                w = w + w_ref[:, there]
            w_ref[:, there] = w
        if squares:
            folded = jnp.sum((w * w).reshape(w.shape[0] // 8, 8, TILE), axis=0)
            total = squares_ref[...]
            for lane in range(0, TILE, 128):
                total = total + folded[:, lane : lane + 128]
            squares_ref[...] = total
        if attn:
            total_ref[...] += lax.dot_general(
                jnp.concatenate(g, axis=0),
                weight_ref[:, there],
                (((1,), (1,)), ((), ())),
                preferred_element_type=jnp.float32,
            )
        return carry

    for first, width, column, pieces in groups:
        step = functools.partial(body, first, column, pieces)
        lax.fori_loop(0, width // TILE, step, 0)
    if attn in ("whole", "last"):
        total = total_ref[...]
        column = lax.broadcasted_iota(jnp.int32, total.shape, 1)
        live = column < heads_ref[0] * HEAD_DIM
        block_ref[...] = jnp.where(live, total, 0.0).astype(jnp.bfloat16)
        copies = []
        for i in range(total.shape[0] // rows):
            owner = table_ref[me_ref[0], begin + i]
            copies.append(
                pltpu.make_async_copy(
                    block_ref.at[pl.ds(i * rows, rows)],
                    out_ref.at[pl.ds(pl.multiple_of(owner * rows, rows), rows)],
                    sems.at[i],
                )
            )
            copies[-1].start()
        for copy in copies:
            copy.wait()


def phase(
    where, shapes, begin, groups, at=None, w=None,
    weight=None, attn=None, before=None, out=None, squares=None, added=None,
    w_from=0,
):
    slots, capacity, features, rows = shapes
    do_w = at is not None
    arrays, described = [], []
    for first, width, column, pieces in groups:
        placed = []
        for array, start, count in pieces:
            known = [i for i, x in enumerate(arrays) if x is array]
            if not known:
                arrays.append(array)
            placed.append((known[0] if known else len(arrays) - 1, start, count))
        described.append((first, width, column, tuple(placed)))
    height = sum(count for _, _, count in groups[0][3])
    vmem = pl.BlockSpec(memory_space=pltpu.VMEM)
    smem = pl.BlockSpec(memory_space=pltpu.SMEM)
    hbm = pl.BlockSpec(memory_space=pl.ANY)

    args, specs, outs, out_specs, aliases, scratch = [], [], [], [], {}, []

    def add(arg, spec):
        args.append(arg)
        specs.append(spec)

    def add_vmem(arg):
        add(pltpu.with_memory_space_constraint(arg, pltpu.VMEM), vmem)

    for scalar in where:
        add(scalar, smem)
    if do_w:
        add_vmem(at)
    if attn:
        add_vmem(weight)
    for array in arrays:
        add_vmem(array)
    if do_w:
        if w is not None:
            aliases[len(args)] = len(outs)
            add_vmem(w)
        outs.append(pltpu.VMEM((capacity, features), jnp.float32))
        out_specs.append(vmem)
    if attn == "last":
        add_vmem(before)
    if squares == "added":
        add_vmem(added)
    if attn == "first":
        outs.append(pltpu.VMEM((height, capacity), jnp.float32))
        out_specs.append(vmem)
    elif attn:
        if out is not None:
            aliases[len(args)] = len(outs)
            add(out, hbm)
        outs.append(jax.ShapeDtypeStruct((slots, capacity), jnp.bfloat16))
        out_specs.append(hbm)
        scratch = [
            pltpu.VMEM((height, capacity), jnp.float32),
            pltpu.VMEM((height, capacity), jnp.bfloat16),
            pltpu.SemaphoreType.DMA((height // rows,)),
        ]
    outs.append(pltpu.VMEM((8, 128), jnp.float32))
    out_specs.append(vmem)
    spec = (
        tuple(described), len(arrays), do_w, w_from, attn, w is None, out is None,
        squares, rows, begin,
    )
    return pl.pallas_call(
        functools.partial(phase_kernel, spec),
        in_specs=specs,
        out_specs=out_specs,
        out_shape=outs,
        scratch_shapes=scratch,
        input_output_aliases=aliases,
        compiler_params=pltpu.CompilerParams(vmem_limit_bytes=12 * MIB),
        cost_estimate=pl.CostEstimate(
            flops=1,
            bytes_accessed=1,
            transcendentals=0,
        ),
        name="phase_" + "w" * do_w + "_" + str(attn),
    )(*args)


def scale_kernel(parts, w_ref, squares_ref, out_ref, block_ref, sems):
    capacity, features = w_ref.shape
    square_sum = jnp.sum(
        jnp.sum(squares_ref[...], axis=0, keepdims=True), axis=1, keepdims=True
    )
    factor = jnp.minimum(
        1.0, 1.0 / jnp.sqrt(square_sum / (HEADS * HEAD_DIM * features) + 1e-06)
    )
    copies = []
    height = capacity // parts
    for i in range(parts):
        part = pl.ds(i * height, height)
        block_ref[part, :] = (w_ref[part, :] * factor).astype(jnp.bfloat16)
        copies.append(pltpu.make_async_copy(block_ref.at[part], out_ref.at[part], sems.at[i]))
        copies[-1].start()
    for copy in copies:
        copy.wait()


def scaled(w, squares):
    capacity, features = w.shape
    vmem = pl.BlockSpec(memory_space=pltpu.VMEM)
    parts = capacity // 48
    return pl.pallas_call(
        functools.partial(scale_kernel, parts),
        in_specs=[vmem, vmem],
        out_specs=pl.BlockSpec(memory_space=pl.ANY),
        out_shape=jax.ShapeDtypeStruct((capacity, features), jnp.bfloat16),
        scratch_shapes=[
            pltpu.VMEM((capacity, features), jnp.bfloat16),
            pltpu.SemaphoreType.DMA((parts,)),
        ],
        compiler_params=pltpu.CompilerParams(vmem_limit_bytes=10 * MIB),
        cost_estimate=pl.CostEstimate(
            flops=capacity * features,
            bytes_accessed=2 * capacity * features,
            transcendentals=0,
        ),
        name="scale",
    )(pltpu.with_memory_space_constraint(w, pltpu.VMEM), squares)


def after(done, *arrays):
    vmem = pl.BlockSpec(memory_space=pltpu.VMEM)
    return pl.pallas_call(
        lambda *refs: None,
        in_specs=[vmem] * (len(arrays) + 1),
        out_specs=[vmem] * len(arrays),
        out_shape=[pltpu.VMEM(x.shape, x.dtype) for x in arrays],
        input_output_aliases={i: i for i in range(len(arrays))},
        compiler_params=pltpu.CompilerParams(vmem_limit_bytes=MIB),
        name="after",
    )(*[pltpu.with_memory_space_constraint(x, pltpu.VMEM) for x in (*arrays, done)])


def split_kernel(x_ref, left_ref, right_ref, sems):
    half = left_ref.shape[1]
    copies = [
        pltpu.make_async_copy(x_ref.at[:, pl.ds(0, half)], left_ref, sems.at[0]),
        pltpu.make_async_copy(x_ref.at[:, pl.ds(half, half)], right_ref, sems.at[1]),
    ]
    for copy in copies:
        copy.start()
    for copy in copies:
        copy.wait()


def split(x):
    vmem = pl.BlockSpec(memory_space=pltpu.VMEM)
    rows, features = x.shape
    return pl.pallas_call(
        split_kernel,
        in_specs=[vmem],
        out_specs=[vmem] * 2,
        out_shape=[pltpu.VMEM((rows, features // 2), x.dtype)] * 2,
        scratch_shapes=[pltpu.SemaphoreType.DMA((2,))],
        compiler_params=pltpu.CompilerParams(vmem_limit_bytes=MIB),
        name="split",
    )(pltpu.with_memory_space_constraint(x, pltpu.VMEM))


def rounds(devices):
    bits = [1 << i for i in range(devices.bit_length() - 1)]
    masks = []
    while bits:
        pair, bits = bits[:2], bits[2:]
        masks.append(pair + [sum(pair)] if len(pair) == 2 else pair)
    return masks


def exchange(x, devices, masks):
    total = x
    for mask in masks:
        total = total + lax.ppermute(x, "dp", [(d, d ^ mask) for d in range(devices)])
    return total


def on_device(ring, attn_out, out_grad, o_weight, head_counts, seq_counts):
    rows, features = out_grad.shape
    slots = attn_out.shape[0]
    devices, last = ring.devices, ring.length // 2
    steps = 2 * last
    spans = [(0, 2)]
    for k in range(1, last):
        joint = k < last - 1
        spans += [(4 * k - 2, 4), None] if joint else [(4 * k - 2, 2), (4 * k, 2)]
    spans += [(2 * steps - 2, 1), (2 * steps - 1, 1)]
    me = lax.axis_index("dp").astype(jnp.int32).reshape(1)
    where = (jnp.asarray(ring.owners()), me, head_counts)
    shapes = (slots, o_weight.shape[0], features, rows)
    weight, half = o_weight, features // 2

    def send(x, pairs):
        return lax.ppermute(x, "dp", pairs)

    def swapped(halves):
        return [send(x, ring.swap()) for x in halves]

    def grouped(*pairs):
        return [
            (c * half, half, 0, [(x[c], 0, rows) for x in pairs])
            for c in range(min(len(x) for x in pairs))
        ]

    x = send(out_grad, ring.along())
    own, near, count, ats = prepared(
        where, seq_counts, out_grad, attn_out, [x for x in spans if x]
    )
    ats = [ats.pop(0) if x else None for x in spans]
    y = send(own, ring.crossing())
    counts = send(count, ring.along()), send(count, ring.crossing())
    w, out, done = phase(
        where, shapes, 0, grouped(near, swapped(near)), at=ats[0], weight=weight, attn="whole"
    )

    for k in range(1, last):
        x = arrived(done, counts[0], x) if k == 1 else after(done, x)[0]
        x, near_x = send(x, ring.along()), split(x)
        far_x = swapped(near_x)
        i = 2 * k - 1
        if k == last - 1:
            w, out, done = phase(
                where, shapes, 2 * i, grouped(near_x, far_x), at=ats[i], w=w,
                weight=weight, attn="whole", out=out,
            )
        y = arrived(done, counts[1], y) if k == 1 else after(done, y)[0]
        y, near_y = send(y, ring.along()) if k < last - 1 else None, split(y)
        far_y = swapped(near_y)
        groups = grouped(near_x, far_x, near_y, far_y)
        if k == last - 1:
            w, out, done = phase(
                where, shapes, 2 * (i + 1), grouped(near_y, far_y), at=ats[i + 1], w=w,
                weight=weight, attn="whole", out=out,
            )
        else:
            w, out, done = phase(
                where, shapes, 2 * i, groups, at=ats[i], w=w,
                weight=weight, attn="whole", out=out,
            )

    (x,) = after(done, x)
    near = split(x)
    far = swapped(near)
    begin = 2 * steps - 2
    w, done = phase(where, shapes, begin, grouped(near), at=ats[-2], w=w)
    w, squares = phase(where, shapes, begin, grouped(far), at=ats[-1], w=w, squares="new")

    pieces = [group[3] for group in grouped(near, far)]
    parts = [[(c * half, half, 0, pieces[c])] for c in range(2)]
    for late, masks in enumerate(rounds(devices)):
        squares = exchange(squares, devices, masks)
        if late == 0:
            before, done = phase(
                where, shapes, begin, parts[0], weight=weight, attn="first"
            )
            (squares,) = after(done, squares)
        elif late == 1:
            out, done = phase(
                where, shapes, begin, parts[1], weight=weight, attn="last",
                before=before, out=out,
            )
    return out, scaled(w, squares)


def solution(mesh):
    placed = (
        P("group", "dp"),
        P(("group", "dp"), None),
        P("dp", None),
        P("dp"),
        P(("group", "dp")),
    )
    ring = Ring(mesh.shape["dp"], 2 if mesh.shape["group"] == 2 else 1)
    return jax.shard_map(
        functools.partial(on_device, ring),
        mesh=mesh,
        in_specs=placed,
        out_specs=(P("group", "dp"), P(("group", "dp"), None)),
        check_vma=False,
    )
```

```python
import functools

import jax
import jax.numpy as jnp
import numpy as np
from jax import lax
from jax.experimental import pallas as pl
from jax.experimental.pallas import tpu as pltpu
from jax.sharding import PartitionSpec as P

HEADS = 64
HEAD_DIM = 128
SEQ = 16
TILE = 1024
MIB = 1024 * 1024


class Ring:
    def __init__(self, devices, columns):
        self.devices = devices
        self.length = devices // 2
        rows = self.length // columns
        if columns == 1:
            self.chips = list(range(rows))
        else:
            self.chips = [2 * z for z in range(rows)]
            self.chips += [2 * z + 1 for z in reversed(range(rows))]
        self.position = {chip: p for p, chip in enumerate(self.chips)}

    def device(self, position, core):
        return 2 * self.chips[position % self.length] + core

    def along(self):
        return [
            (self.device(p, core), self.device(p + 1 - 2 * core, core))
            for p in range(self.length)
            for core in range(2)
        ]

    def crossing(self):
        return [
            (self.device(p, core), self.device(p - 1 + 2 * core, 1 - core))
            for p in range(self.length)
            for core in range(2)
        ]

    def swap(self):
        return [(d, d ^ 1) for d in range(self.devices)]

    def owners(self):
        table, last = [], self.length // 2
        for d in range(self.devices):
            p, core = self.position[d // 2], d % 2
            row = [d, d ^ 1]
            for k in range(1, last + 1):
                step = k if core else -k
                row += [self.device(p + step, core), self.device(p - step, 1 - core)]
                if k < last:
                    row += [self.device(p + step, 1 - core), self.device(p - step, core)]
            table.append(row)
        return np.array(table, np.int32)


def zero_dead(count, ref):
    for s in range(ref.shape[0] // SEQ):

        @pl.when(s >= count)
        def _():
            dead = ref.at[s * SEQ : (s + 1) * SEQ]
            dead[...] = jnp.zeros_like(dead)


def prep_kernel(
    spans, rows, table_ref, me_ref, heads_ref, seqs_ref, grad_ref, a_ref, *refs
):
    copy_ref, left_ref, right_ref, count_ref, *at_refs, block_ref, sems, own_sems = refs
    half = left_ref.shape[1]
    owns = [
        pltpu.make_async_copy(grad_ref, copy_ref, own_sems.at[0]),
        pltpu.make_async_copy(grad_ref.at[:, pl.ds(0, half)], left_ref, own_sems.at[1]),
        pltpu.make_async_copy(grad_ref.at[:, pl.ds(half, half)], right_ref, own_sems.at[2]),
    ]
    for copy in owns:
        copy.start()
    count_ref[...] = jnp.full(count_ref.shape, seqs_ref[0], jnp.int32)
    width = heads_ref[0] * HEAD_DIM
    copies = []
    for i in range(block_ref.shape[0] // rows):
        owner = table_ref[me_ref[0], i]
        copies.append(
            pltpu.make_async_copy(
                a_ref.at[pl.ds(pl.multiple_of(owner * rows, rows), rows)],
                block_ref.at[pl.ds(i * rows, rows)],
                sems.at[i],
            )
        )
        copies[-1].start()
    waited = 0
    for at_ref, (begin, count) in zip(at_refs, spans):
        for copy in copies[waited : begin + count]:
            copy.wait()
        waited = max(waited, begin + count)
        block = block_ref[begin * rows : (begin + count) * rows, :]
        column = lax.broadcasted_iota(jnp.int32, block.shape, 1)
        at_ref[...] = jnp.where(column < width, block, jnp.zeros_like(block)).T
    for copy in owns:
        copy.wait()
    zero_dead(seqs_ref[0], left_ref)
    zero_dead(seqs_ref[0], right_ref)


def prepared(where, seq_counts, out_grad, attn_out, spans):
    slots, capacity = attn_out.shape
    rows, features = out_grad.shape
    vmem = pl.BlockSpec(memory_space=pltpu.VMEM)
    smem = pl.BlockSpec(memory_space=pltpu.SMEM)
    outs = [(rows, features), (rows, features // 2), (rows, features // 2)]
    outs += [(capacity, count * rows) for _, count in spans]
    shapes = [pltpu.VMEM(shape, jnp.bfloat16) for shape in outs]
    shapes.insert(3, pltpu.VMEM((8, 128), jnp.int32))
    copy, left, right, count, *ats = pl.pallas_call(
        functools.partial(prep_kernel, spans, rows),
        in_specs=[smem] * 4 + [pl.BlockSpec(memory_space=pl.ANY)] * 2,
        out_specs=[vmem] * len(shapes),
        out_shape=shapes,
        scratch_shapes=[
            pltpu.VMEM((slots, capacity), jnp.bfloat16),
            pltpu.SemaphoreType.DMA((slots // rows,)),
            pltpu.SemaphoreType.DMA((3,)),
        ],
        compiler_params=pltpu.CompilerParams(vmem_limit_bytes=12 * MIB),
        cost_estimate=pl.CostEstimate(flops=1, bytes_accessed=1, transcendentals=0),
        name="prep",
    )(
        *where,
        seq_counts,
        pltpu.with_memory_space_constraint(out_grad, pltpu.HBM),
        pltpu.with_memory_space_constraint(attn_out, pltpu.HBM),
    )
    return copy, (left, right), count, ats


def arrive_kernel(count_ref, x_ref, done_ref, out_ref):
    zero_dead(count_ref[0, 0], out_ref)


def arrived(done, count, x):
    vmem = pl.BlockSpec(memory_space=pltpu.VMEM)
    return pl.pallas_call(
        arrive_kernel,
        in_specs=[pl.BlockSpec(memory_space=pltpu.SMEM), vmem, vmem],
        out_specs=vmem,
        out_shape=pltpu.VMEM(x.shape, x.dtype),
        input_output_aliases={1: 0},
        compiler_params=pltpu.CompilerParams(vmem_limit_bytes=MIB),
        name="arrived",
    )(count, *[pltpu.with_memory_space_constraint(x, pltpu.VMEM) for x in (x, done)])


def phase_kernel(spec, *refs):
    groups, arrays, do_w, w_from, attn, fresh_w, fresh_out, squares, rows, begin = spec
    refs = list(refs)
    table_ref, me_ref, heads_ref = refs.pop(0), refs.pop(0), refs.pop(0)
    at_ref = refs.pop(0) if do_w else None
    weight_ref = refs.pop(0) if attn else None
    g_refs = [refs.pop(0) for _ in range(arrays)]
    w_before_ref = refs.pop(0) if do_w and not fresh_w else None
    before_ref = refs.pop(0) if attn == "last" else None
    added_ref = refs.pop(0) if squares == "added" else None
    if attn in ("whole", "last") and not fresh_out:
        refs.pop(0)
    w_ref = refs.pop(0) if do_w else None
    total_ref = refs.pop(0) if attn == "first" else None
    out_ref = refs.pop(0) if attn in ("whole", "last") else None
    squares_ref = refs.pop(0)
    if attn in ("whole", "last"):
        total_ref, block_ref, sems = refs
    if attn == "last":
        total_ref[...] = before_ref[...]
    elif attn:
        total_ref[...] = jnp.zeros_like(total_ref)
    if squares == "added":
        squares_ref[...] = added_ref[...]
    else:
        squares_ref[...] = jnp.zeros_like(squares_ref)

    def body(first, column, pieces, j, carry):
        here = pl.ds(pl.multiple_of(column + j * TILE, TILE), TILE)
        there = pl.ds(pl.multiple_of(first + j * TILE, TILE), TILE)
        g = [g_refs[i][start : start + count, here] for i, start, count in pieces]
        if do_w:
            fresh = jnp.concatenate(g[w_from:], axis=0) if len(g) > w_from + 1 else g[-1]
            w = jnp.dot(at_ref[...], fresh, preferred_element_type=jnp.float32)
            if not fresh_w:
                w = w + w_before_ref[:, there]
            w_ref[:, there] = w
        if squares:
            folded = jnp.sum((w * w).reshape(w.shape[0] // 8, 8, TILE), axis=0)
            total = squares_ref[...]
            for lane in range(0, TILE, 128):
                total = total + folded[:, lane : lane + 128]
            squares_ref[...] = total
        if attn:
            total_ref[...] += lax.dot_general(
                jnp.concatenate(g, axis=0),
                weight_ref[:, there],
                (((1,), (1,)), ((), ())),
                preferred_element_type=jnp.float32,
            )
        return carry

    for first, width, column, pieces in groups:
        step = functools.partial(body, first, column, pieces)
        lax.fori_loop(0, width // TILE, step, 0)
    if attn in ("whole", "last"):
        total = total_ref[...]
        column = lax.broadcasted_iota(jnp.int32, total.shape, 1)
        live = column < heads_ref[0] * HEAD_DIM
        block_ref[...] = jnp.where(live, total, 0.0).astype(jnp.bfloat16)
        copies = []
        for i in range(total.shape[0] // rows):
            owner = table_ref[me_ref[0], begin + i]
            copies.append(
                pltpu.make_async_copy(
                    block_ref.at[pl.ds(i * rows, rows)],
                    out_ref.at[pl.ds(pl.multiple_of(owner * rows, rows), rows)],
                    sems.at[i],
                )
            )
            copies[-1].start()
        for copy in copies:
            copy.wait()


def phase(
    where, shapes, begin, groups, at=None, w=None,
    weight=None, attn=None, before=None, out=None, squares=None, added=None,
    w_from=0,
):
    slots, capacity, features, rows = shapes
    do_w = at is not None
    arrays, described = [], []
    for first, width, column, pieces in groups:
        placed = []
        for array, start, count in pieces:
            known = [i for i, x in enumerate(arrays) if x is array]
            if not known:
                arrays.append(array)
            placed.append((known[0] if known else len(arrays) - 1, start, count))
        described.append((first, width, column, tuple(placed)))
    height = sum(count for _, _, count in groups[0][3])
    vmem = pl.BlockSpec(memory_space=pltpu.VMEM)
    smem = pl.BlockSpec(memory_space=pltpu.SMEM)
    hbm = pl.BlockSpec(memory_space=pl.ANY)

    args, specs, outs, out_specs, aliases, scratch = [], [], [], [], {}, []

    def add(arg, spec):
        args.append(arg)
        specs.append(spec)

    def add_vmem(arg):
        add(pltpu.with_memory_space_constraint(arg, pltpu.VMEM), vmem)

    for scalar in where:
        add(scalar, smem)
    if do_w:
        add_vmem(at)
    if attn:
        add_vmem(weight)
    for array in arrays:
        add_vmem(array)
    if do_w:
        if w is not None:
            aliases[len(args)] = len(outs)
            add_vmem(w)
        outs.append(pltpu.VMEM((capacity, features), jnp.float32))
        out_specs.append(vmem)
    if attn == "last":
        add_vmem(before)
    if squares == "added":
        add_vmem(added)
    if attn == "first":
        outs.append(pltpu.VMEM((height, capacity), jnp.float32))
        out_specs.append(vmem)
    elif attn:
        if out is not None:
            aliases[len(args)] = len(outs)
            add(out, hbm)
        outs.append(jax.ShapeDtypeStruct((slots, capacity), jnp.bfloat16))
        out_specs.append(hbm)
        scratch = [
            pltpu.VMEM((height, capacity), jnp.float32),
            pltpu.VMEM((height, capacity), jnp.bfloat16),
            pltpu.SemaphoreType.DMA((height // rows,)),
        ]
    outs.append(pltpu.VMEM((8, 128), jnp.float32))
    out_specs.append(vmem)
    spec = (
        tuple(described), len(arrays), do_w, w_from, attn, w is None, out is None,
        squares, rows, begin,
    )
    return pl.pallas_call(
        functools.partial(phase_kernel, spec),
        in_specs=specs,
        out_specs=out_specs,
        out_shape=outs,
        scratch_shapes=scratch,
        input_output_aliases=aliases,
        compiler_params=pltpu.CompilerParams(vmem_limit_bytes=12 * MIB),
        cost_estimate=pl.CostEstimate(
            flops=1,
            bytes_accessed=1,
            transcendentals=0,
        ),
        name="phase_" + "w" * do_w + "_" + str(attn),
    )(*args)


def scale_kernel(parts, w_ref, squares_ref, out_ref, block_ref, sems):
    capacity, features = w_ref.shape
    square_sum = jnp.sum(
        jnp.sum(squares_ref[...], axis=0, keepdims=True), axis=1, keepdims=True
    )
    factor = jnp.minimum(
        1.0, 1.0 / jnp.sqrt(square_sum / (HEADS * HEAD_DIM * features) + 1e-06)
    )
    copies = []
    height = capacity // parts
    for i in range(parts):
        part = pl.ds(i * height, height)
        block_ref[part, :] = (w_ref[part, :] * factor).astype(jnp.bfloat16)
        copies.append(pltpu.make_async_copy(block_ref.at[part], out_ref.at[part], sems.at[i]))
        copies[-1].start()
    for copy in copies:
        copy.wait()


def scaled(w, squares):
    capacity, features = w.shape
    vmem = pl.BlockSpec(memory_space=pltpu.VMEM)
    parts = capacity // 48
    return pl.pallas_call(
        functools.partial(scale_kernel, parts),
        in_specs=[vmem, vmem],
        out_specs=pl.BlockSpec(memory_space=pl.ANY),
        out_shape=jax.ShapeDtypeStruct((capacity, features), jnp.bfloat16),
        scratch_shapes=[
            pltpu.VMEM((capacity, features), jnp.bfloat16),
            pltpu.SemaphoreType.DMA((parts,)),
        ],
        compiler_params=pltpu.CompilerParams(vmem_limit_bytes=10 * MIB),
        cost_estimate=pl.CostEstimate(
            flops=capacity * features,
            bytes_accessed=2 * capacity * features,
            transcendentals=0,
        ),
        name="scale",
    )(pltpu.with_memory_space_constraint(w, pltpu.VMEM), squares)


def after(done, *arrays):
    vmem = pl.BlockSpec(memory_space=pltpu.VMEM)
    return pl.pallas_call(
        lambda *refs: None,
        in_specs=[vmem] * (len(arrays) + 1),
        out_specs=[vmem] * len(arrays),
        out_shape=[pltpu.VMEM(x.shape, x.dtype) for x in arrays],
        input_output_aliases={i: i for i in range(len(arrays))},
        compiler_params=pltpu.CompilerParams(vmem_limit_bytes=MIB),
        name="after",
    )(*[pltpu.with_memory_space_constraint(x, pltpu.VMEM) for x in (*arrays, done)])


def split_kernel(x_ref, left_ref, right_ref, sems):
    half = left_ref.shape[1]
    copies = [
        pltpu.make_async_copy(x_ref.at[:, pl.ds(0, half)], left_ref, sems.at[0]),
        pltpu.make_async_copy(x_ref.at[:, pl.ds(half, half)], right_ref, sems.at[1]),
    ]
    for copy in copies:
        copy.start()
    for copy in copies:
        copy.wait()


def split(x):
    vmem = pl.BlockSpec(memory_space=pltpu.VMEM)
    rows, features = x.shape
    return pl.pallas_call(
        split_kernel,
        in_specs=[vmem],
        out_specs=[vmem] * 2,
        out_shape=[pltpu.VMEM((rows, features // 2), x.dtype)] * 2,
        scratch_shapes=[pltpu.SemaphoreType.DMA((2,))],
        compiler_params=pltpu.CompilerParams(vmem_limit_bytes=MIB),
        name="split",
    )(pltpu.with_memory_space_constraint(x, pltpu.VMEM))


def rounds(devices):
    bits = [1 << i for i in range(devices.bit_length() - 1)]
    masks = []
    while bits:
        pair, bits = bits[:2], bits[2:]
        masks.append(pair + [sum(pair)] if len(pair) == 2 else pair)
    return masks


def exchange(x, devices, masks):
    total = x
    for mask in masks:
        total = total + lax.ppermute(x, "dp", [(d, d ^ mask) for d in range(devices)])
    return total


def on_device(ring, attn_out, out_grad, o_weight, head_counts, seq_counts):
    rows, features = out_grad.shape
    slots = attn_out.shape[0]
    devices, last = ring.devices, ring.length // 2
    steps = 2 * last
    spans = [(0, 2)]
    for k in range(1, last):
        joint = k < last - 1
        spans += [(4 * k - 2, 4), None] if joint else [(4 * k - 2, 2), (4 * k, 2)]
    spans += [(2 * steps - 2, 1), (2 * steps - 1, 1)]
    me = lax.axis_index("dp").astype(jnp.int32).reshape(1)
    where = (jnp.asarray(ring.owners()), me, head_counts)
    shapes = (slots, o_weight.shape[0], features, rows)
    weight, half = o_weight, features // 2

    def send(x, pairs):
        return lax.ppermute(x, "dp", pairs)

    def swapped(halves):
        return [send(x, ring.swap()) for x in halves]

    def grouped(*pairs):
        return [
            (c * half, half, 0, [(x[c], 0, rows) for x in pairs])
            for c in range(min(len(x) for x in pairs))
        ]

    x = send(out_grad, ring.along())
    own, near, count, ats = prepared(
        where, seq_counts, out_grad, attn_out, [x for x in spans if x]
    )
    ats = [ats.pop(0) if x else None for x in spans]
    y = send(own, ring.crossing())
    counts = send(count, ring.along()), send(count, ring.crossing())
    w, out, done = phase(
        where, shapes, 0, grouped(near, swapped(near)), at=ats[0], weight=weight, attn="whole"
    )

    for k in range(1, last):
        x = arrived(done, counts[0], x) if k == 1 else after(done, x)[0]
        x, near_x = send(x, ring.along()), split(x)
        far_x = swapped(near_x)
        i = 2 * k - 1
        if k == last - 1:
            w, out, done = phase(
                where, shapes, 2 * i, grouped(near_x, far_x), at=ats[i], w=w,
                weight=weight, attn="whole", out=out,
            )
        y = arrived(done, counts[1], y) if k == 1 else after(done, y)[0]
        y, near_y = send(y, ring.along()) if k < last - 1 else None, split(y)
        far_y = swapped(near_y)
        groups = grouped(near_x, far_x, near_y, far_y)
        if k == last - 1:
            w, out, done = phase(
                where, shapes, 2 * (i + 1), grouped(near_y, far_y), at=ats[i + 1], w=w,
                weight=weight, attn="whole", out=out,
            )
        else:
            w, out, done = phase(
                where, shapes, 2 * i, groups, at=ats[i], w=w,
                weight=weight, attn="whole", out=out,
            )

    (x,) = after(done, x)
    near = split(x)
    far = swapped(near)
    begin = 2 * steps - 2
    w, done = phase(where, shapes, begin, grouped(near), at=ats[-2], w=w)
    w, squares = phase(where, shapes, begin, grouped(far), at=ats[-1], w=w, squares="new")

    pieces = [group[3] for group in grouped(near, far)]
    parts = [
        [(0, half, 0, pieces[0]), (half, half // 2, 0, pieces[1])],
        [(half + half // 2, half // 2, half // 2, pieces[1])],
    ]
    for late, masks in enumerate(rounds(devices)):
        squares = exchange(squares, devices, masks)
        if late == 0:
            before, done = phase(
                where, shapes, begin, parts[0], weight=weight, attn="first"
            )
            (squares,) = after(done, squares)
        elif late == 1:
            out, done = phase(
                where, shapes, begin, parts[1], weight=weight, attn="last",
                before=before, out=out,
            )
    return out, scaled(w, squares)


def solution(mesh):
    placed = (
        P("group", "dp"),
        P(("group", "dp"), None),
        P("dp", None),
        P("dp"),
        P(("group", "dp")),
    )
    ring = Ring(mesh.shape["dp"], 2 if mesh.shape["group"] == 2 else 1)
    return jax.shard_map(
        functools.partial(on_device, ring),
        mesh=mesh,
        in_specs=placed,
        out_specs=(P("group", "dp"), P(("group", "dp"), None)),
        check_vma=False,
    )
```

```python
import functools

import jax
import jax.numpy as jnp
import numpy as np
from jax import lax
from jax.experimental import pallas as pl
from jax.experimental.pallas import tpu as pltpu
from jax.sharding import PartitionSpec as P

HEADS = 64
HEAD_DIM = 128
SEQ = 16
TILE = 1024
MIB = 1024 * 1024


class Ring:
    def __init__(self, devices, columns):
        self.devices = devices
        self.length = devices // 2
        rows = self.length // columns
        if columns == 1:
            self.chips = list(range(rows))
        else:
            self.chips = [2 * z for z in range(rows)]
            self.chips += [2 * z + 1 for z in reversed(range(rows))]
        self.position = {chip: p for p, chip in enumerate(self.chips)}

    def device(self, position, core):
        return 2 * self.chips[position % self.length] + core

    def along(self):
        return [
            (self.device(p, core), self.device(p + 1 - 2 * core, core))
            for p in range(self.length)
            for core in range(2)
        ]

    def crossing(self):
        return [
            (self.device(p, core), self.device(p - 1 + 2 * core, 1 - core))
            for p in range(self.length)
            for core in range(2)
        ]

    def swap(self):
        return [(d, d ^ 1) for d in range(self.devices)]

    def owners(self):
        table, last = [], self.length // 2
        for d in range(self.devices):
            p, core = self.position[d // 2], d % 2
            row = [d, d ^ 1]
            for k in range(1, last + 1):
                step = k if core else -k
                row += [self.device(p + step, core), self.device(p - step, 1 - core)]
                if k < last:
                    row += [self.device(p + step, 1 - core), self.device(p - step, core)]
            table.append(row)
        return np.array(table, np.int32)


def zero_dead(count, ref):
    for s in range(ref.shape[0] // SEQ):

        @pl.when(s >= count)
        def _():
            dead = ref.at[s * SEQ : (s + 1) * SEQ]
            dead[...] = jnp.zeros_like(dead)


def prep_kernel(
    spans, rows, table_ref, me_ref, heads_ref, seqs_ref, grad_ref, a_ref, *refs
):
    copy_ref, left_ref, right_ref, count_ref, *at_refs, block_ref, sems, own_sems = refs
    half = left_ref.shape[1]
    owns = [
        pltpu.make_async_copy(grad_ref, copy_ref, own_sems.at[0]),
        pltpu.make_async_copy(grad_ref.at[:, pl.ds(0, half)], left_ref, own_sems.at[1]),
        pltpu.make_async_copy(grad_ref.at[:, pl.ds(half, half)], right_ref, own_sems.at[2]),
    ]
    for copy in owns:
        copy.start()
    count_ref[...] = jnp.full(count_ref.shape, seqs_ref[0], jnp.int32)
    width = heads_ref[0] * HEAD_DIM
    copies = []
    for i in range(block_ref.shape[0] // rows):
        owner = table_ref[me_ref[0], i]
        copies.append(
            pltpu.make_async_copy(
                a_ref.at[pl.ds(pl.multiple_of(owner * rows, rows), rows)],
                block_ref.at[pl.ds(i * rows, rows)],
                sems.at[i],
            )
        )
        copies[-1].start()
    waited = 0
    for at_ref, (begin, count) in zip(at_refs, spans):
        for copy in copies[waited : begin + count]:
            copy.wait()
        waited = max(waited, begin + count)
        block = block_ref[begin * rows : (begin + count) * rows, :]
        column = lax.broadcasted_iota(jnp.int32, block.shape, 1)
        at_ref[...] = jnp.where(column < width, block, jnp.zeros_like(block)).T
    for copy in owns:
        copy.wait()
    zero_dead(seqs_ref[0], left_ref)
    zero_dead(seqs_ref[0], right_ref)


def prepared(where, seq_counts, out_grad, attn_out, spans):
    slots, capacity = attn_out.shape
    rows, features = out_grad.shape
    vmem = pl.BlockSpec(memory_space=pltpu.VMEM)
    smem = pl.BlockSpec(memory_space=pltpu.SMEM)
    outs = [(rows, features), (rows, features // 2), (rows, features // 2)]
    outs += [(capacity, count * rows) for _, count in spans]
    shapes = [pltpu.VMEM(shape, jnp.bfloat16) for shape in outs]
    shapes.insert(3, pltpu.VMEM((8, 128), jnp.int32))
    copy, left, right, count, *ats = pl.pallas_call(
        functools.partial(prep_kernel, spans, rows),
        in_specs=[smem] * 4 + [pl.BlockSpec(memory_space=pl.ANY)] * 2,
        out_specs=[vmem] * len(shapes),
        out_shape=shapes,
        scratch_shapes=[
            pltpu.VMEM((slots, capacity), jnp.bfloat16),
            pltpu.SemaphoreType.DMA((slots // rows,)),
            pltpu.SemaphoreType.DMA((3,)),
        ],
        compiler_params=pltpu.CompilerParams(vmem_limit_bytes=12 * MIB),
        cost_estimate=pl.CostEstimate(flops=1, bytes_accessed=1, transcendentals=0),
        name="prep",
    )(
        *where,
        seq_counts,
        pltpu.with_memory_space_constraint(out_grad, pltpu.HBM),
        pltpu.with_memory_space_constraint(attn_out, pltpu.HBM),
    )
    return copy, (left, right), count, ats


def arrive_kernel(count_ref, x_ref, done_ref, out_ref):
    zero_dead(count_ref[0, 0], out_ref)


def arrived(done, count, x):
    vmem = pl.BlockSpec(memory_space=pltpu.VMEM)
    return pl.pallas_call(
        arrive_kernel,
        in_specs=[pl.BlockSpec(memory_space=pltpu.SMEM), vmem, vmem],
        out_specs=vmem,
        out_shape=pltpu.VMEM(x.shape, x.dtype),
        input_output_aliases={1: 0},
        compiler_params=pltpu.CompilerParams(vmem_limit_bytes=MIB),
        name="arrived",
    )(count, *[pltpu.with_memory_space_constraint(x, pltpu.VMEM) for x in (x, done)])


def phase_kernel(spec, *refs):
    groups, arrays, do_w, w_from, attn, fresh_w, fresh_out, squares, rows, begin = spec
    refs = list(refs)
    table_ref, me_ref, heads_ref = refs.pop(0), refs.pop(0), refs.pop(0)
    at_ref = refs.pop(0) if do_w else None
    weight_ref = refs.pop(0) if attn else None
    g_refs = [refs.pop(0) for _ in range(arrays)]
    if do_w and not fresh_w:
        refs.pop(0)
    before_ref = refs.pop(0) if attn == "last" else None
    added_ref = refs.pop(0) if squares == "added" else None
    if attn in ("whole", "last") and not fresh_out:
        refs.pop(0)
    w_ref = refs.pop(0) if do_w else None
    total_ref = refs.pop(0) if attn == "first" else None
    out_ref = refs.pop(0) if attn in ("whole", "last") else None
    squares_ref = refs.pop(0)
    if attn in ("whole", "last"):
        total_ref, block_ref, sems = refs
    if attn == "last":
        total_ref[...] = before_ref[...]
    elif attn:
        total_ref[...] = jnp.zeros_like(total_ref)
    if squares == "added":
        squares_ref[...] = added_ref[...]
    else:
        squares_ref[...] = jnp.zeros_like(squares_ref)

    def body(first, column, pieces, j, carry):
        here = pl.ds(pl.multiple_of(column + j * TILE, TILE), TILE)
        there = pl.ds(pl.multiple_of(first + j * TILE, TILE), TILE)
        g = [g_refs[i][start : start + count, here] for i, start, count in pieces]
        if do_w:
            fresh = jnp.concatenate(g[w_from:], axis=0) if len(g) > w_from + 1 else g[-1]
            w = jnp.dot(at_ref[...], fresh, preferred_element_type=jnp.float32)
            if not fresh_w:
                w = w + w_ref[:, there]
            w_ref[:, there] = w
        if squares:
            folded = jnp.sum((w * w).reshape(w.shape[0] // 8, 8, TILE), axis=0)
            total = squares_ref[...]
            for lane in range(0, TILE, 128):
                total = total + folded[:, lane : lane + 128]
            squares_ref[...] = total
        if attn:
            total_ref[...] += lax.dot_general(
                jnp.concatenate(g, axis=0),
                weight_ref[:, there],
                (((1,), (1,)), ((), ())),
                preferred_element_type=jnp.float32,
            )
        return carry

    for first, width, column, pieces in groups:
        step = functools.partial(body, first, column, pieces)
        lax.fori_loop(0, width // TILE, step, 0, unroll=True)
    if attn in ("whole", "last"):
        total = total_ref[...]
        column = lax.broadcasted_iota(jnp.int32, total.shape, 1)
        live = column < heads_ref[0] * HEAD_DIM
        block_ref[...] = jnp.where(live, total, 0.0).astype(jnp.bfloat16)
        copies = []
        for i in range(total.shape[0] // rows):
            owner = table_ref[me_ref[0], begin + i]
            copies.append(
                pltpu.make_async_copy(
                    block_ref.at[pl.ds(i * rows, rows)],
                    out_ref.at[pl.ds(pl.multiple_of(owner * rows, rows), rows)],
                    sems.at[i],
                )
            )
            copies[-1].start()
        for copy in copies:
            copy.wait()


def phase(
    where, shapes, begin, groups, at=None, w=None,
    weight=None, attn=None, before=None, out=None, squares=None, added=None,
    w_from=0,
):
    slots, capacity, features, rows = shapes
    do_w = at is not None
    arrays, described = [], []
    for first, width, column, pieces in groups:
        placed = []
        for array, start, count in pieces:
            known = [i for i, x in enumerate(arrays) if x is array]
            if not known:
                arrays.append(array)
            placed.append((known[0] if known else len(arrays) - 1, start, count))
        described.append((first, width, column, tuple(placed)))
    height = sum(count for _, _, count in groups[0][3])
    vmem = pl.BlockSpec(memory_space=pltpu.VMEM)
    smem = pl.BlockSpec(memory_space=pltpu.SMEM)
    hbm = pl.BlockSpec(memory_space=pl.ANY)

    args, specs, outs, out_specs, aliases, scratch = [], [], [], [], {}, []

    def add(arg, spec):
        args.append(arg)
        specs.append(spec)

    def add_vmem(arg):
        add(pltpu.with_memory_space_constraint(arg, pltpu.VMEM), vmem)

    for scalar in where:
        add(scalar, smem)
    if do_w:
        add_vmem(at)
    if attn:
        add_vmem(weight)
    for array in arrays:
        add_vmem(array)
    if do_w:
        if w is not None:
            aliases[len(args)] = len(outs)
            add_vmem(w)
        outs.append(pltpu.VMEM((capacity, features), jnp.float32))
        out_specs.append(vmem)
    if attn == "last":
        add_vmem(before)
    if squares == "added":
        add_vmem(added)
    if attn == "first":
        outs.append(pltpu.VMEM((height, capacity), jnp.float32))
        out_specs.append(vmem)
    elif attn:
        if out is not None:
            aliases[len(args)] = len(outs)
            add(out, hbm)
        outs.append(jax.ShapeDtypeStruct((slots, capacity), jnp.bfloat16))
        out_specs.append(hbm)
        scratch = [
            pltpu.VMEM((height, capacity), jnp.float32),
            pltpu.VMEM((height, capacity), jnp.bfloat16),
            pltpu.SemaphoreType.DMA((height // rows,)),
        ]
    outs.append(pltpu.VMEM((8, 128), jnp.float32))
    out_specs.append(vmem)
    spec = (
        tuple(described), len(arrays), do_w, w_from, attn, w is None, out is None,
        squares, rows, begin,
    )
    return pl.pallas_call(
        functools.partial(phase_kernel, spec),
        in_specs=specs,
        out_specs=out_specs,
        out_shape=outs,
        scratch_shapes=scratch,
        input_output_aliases=aliases,
        compiler_params=pltpu.CompilerParams(vmem_limit_bytes=12 * MIB),
        cost_estimate=pl.CostEstimate(
            flops=1,
            bytes_accessed=1,
            transcendentals=0,
        ),
        name="phase_" + "w" * do_w + "_" + str(attn),
    )(*args)


def scale_kernel(parts, w_ref, squares_ref, out_ref, block_ref, sems):
    capacity, features = w_ref.shape
    square_sum = jnp.sum(
        jnp.sum(squares_ref[...], axis=0, keepdims=True), axis=1, keepdims=True
    )
    factor = jnp.minimum(
        1.0, 1.0 / jnp.sqrt(square_sum / (HEADS * HEAD_DIM * features) + 1e-06)
    )
    copies = []
    height = capacity // parts
    for i in range(parts):
        part = pl.ds(i * height, height)
        block_ref[part, :] = (w_ref[part, :] * factor).astype(jnp.bfloat16)
        copies.append(pltpu.make_async_copy(block_ref.at[part], out_ref.at[part], sems.at[i]))
        copies[-1].start()
    for copy in copies:
        copy.wait()


def scaled(w, squares):
    capacity, features = w.shape
    vmem = pl.BlockSpec(memory_space=pltpu.VMEM)
    parts = capacity // 48
    return pl.pallas_call(
        functools.partial(scale_kernel, parts),
        in_specs=[vmem, vmem],
        out_specs=pl.BlockSpec(memory_space=pl.ANY),
        out_shape=jax.ShapeDtypeStruct((capacity, features), jnp.bfloat16),
        scratch_shapes=[
            pltpu.VMEM((capacity, features), jnp.bfloat16),
            pltpu.SemaphoreType.DMA((parts,)),
        ],
        compiler_params=pltpu.CompilerParams(vmem_limit_bytes=10 * MIB),
        cost_estimate=pl.CostEstimate(
            flops=capacity * features,
            bytes_accessed=2 * capacity * features,
            transcendentals=0,
        ),
        name="scale",
    )(pltpu.with_memory_space_constraint(w, pltpu.VMEM), squares)


def after(done, *arrays):
    vmem = pl.BlockSpec(memory_space=pltpu.VMEM)
    return pl.pallas_call(
        lambda *refs: None,
        in_specs=[vmem] * (len(arrays) + 1),
        out_specs=[vmem] * len(arrays),
        out_shape=[pltpu.VMEM(x.shape, x.dtype) for x in arrays],
        input_output_aliases={i: i for i in range(len(arrays))},
        compiler_params=pltpu.CompilerParams(vmem_limit_bytes=MIB),
        name="after",
    )(*[pltpu.with_memory_space_constraint(x, pltpu.VMEM) for x in (*arrays, done)])


def split_kernel(x_ref, left_ref, right_ref, sems):
    half = left_ref.shape[1]
    copies = [
        pltpu.make_async_copy(x_ref.at[:, pl.ds(0, half)], left_ref, sems.at[0]),
        pltpu.make_async_copy(x_ref.at[:, pl.ds(half, half)], right_ref, sems.at[1]),
    ]
    for copy in copies:
        copy.start()
    for copy in copies:
        copy.wait()


def split(x):
    vmem = pl.BlockSpec(memory_space=pltpu.VMEM)
    rows, features = x.shape
    return pl.pallas_call(
        split_kernel,
        in_specs=[vmem],
        out_specs=[vmem] * 2,
        out_shape=[pltpu.VMEM((rows, features // 2), x.dtype)] * 2,
        scratch_shapes=[pltpu.SemaphoreType.DMA((2,))],
        compiler_params=pltpu.CompilerParams(vmem_limit_bytes=MIB),
        name="split",
    )(pltpu.with_memory_space_constraint(x, pltpu.VMEM))


def rounds(devices):
    bits = [1 << i for i in range(devices.bit_length() - 1)]
    if len(bits) >= 4:
        bits = bits[1:3] + [bits[0]] + bits[3:]
    masks = []
    while bits:
        pair, bits = bits[:2], bits[2:]
        masks.append(pair + [sum(pair)] if len(pair) == 2 else pair)
    return masks


def exchange(x, devices, masks):
    total = x
    for mask in masks:
        total = total + lax.ppermute(x, "dp", [(d, d ^ mask) for d in range(devices)])
    return total


def on_device(ring, attn_out, out_grad, o_weight, head_counts, seq_counts):
    rows, features = out_grad.shape
    slots = attn_out.shape[0]
    devices, last = ring.devices, ring.length // 2
    steps = 2 * last
    spans = [(0, 2)]
    for k in range(1, last):
        joint = k < last - 1
        spans += [(4 * k - 2, 4), None] if joint else [(4 * k - 2, 2), (4 * k, 2)]
    spans += [(2 * steps - 2, 1), (2 * steps - 1, 1)]
    me = lax.axis_index("dp").astype(jnp.int32).reshape(1)
    where = (jnp.asarray(ring.owners()), me, head_counts)
    shapes = (slots, o_weight.shape[0], features, rows)
    weight, half = o_weight, features // 2

    def send(x, pairs):
        return lax.ppermute(x, "dp", pairs)

    def swapped(halves):
        return [send(x, ring.swap()) for x in halves]

    def grouped(*pairs):
        return [
            (c * half, half, 0, [(x[c], 0, rows) for x in pairs])
            for c in range(min(len(x) for x in pairs))
        ]

    x = send(out_grad, ring.along())
    own, near, count, ats = prepared(
        where, seq_counts, out_grad, attn_out, [x for x in spans if x]
    )
    ats = [ats.pop(0) if x else None for x in spans]
    y = send(own, ring.crossing())
    counts = send(count, ring.along()), send(count, ring.crossing())
    w, out, done = phase(
        where, shapes, 0, grouped(near, swapped(near)), at=ats[0], weight=weight, attn="whole"
    )

    for k in range(1, last):
        x = arrived(done, counts[0], x) if k == 1 else after(done, x)[0]
        x, near_x = send(x, ring.along()), split(x)
        far_x = swapped(near_x)
        i = 2 * k - 1
        if k == last - 1:
            w, out, done = phase(
                where, shapes, 2 * i, grouped(near_x, far_x), at=ats[i], w=w,
                weight=weight, attn="whole", out=out,
            )
        y = arrived(done, counts[1], y) if k == 1 else after(done, y)[0]
        y, near_y = send(y, ring.along()) if k < last - 1 else None, split(y)
        far_y = swapped(near_y)
        groups = grouped(near_x, far_x, near_y, far_y)
        if k == last - 1:
            w, out, done = phase(
                where, shapes, 2 * (i + 1), grouped(near_y, far_y), at=ats[i + 1], w=w,
                weight=weight, attn="whole", out=out,
            )
        else:
            w, out, done = phase(
                where, shapes, 2 * i, groups, at=ats[i], w=w,
                weight=weight, attn="whole", out=out,
            )

    (x,) = after(done, x)
    near = split(x)
    far = swapped(near)
    begin = 2 * steps - 2
    w, done = phase(where, shapes, begin, grouped(near), at=ats[-2], w=w)
    w, squares = phase(where, shapes, begin, grouped(far), at=ats[-1], w=w, squares="new")

    pieces = [group[3] for group in grouped(near, far)]
    parts = [
        [(0, half, 0, pieces[0]), (half, half // 2, 0, pieces[1])],
        [(half + half // 2, half // 2, half // 2, pieces[1])],
    ]
    for late, masks in enumerate(rounds(devices)):
        squares = exchange(squares, devices, masks)
        if late == 0:
            before, done = phase(
                where, shapes, begin, parts[0], weight=weight, attn="first"
            )
            (squares,) = after(done, squares)
        elif late == 1:
            out, done = phase(
                where, shapes, begin, parts[1], weight=weight, attn="last",
                before=before, out=out,
            )
    return out, scaled(w, squares)


def solution(mesh):
    placed = (
        P("group", "dp"),
        P(("group", "dp"), None),
        P("dp", None),
        P("dp"),
        P(("group", "dp")),
    )
    ring = Ring(mesh.shape["dp"], 2 if mesh.shape["group"] == 2 else 1)
    return jax.shard_map(
        functools.partial(on_device, ring),
        mesh=mesh,
        in_specs=placed,
        out_specs=(P("group", "dp"), P(("group", "dp"), None)),
        check_vma=False,
    )
```

```python
import functools

import jax
import jax.numpy as jnp
import numpy as np
from jax import lax
from jax.experimental import pallas as pl
from jax.experimental.pallas import tpu as pltpu
from jax.sharding import PartitionSpec as P

HEADS = 64
HEAD_DIM = 128
SEQ = 16
TILE = 1024
MIB = 1024 * 1024


class Ring:
    def __init__(self, devices, columns):
        self.devices = devices
        self.length = devices // 2
        rows = self.length // columns
        if columns == 1:
            self.chips = list(range(rows))
        else:
            self.chips = [2 * z for z in range(rows)]
            self.chips += [2 * z + 1 for z in reversed(range(rows))]
        self.position = {chip: p for p, chip in enumerate(self.chips)}

    def device(self, position, core):
        return 2 * self.chips[position % self.length] + core

    def along(self):
        return [
            (self.device(p, core), self.device(p + 1 - 2 * core, core))
            for p in range(self.length)
            for core in range(2)
        ]

    def crossing(self):
        return [
            (self.device(p, core), self.device(p - 1 + 2 * core, 1 - core))
            for p in range(self.length)
            for core in range(2)
        ]

    def swap(self):
        return [(d, d ^ 1) for d in range(self.devices)]

    def owners(self):
        table, last = [], self.length // 2
        for d in range(self.devices):
            p, core = self.position[d // 2], d % 2
            row = [d, d ^ 1]
            for k in range(1, last + 1):
                step = k if core else -k
                row += [self.device(p + step, core), self.device(p - step, 1 - core)]
                if k < last:
                    row += [self.device(p + step, 1 - core), self.device(p - step, core)]
            table.append(row)
        return np.array(table, np.int32)


def zero_dead(count, ref):
    for s in range(ref.shape[0] // SEQ):

        @pl.when(s >= count)
        def _():
            dead = ref.at[s * SEQ : (s + 1) * SEQ]
            dead[...] = jnp.zeros_like(dead)


def stage_kernel(me_ref, seqs_ref, grad_ref, copy_ref, left_ref, right_ref, count_ref, sems):
    half = left_ref.shape[1]
    copies = [
        pltpu.make_async_copy(grad_ref, copy_ref, sems.at[0]),
        pltpu.make_async_copy(grad_ref.at[:, pl.ds(0, half)], left_ref, sems.at[1]),
        pltpu.make_async_copy(grad_ref.at[:, pl.ds(half, half)], right_ref, sems.at[2]),
    ]
    for copy in copies:
        copy.start()
    count_ref[...] = jnp.full(count_ref.shape, seqs_ref[0], jnp.int32)
    for copy in copies:
        copy.wait()
    zero_dead(seqs_ref[0], left_ref)
    zero_dead(seqs_ref[0], right_ref)


def staged(me, seq_counts, out_grad):
    rows, features = out_grad.shape
    vmem = pl.BlockSpec(memory_space=pltpu.VMEM)
    smem = pl.BlockSpec(memory_space=pltpu.SMEM)
    outs = [(rows, features), (rows, features // 2), (rows, features // 2)]
    shapes = [pltpu.VMEM(shape, jnp.bfloat16) for shape in outs]
    copy, left, right, count = pl.pallas_call(
        stage_kernel,
        in_specs=[smem, smem, pl.BlockSpec(memory_space=pl.ANY)],
        out_specs=[vmem] * 4,
        out_shape=shapes + [pltpu.VMEM((8, 128), jnp.int32)],
        scratch_shapes=[pltpu.SemaphoreType.DMA((3,))],
        compiler_params=pltpu.CompilerParams(vmem_limit_bytes=2 * MIB),
        cost_estimate=pl.CostEstimate(flops=1, bytes_accessed=1, transcendentals=0),
        name="stage",
    )(me, seq_counts, pltpu.with_memory_space_constraint(out_grad, pltpu.HBM))
    return copy, (left, right), count


def prep_kernel(spans, rows, table_ref, me_ref, heads_ref, _, a_ref, *refs):
    *at_refs, block_ref, sems = refs
    width = heads_ref[0] * HEAD_DIM
    copies = []
    for i in range(block_ref.shape[0] // rows):
        owner = table_ref[me_ref[0], i]
        copies.append(
            pltpu.make_async_copy(
                a_ref.at[pl.ds(pl.multiple_of(owner * rows, rows), rows)],
                block_ref.at[pl.ds(i * rows, rows)],
                sems.at[i],
            )
        )
        copies[-1].start()
    waited = 0
    for at_ref, (begin, count) in zip(at_refs, spans):
        for copy in copies[waited : begin + count]:
            copy.wait()
        waited = max(waited, begin + count)
        block = block_ref[begin * rows : (begin + count) * rows, :]
        column = lax.broadcasted_iota(jnp.int32, block.shape, 1)
        at_ref[...] = jnp.where(column < width, block, jnp.zeros_like(block)).T


def prepared(where, count, attn_out, spans, rows):
    slots, capacity = attn_out.shape
    vmem = pl.BlockSpec(memory_space=pltpu.VMEM)
    smem = pl.BlockSpec(memory_space=pltpu.SMEM)
    return pl.pallas_call(
        functools.partial(prep_kernel, spans, rows),
        in_specs=[smem] * 3 + [vmem, pl.BlockSpec(memory_space=pl.ANY)],
        out_specs=[vmem] * len(spans),
        out_shape=[pltpu.VMEM((capacity, n * rows), jnp.bfloat16) for _, n in spans],
        scratch_shapes=[
            pltpu.VMEM((slots, capacity), jnp.bfloat16),
            pltpu.SemaphoreType.DMA((slots // rows,)),
        ],
        compiler_params=pltpu.CompilerParams(vmem_limit_bytes=12 * MIB),
        cost_estimate=pl.CostEstimate(flops=1, bytes_accessed=1, transcendentals=0),
        name="prep",
    )(
        *where,
        pltpu.with_memory_space_constraint(count, pltpu.VMEM),
        pltpu.with_memory_space_constraint(attn_out, pltpu.HBM),
    )


def arrive_kernel(count_ref, x_ref, done_ref, out_ref):
    zero_dead(count_ref[0, 0], out_ref)


def arrived(done, count, x):
    vmem = pl.BlockSpec(memory_space=pltpu.VMEM)
    return pl.pallas_call(
        arrive_kernel,
        in_specs=[pl.BlockSpec(memory_space=pltpu.SMEM), vmem, vmem],
        out_specs=vmem,
        out_shape=pltpu.VMEM(x.shape, x.dtype),
        input_output_aliases={1: 0},
        compiler_params=pltpu.CompilerParams(vmem_limit_bytes=MIB),
        name="arrived",
    )(count, *[pltpu.with_memory_space_constraint(x, pltpu.VMEM) for x in (x, done)])


def phase_kernel(spec, *refs):
    groups, arrays, do_w, w_from, attn, fresh_w, fresh_out, squares, rows, begin = spec
    refs = list(refs)
    table_ref, me_ref, heads_ref = refs.pop(0), refs.pop(0), refs.pop(0)
    at_ref = refs.pop(0) if do_w else None
    weight_ref = refs.pop(0) if attn else None
    g_refs = [refs.pop(0) for _ in range(arrays)]
    if do_w and not fresh_w:
        refs.pop(0)
    before_ref = refs.pop(0) if attn == "last" else None
    added_ref = refs.pop(0) if squares == "added" else None
    if attn in ("whole", "last") and not fresh_out:
        refs.pop(0)
    w_ref = refs.pop(0) if do_w else None
    total_ref = refs.pop(0) if attn == "first" else None
    out_ref = refs.pop(0) if attn in ("whole", "last") else None
    squares_ref = refs.pop(0)
    if attn in ("whole", "last"):
        total_ref, block_ref, sems = refs
    if attn == "last":
        total_ref[...] = before_ref[...]
    elif attn:
        total_ref[...] = jnp.zeros_like(total_ref)
    if squares == "added":
        squares_ref[...] = added_ref[...]
    else:
        squares_ref[...] = jnp.zeros_like(squares_ref)

    def body(first, column, pieces, j, carry):
        here = pl.ds(pl.multiple_of(column + j * TILE, TILE), TILE)
        there = pl.ds(pl.multiple_of(first + j * TILE, TILE), TILE)
        g = [g_refs[i][start : start + count, here] for i, start, count in pieces]
        if do_w:
            fresh = jnp.concatenate(g[w_from:], axis=0) if len(g) > w_from + 1 else g[-1]
            w = jnp.dot(at_ref[...], fresh, preferred_element_type=jnp.float32)
            if not fresh_w:
                w = w + w_ref[:, there]
            w_ref[:, there] = w
        if squares:
            folded = jnp.sum((w * w).reshape(w.shape[0] // 8, 8, TILE), axis=0)
            total = squares_ref[...]
            for lane in range(0, TILE, 128):
                total = total + folded[:, lane : lane + 128]
            squares_ref[...] = total
        if attn:
            total_ref[...] += lax.dot_general(
                jnp.concatenate(g, axis=0),
                weight_ref[:, there],
                (((1,), (1,)), ((), ())),
                preferred_element_type=jnp.float32,
            )
        return carry

    for first, width, column, pieces in groups:
        step = functools.partial(body, first, column, pieces)
        lax.fori_loop(0, width // TILE, step, 0)
    if attn in ("whole", "last"):
        total = total_ref[...]
        column = lax.broadcasted_iota(jnp.int32, total.shape, 1)
        live = column < heads_ref[0] * HEAD_DIM
        block_ref[...] = jnp.where(live, total, 0.0).astype(jnp.bfloat16)
        copies = []
        for i in range(total.shape[0] // rows):
            owner = table_ref[me_ref[0], begin + i]
            copies.append(
                pltpu.make_async_copy(
                    block_ref.at[pl.ds(i * rows, rows)],
                    out_ref.at[pl.ds(pl.multiple_of(owner * rows, rows), rows)],
                    sems.at[i],
                )
            )
            copies[-1].start()
        for copy in copies:
            copy.wait()


def phase(
    where, shapes, begin, groups, at=None, w=None,
    weight=None, attn=None, before=None, out=None, squares=None, added=None,
    w_from=0,
):
    slots, capacity, features, rows = shapes
    do_w = at is not None
    arrays, described = [], []
    for first, width, column, pieces in groups:
        placed = []
        for array, start, count in pieces:
            known = [i for i, x in enumerate(arrays) if x is array]
            if not known:
                arrays.append(array)
            placed.append((known[0] if known else len(arrays) - 1, start, count))
        described.append((first, width, column, tuple(placed)))
    height = sum(count for _, _, count in groups[0][3])
    vmem = pl.BlockSpec(memory_space=pltpu.VMEM)
    smem = pl.BlockSpec(memory_space=pltpu.SMEM)
    hbm = pl.BlockSpec(memory_space=pl.ANY)

    args, specs, outs, out_specs, aliases, scratch = [], [], [], [], {}, []

    def add(arg, spec):
        args.append(arg)
        specs.append(spec)

    def add_vmem(arg):
        add(pltpu.with_memory_space_constraint(arg, pltpu.VMEM), vmem)

    for scalar in where:
        add(scalar, smem)
    if do_w:
        add_vmem(at)
    if attn:
        add_vmem(weight)
    for array in arrays:
        add_vmem(array)
    if do_w:
        if w is not None:
            aliases[len(args)] = len(outs)
            add_vmem(w)
        outs.append(pltpu.VMEM((capacity, features), jnp.float32))
        out_specs.append(vmem)
    if attn == "last":
        add_vmem(before)
    if squares == "added":
        add_vmem(added)
    if attn == "first":
        outs.append(pltpu.VMEM((height, capacity), jnp.float32))
        out_specs.append(vmem)
    elif attn:
        if out is not None:
            aliases[len(args)] = len(outs)
            add(out, hbm)
        outs.append(jax.ShapeDtypeStruct((slots, capacity), jnp.bfloat16))
        out_specs.append(hbm)
        scratch = [
            pltpu.VMEM((height, capacity), jnp.float32),
            pltpu.VMEM((height, capacity), jnp.bfloat16),
            pltpu.SemaphoreType.DMA((height // rows,)),
        ]
    outs.append(pltpu.VMEM((8, 128), jnp.float32))
    out_specs.append(vmem)
    spec = (
        tuple(described), len(arrays), do_w, w_from, attn, w is None, out is None,
        squares, rows, begin,
    )
    return pl.pallas_call(
        functools.partial(phase_kernel, spec),
        in_specs=specs,
        out_specs=out_specs,
        out_shape=outs,
        scratch_shapes=scratch,
        input_output_aliases=aliases,
        compiler_params=pltpu.CompilerParams(vmem_limit_bytes=12 * MIB),
        cost_estimate=pl.CostEstimate(
            flops=1,
            bytes_accessed=1,
            transcendentals=0,
        ),
        name="phase_" + "w" * do_w + "_" + str(attn),
    )(*args)


def scale_kernel(parts, w_ref, squares_ref, out_ref, block_ref, sems):
    capacity, features = w_ref.shape
    square_sum = jnp.sum(
        jnp.sum(squares_ref[...], axis=0, keepdims=True), axis=1, keepdims=True
    )
    factor = jnp.minimum(
        1.0, 1.0 / jnp.sqrt(square_sum / (HEADS * HEAD_DIM * features) + 1e-06)
    )
    copies = []
    height = capacity // parts
    for i in range(parts):
        part = pl.ds(i * height, height)
        block_ref[part, :] = (w_ref[part, :] * factor).astype(jnp.bfloat16)
        copies.append(pltpu.make_async_copy(block_ref.at[part], out_ref.at[part], sems.at[i]))
        copies[-1].start()
    for copy in copies:
        copy.wait()


def scaled(w, squares):
    capacity, features = w.shape
    vmem = pl.BlockSpec(memory_space=pltpu.VMEM)
    parts = capacity // 48
    return pl.pallas_call(
        functools.partial(scale_kernel, parts),
        in_specs=[vmem, vmem],
        out_specs=pl.BlockSpec(memory_space=pl.ANY),
        out_shape=jax.ShapeDtypeStruct((capacity, features), jnp.bfloat16),
        scratch_shapes=[
            pltpu.VMEM((capacity, features), jnp.bfloat16),
            pltpu.SemaphoreType.DMA((parts,)),
        ],
        compiler_params=pltpu.CompilerParams(vmem_limit_bytes=10 * MIB),
        cost_estimate=pl.CostEstimate(
            flops=capacity * features,
            bytes_accessed=2 * capacity * features,
            transcendentals=0,
        ),
        name="scale",
    )(pltpu.with_memory_space_constraint(w, pltpu.VMEM), squares)


def after(done, *arrays):
    vmem = pl.BlockSpec(memory_space=pltpu.VMEM)
    return pl.pallas_call(
        lambda *refs: None,
        in_specs=[vmem] * (len(arrays) + 1),
        out_specs=[vmem] * len(arrays),
        out_shape=[pltpu.VMEM(x.shape, x.dtype) for x in arrays],
        input_output_aliases={i: i for i in range(len(arrays))},
        compiler_params=pltpu.CompilerParams(vmem_limit_bytes=MIB),
        name="after",
    )(*[pltpu.with_memory_space_constraint(x, pltpu.VMEM) for x in (*arrays, done)])


def split_kernel(x_ref, left_ref, right_ref, sems):
    half = left_ref.shape[1]
    copies = [
        pltpu.make_async_copy(x_ref.at[:, pl.ds(0, half)], left_ref, sems.at[0]),
        pltpu.make_async_copy(x_ref.at[:, pl.ds(half, half)], right_ref, sems.at[1]),
    ]
    for copy in copies:
        copy.start()
    for copy in copies:
        copy.wait()


def split(x):
    vmem = pl.BlockSpec(memory_space=pltpu.VMEM)
    rows, features = x.shape
    return pl.pallas_call(
        split_kernel,
        in_specs=[vmem],
        out_specs=[vmem] * 2,
        out_shape=[pltpu.VMEM((rows, features // 2), x.dtype)] * 2,
        scratch_shapes=[pltpu.SemaphoreType.DMA((2,))],
        compiler_params=pltpu.CompilerParams(vmem_limit_bytes=MIB),
        name="split",
    )(pltpu.with_memory_space_constraint(x, pltpu.VMEM))


def rounds(devices):
    bits = [1 << i for i in range(devices.bit_length() - 1)]
    if len(bits) >= 4:
        bits = bits[1:3] + [bits[0]] + bits[3:]
    masks = []
    while bits:
        pair, bits = bits[:2], bits[2:]
        masks.append(pair + [sum(pair)] if len(pair) == 2 else pair)
    return masks


def exchange(x, devices, masks):
    total = x
    for mask in masks:
        total = total + lax.ppermute(x, "dp", [(d, d ^ mask) for d in range(devices)])
    return total


def on_device(ring, attn_out, out_grad, o_weight, head_counts, seq_counts):
    rows, features = out_grad.shape
    slots = attn_out.shape[0]
    devices, last = ring.devices, ring.length // 2
    steps = 2 * last
    spans = [(0, 2)]
    for k in range(1, last):
        joint = k < last - 1
        spans += [(4 * k - 2, 4), None] if joint else [(4 * k - 2, 2), (4 * k, 2)]
    spans += [(2 * steps - 2, 1), (2 * steps - 1, 1)]
    me = lax.axis_index("dp").astype(jnp.int32).reshape(1)
    where = (jnp.asarray(ring.owners()), me, head_counts)
    shapes = (slots, o_weight.shape[0], features, rows)
    weight, half = o_weight, features // 2

    def send(x, pairs):
        return lax.ppermute(x, "dp", pairs)

    def swapped(halves):
        return [send(x, ring.swap()) for x in halves]

    def grouped(*pairs):
        return [
            (c * half, half, 0, [(x[c], 0, rows) for x in pairs])
            for c in range(min(len(x) for x in pairs))
        ]

    x = send(out_grad, ring.along())
    own, near, count = staged(me, seq_counts, out_grad)
    ats = list(prepared(where, count, attn_out, [x for x in spans if x], rows))
    ats = [ats.pop(0) if x else None for x in spans]
    y = send(own, ring.crossing())
    counts = send(count, ring.along()), send(count, ring.crossing())
    w, out, done = phase(
        where, shapes, 0, grouped(near, swapped(near)), at=ats[0], weight=weight, attn="whole"
    )

    for k in range(1, last):
        x = arrived(done, counts[0], x) if k == 1 else after(done, x)[0]
        x, near_x = send(x, ring.along()), split(x)
        far_x = swapped(near_x)
        i = 2 * k - 1
        if k == last - 1:
            w, out, done = phase(
                where, shapes, 2 * i, grouped(near_x, far_x), at=ats[i], w=w,
                weight=weight, attn="whole", out=out,
            )
        y = arrived(done, counts[1], y) if k == 1 else after(done, y)[0]
        y, near_y = send(y, ring.along()) if k < last - 1 else None, split(y)
        far_y = swapped(near_y)
        groups = grouped(near_x, far_x, near_y, far_y)
        if k == last - 1:
            w, out, done = phase(
                where, shapes, 2 * (i + 1), grouped(near_y, far_y), at=ats[i + 1], w=w,
                weight=weight, attn="whole", out=out,
            )
        else:
            w, out, done = phase(
                where, shapes, 2 * i, groups, at=ats[i], w=w,
                weight=weight, attn="whole", out=out,
            )

    (x,) = after(done, x)
    near = split(x)
    far = swapped(near)
    begin = 2 * steps - 2
    w, done = phase(where, shapes, begin, grouped(near), at=ats[-2], w=w)
    w, squares = phase(where, shapes, begin, grouped(far), at=ats[-1], w=w, squares="new")

    pieces = [group[3] for group in grouped(near, far)]
    parts = [
        [(0, half, 0, pieces[0]), (half, half // 2, 0, pieces[1])],
        [(half + half // 2, half // 2, half // 2, pieces[1])],
    ]
    for late, masks in enumerate(rounds(devices)):
        squares = exchange(squares, devices, masks)
        if late == 0:
            before, done = phase(
                where, shapes, begin, parts[0], weight=weight, attn="first"
            )
            (squares,) = after(done, squares)
        elif late == 1:
            out, done = phase(
                where, shapes, begin, parts[1], weight=weight, attn="last",
                before=before, out=out,
            )
    return out, scaled(w, squares)


def solution(mesh):
    placed = (
        P("group", "dp"),
        P(("group", "dp"), None),
        P("dp", None),
        P("dp"),
        P(("group", "dp")),
    )
    ring = Ring(mesh.shape["dp"], 2 if mesh.shape["group"] == 2 else 1)
    return jax.shard_map(
        functools.partial(on_device, ring),
        mesh=mesh,
        in_specs=placed,
        out_specs=(P("group", "dp"), P(("group", "dp"), None)),
        check_vma=False,
    )
```

```python
import functools

import jax
import jax.numpy as jnp
import numpy as np
from jax import lax
from jax.experimental import pallas as pl
from jax.experimental.pallas import tpu as pltpu
from jax.sharding import PartitionSpec as P

HEADS = 64
HEAD_DIM = 128
SEQ = 16
TILE = 1024
MIB = 1024 * 1024


class Ring:
    def __init__(self, devices, columns):
        self.devices = devices
        self.length = devices // 2
        rows = self.length // columns
        if columns == 1:
            self.chips = list(range(rows))
        else:
            self.chips = [2 * z for z in range(rows)]
            self.chips += [2 * z + 1 for z in reversed(range(rows))]
        self.position = {chip: p for p, chip in enumerate(self.chips)}

    def device(self, position, core):
        return 2 * self.chips[position % self.length] + core

    def along(self):
        return [
            (self.device(p, core), self.device(p + 1 - 2 * core, core))
            for p in range(self.length)
            for core in range(2)
        ]

    def crossing(self):
        return [
            (self.device(p, core), self.device(p - 1 + 2 * core, 1 - core))
            for p in range(self.length)
            for core in range(2)
        ]

    def swap(self):
        return [(d, d ^ 1) for d in range(self.devices)]

    def owners(self):
        table, last = [], self.length // 2
        for d in range(self.devices):
            p, core = self.position[d // 2], d % 2
            row = [d, d ^ 1]
            for k in range(1, last + 1):
                step = k if core else -k
                row += [self.device(p + step, core), self.device(p - step, 1 - core)]
                if k < last:
                    row += [self.device(p + step, 1 - core), self.device(p - step, core)]
            table.append(row)
        return np.array(table, np.int32)


def zero_dead(count, ref):
    for s in range(ref.shape[0] // SEQ):

        @pl.when(s >= count)
        def _():
            dead = ref.at[s * SEQ : (s + 1) * SEQ]
            dead[...] = jnp.zeros_like(dead)


def prep_kernel(
    spans, rows, table_ref, me_ref, heads_ref, seqs_ref, grad_ref, a_ref, *refs
):
    copy_ref, left_ref, right_ref, count_ref, *at_refs, block_ref, sems, own_sems = refs
    half = left_ref.shape[1]
    owns = [
        pltpu.make_async_copy(grad_ref, copy_ref, own_sems.at[0]),
        pltpu.make_async_copy(grad_ref.at[:, pl.ds(0, half)], left_ref, own_sems.at[1]),
        pltpu.make_async_copy(grad_ref.at[:, pl.ds(half, half)], right_ref, own_sems.at[2]),
    ]
    for copy in owns:
        copy.start()
    count_ref[...] = jnp.full(count_ref.shape, seqs_ref[0], jnp.int32)
    width = heads_ref[0] * HEAD_DIM
    copies = []
    for i in range(block_ref.shape[0] // rows):
        owner = table_ref[me_ref[0], i]
        copies.append(
            pltpu.make_async_copy(
                a_ref.at[pl.ds(pl.multiple_of(owner * rows, rows), rows)],
                block_ref.at[pl.ds(i * rows, rows)],
                sems.at[i],
            )
        )
        copies[-1].start()
    waited = 0
    for at_ref, (begin, count) in zip(at_refs, spans):
        for copy in copies[waited : begin + count]:
            copy.wait()
        waited = max(waited, begin + count)
        block = block_ref[begin * rows : (begin + count) * rows, :]
        column = lax.broadcasted_iota(jnp.int32, block.shape, 1)
        at_ref[...] = jnp.where(column < width, block, jnp.zeros_like(block)).T
    for copy in owns:
        copy.wait()
    zero_dead(seqs_ref[0], left_ref)
    zero_dead(seqs_ref[0], right_ref)


def prepared(where, seq_counts, out_grad, attn_out, spans):
    slots, capacity = attn_out.shape
    rows, features = out_grad.shape
    vmem = pl.BlockSpec(memory_space=pltpu.VMEM)
    smem = pl.BlockSpec(memory_space=pltpu.SMEM)
    outs = [(rows, features), (rows, features // 2), (rows, features // 2)]
    outs += [(capacity, count * rows) for _, count in spans]
    shapes = [pltpu.VMEM(shape, jnp.bfloat16) for shape in outs]
    shapes.insert(3, pltpu.VMEM((8, 128), jnp.int32))
    copy, left, right, count, *ats = pl.pallas_call(
        functools.partial(prep_kernel, spans, rows),
        in_specs=[smem] * 4 + [pl.BlockSpec(memory_space=pl.ANY)] * 2,
        out_specs=[vmem] * len(shapes),
        out_shape=shapes,
        scratch_shapes=[
            pltpu.VMEM((slots, capacity), jnp.bfloat16),
            pltpu.SemaphoreType.DMA((slots // rows,)),
            pltpu.SemaphoreType.DMA((3,)),
        ],
        compiler_params=pltpu.CompilerParams(vmem_limit_bytes=12 * MIB),
        cost_estimate=pl.CostEstimate(flops=1, bytes_accessed=1, transcendentals=0),
        name="prep",
    )(
        *where,
        seq_counts,
        pltpu.with_memory_space_constraint(out_grad, pltpu.HBM),
        pltpu.with_memory_space_constraint(attn_out, pltpu.HBM),
    )
    return copy, (left, right), count, ats


def arrive_kernel(count_ref, x_ref, done_ref, out_ref):
    zero_dead(count_ref[0, 0], out_ref)


def arrived(done, count, x):
    vmem = pl.BlockSpec(memory_space=pltpu.VMEM)
    return pl.pallas_call(
        arrive_kernel,
        in_specs=[pl.BlockSpec(memory_space=pltpu.SMEM), vmem, vmem],
        out_specs=vmem,
        out_shape=pltpu.VMEM(x.shape, x.dtype),
        input_output_aliases={1: 0},
        compiler_params=pltpu.CompilerParams(vmem_limit_bytes=MIB),
        name="arrived",
    )(count, *[pltpu.with_memory_space_constraint(x, pltpu.VMEM) for x in (x, done)])


def phase_kernel(spec, *refs):
    groups, arrays, do_w, w_from, attn, fresh_w, fresh_out, squares, rows, begin = spec
    refs = list(refs)
    table_ref, me_ref, heads_ref = refs.pop(0), refs.pop(0), refs.pop(0)
    at_ref = refs.pop(0) if do_w else None
    weight_ref = refs.pop(0) if attn else None
    g_refs = [refs.pop(0) for _ in range(arrays)]
    if do_w and not fresh_w:
        refs.pop(0)
    before_ref = refs.pop(0) if attn == "last" else None
    added_ref = refs.pop(0) if squares == "added" else None
    if attn in ("whole", "last") and not fresh_out:
        refs.pop(0)
    w_ref = refs.pop(0) if do_w else None
    total_ref = refs.pop(0) if attn == "first" else None
    out_ref = refs.pop(0) if attn in ("whole", "last") else None
    squares_ref = refs.pop(0)
    if attn in ("whole", "last"):
        total_ref, block_ref, sems = refs
    if attn == "last":
        total_ref[...] = before_ref[...]
    elif attn:
        total_ref[...] = jnp.zeros_like(total_ref)
    if squares == "added":
        squares_ref[...] = added_ref[...]
    else:
        squares_ref[...] = jnp.zeros_like(squares_ref)

    def body(first, column, pieces, j, carry):
        here = pl.ds(pl.multiple_of(column + j * TILE, TILE), TILE)
        there = pl.ds(pl.multiple_of(first + j * TILE, TILE), TILE)
        g = [g_refs[i][start : start + count, here] for i, start, count in pieces]
        if do_w:
            fresh = jnp.concatenate(g[w_from:], axis=0) if len(g) > w_from + 1 else g[-1]
            w = jnp.dot(at_ref[...], fresh, preferred_element_type=jnp.float32)
            if not fresh_w:
                w = w + w_ref[:, there]
            w_ref[:, there] = w
        if squares:
            folded = jnp.sum((w * w).reshape(w.shape[0] // 8, 8, TILE), axis=0)
            total = squares_ref[...]
            for lane in range(0, TILE, 128):
                total = total + folded[:, lane : lane + 128]
            squares_ref[...] = total
        if attn:
            total_ref[...] += lax.dot_general(
                jnp.concatenate(g, axis=0),
                weight_ref[:, there],
                (((1,), (1,)), ((), ())),
                preferred_element_type=jnp.float32,
            )
        return carry

    for first, width, column, pieces in groups:
        step = functools.partial(body, first, column, pieces)
        lax.fori_loop(0, width // TILE, step, 0)
    if attn in ("whole", "last"):
        total = total_ref[...]
        column = lax.broadcasted_iota(jnp.int32, total.shape, 1)
        live = column < heads_ref[0] * HEAD_DIM
        block_ref[...] = jnp.where(live, total, 0.0).astype(jnp.bfloat16)
        copies = []
        for i in range(total.shape[0] // rows):
            owner = table_ref[me_ref[0], begin + i]
            copies.append(
                pltpu.make_async_copy(
                    block_ref.at[pl.ds(i * rows, rows)],
                    out_ref.at[pl.ds(pl.multiple_of(owner * rows, rows), rows)],
                    sems.at[i],
                )
            )
            copies[-1].start()
        for copy in copies:
            copy.wait()


def phase(
    where, shapes, begin, groups, at=None, w=None,
    weight=None, attn=None, before=None, out=None, squares=None, added=None,
    w_from=0,
):
    slots, capacity, features, rows = shapes
    do_w = at is not None
    arrays, described = [], []
    for first, width, column, pieces in groups:
        placed = []
        for array, start, count in pieces:
            known = [i for i, x in enumerate(arrays) if x is array]
            if not known:
                arrays.append(array)
            placed.append((known[0] if known else len(arrays) - 1, start, count))
        described.append((first, width, column, tuple(placed)))
    height = sum(count for _, _, count in groups[0][3])
    vmem = pl.BlockSpec(memory_space=pltpu.VMEM)
    smem = pl.BlockSpec(memory_space=pltpu.SMEM)
    hbm = pl.BlockSpec(memory_space=pl.ANY)

    args, specs, outs, out_specs, aliases, scratch = [], [], [], [], {}, []

    def add(arg, spec):
        args.append(arg)
        specs.append(spec)

    def add_vmem(arg):
        add(pltpu.with_memory_space_constraint(arg, pltpu.VMEM), vmem)

    for scalar in where:
        add(scalar, smem)
    if do_w:
        add_vmem(at)
    if attn:
        add_vmem(weight)
    for array in arrays:
        add_vmem(array)
    if do_w:
        if w is not None:
            aliases[len(args)] = len(outs)
            add_vmem(w)
        outs.append(pltpu.VMEM((capacity, features), jnp.float32))
        out_specs.append(vmem)
    if attn == "last":
        add_vmem(before)
    if squares == "added":
        add_vmem(added)
    if attn == "first":
        outs.append(pltpu.VMEM((height, capacity), jnp.float32))
        out_specs.append(vmem)
    elif attn:
        if out is not None:
            aliases[len(args)] = len(outs)
            add(out, hbm)
        outs.append(jax.ShapeDtypeStruct((slots, capacity), jnp.bfloat16))
        out_specs.append(hbm)
        scratch = [
            pltpu.VMEM((height, capacity), jnp.float32),
            pltpu.VMEM((height, capacity), jnp.bfloat16),
            pltpu.SemaphoreType.DMA((height // rows,)),
        ]
    outs.append(pltpu.VMEM((8, 128), jnp.float32))
    out_specs.append(vmem)
    spec = (
        tuple(described), len(arrays), do_w, w_from, attn, w is None, out is None,
        squares, rows, begin,
    )
    return pl.pallas_call(
        functools.partial(phase_kernel, spec),
        in_specs=specs,
        out_specs=out_specs,
        out_shape=outs,
        scratch_shapes=scratch,
        input_output_aliases=aliases,
        compiler_params=pltpu.CompilerParams(vmem_limit_bytes=12 * MIB),
        cost_estimate=pl.CostEstimate(
            flops=1,
            bytes_accessed=1,
            transcendentals=0,
        ),
        name="phase_" + "w" * do_w + "_" + str(attn),
    )(*args)


def scale_kernel(parts, w_ref, squares_ref, out_ref, block_ref, sems):
    capacity, features = w_ref.shape
    square_sum = jnp.sum(
        jnp.sum(squares_ref[...], axis=0, keepdims=True), axis=1, keepdims=True
    )
    factor = jnp.minimum(
        1.0, 1.0 / jnp.sqrt(square_sum / (HEADS * HEAD_DIM * features) + 1e-06)
    )
    copies = []
    height = capacity // parts
    for i in range(parts):
        part = pl.ds(i * height, height)
        block_ref[part, :] = (w_ref[part, :] * factor).astype(jnp.bfloat16)
        copies.append(pltpu.make_async_copy(block_ref.at[part], out_ref.at[part], sems.at[i]))
        copies[-1].start()
    for copy in copies:
        copy.wait()


def scaled(w, squares):
    capacity, features = w.shape
    vmem = pl.BlockSpec(memory_space=pltpu.VMEM)
    parts = capacity // 48
    return pl.pallas_call(
        functools.partial(scale_kernel, parts),
        in_specs=[vmem, vmem],
        out_specs=pl.BlockSpec(memory_space=pl.ANY),
        out_shape=jax.ShapeDtypeStruct((capacity, features), jnp.bfloat16),
        scratch_shapes=[
            pltpu.VMEM((capacity, features), jnp.bfloat16),
            pltpu.SemaphoreType.DMA((parts,)),
        ],
        compiler_params=pltpu.CompilerParams(vmem_limit_bytes=10 * MIB),
        cost_estimate=pl.CostEstimate(
            flops=capacity * features,
            bytes_accessed=2 * capacity * features,
            transcendentals=0,
        ),
        name="scale",
    )(pltpu.with_memory_space_constraint(w, pltpu.VMEM), squares)


def after(done, *arrays):
    vmem = pl.BlockSpec(memory_space=pltpu.VMEM)
    return pl.pallas_call(
        lambda *refs: None,
        in_specs=[vmem] * (len(arrays) + 1),
        out_specs=[vmem] * len(arrays),
        out_shape=[pltpu.VMEM(x.shape, x.dtype) for x in arrays],
        input_output_aliases={i: i for i in range(len(arrays))},
        compiler_params=pltpu.CompilerParams(vmem_limit_bytes=MIB),
        name="after",
    )(*[pltpu.with_memory_space_constraint(x, pltpu.VMEM) for x in (*arrays, done)])


def split_kernel(x_ref, left_ref, right_ref, sems):
    half = left_ref.shape[1]
    copies = [
        pltpu.make_async_copy(x_ref.at[:, pl.ds(0, half)], left_ref, sems.at[0]),
        pltpu.make_async_copy(x_ref.at[:, pl.ds(half, half)], right_ref, sems.at[1]),
    ]
    for copy in copies:
        copy.start()
    for copy in copies:
        copy.wait()


def split(x):
    vmem = pl.BlockSpec(memory_space=pltpu.VMEM)
    rows, features = x.shape
    return pl.pallas_call(
        split_kernel,
        in_specs=[vmem],
        out_specs=[vmem] * 2,
        out_shape=[pltpu.VMEM((rows, features // 2), x.dtype)] * 2,
        scratch_shapes=[pltpu.SemaphoreType.DMA((2,))],
        compiler_params=pltpu.CompilerParams(vmem_limit_bytes=MIB),
        name="split",
    )(pltpu.with_memory_space_constraint(x, pltpu.VMEM))


def rounds(devices):
    bits = [1 << i for i in range(devices.bit_length() - 1)]
    if len(bits) >= 4:
        bits = bits[1:3] + [bits[0]] + bits[3:]
    masks = []
    while bits:
        pair, bits = bits[:2], bits[2:]
        masks.append(pair + [sum(pair)] if len(pair) == 2 else pair)
    return masks


def exchange(x, devices, masks):
    total = x
    for mask in masks:
        total = total + lax.ppermute(x, "dp", [(d, d ^ mask) for d in range(devices)])
    return total


def on_device(ring, attn_out, out_grad, o_weight, head_counts, seq_counts):
    rows, features = out_grad.shape
    slots = attn_out.shape[0]
    devices, last = ring.devices, ring.length // 2
    steps = 2 * last
    spans = [(0, 2)]
    for k in range(1, last):
        joint = k < last - 1
        spans += [(4 * k - 2, 4), None] if joint else [(4 * k - 2, 2), (4 * k, 2)]
    spans += [(2 * steps - 2, 1), (2 * steps - 1, 1)]
    me = lax.axis_index("dp").astype(jnp.int32).reshape(1)
    where = (jnp.asarray(ring.owners()), me, head_counts)
    shapes = (slots, o_weight.shape[0], features, rows)
    weight, half = o_weight, features // 2

    def send(x, pairs):
        return lax.ppermute(x, "dp", pairs)

    def swapped(halves):
        return [send(x, ring.swap()) for x in halves]

    def grouped(*pairs):
        return [
            (c * half, half, 0, [(x[c], 0, rows) for x in pairs])
            for c in range(min(len(x) for x in pairs))
        ]

    x = send(out_grad, ring.along())
    own, near, count, ats = prepared(
        where, seq_counts, out_grad, attn_out, [x for x in spans if x]
    )
    ats = [ats.pop(0) if x else None for x in spans]
    others = swapped(near)
    y = send(after(others[1], own)[0], ring.crossing())
    counts = send(count, ring.along()), send(count, ring.crossing())
    w, out, done = phase(
        where, shapes, 0, grouped(near, others), at=ats[0], weight=weight, attn="whole"
    )

    for k in range(1, last):
        x = arrived(done, counts[0], x) if k == 1 else after(done, x)[0]
        x, near_x = send(x, ring.along()), split(x)
        far_x = swapped(near_x)
        i = 2 * k - 1
        if k == last - 1:
            w, out, done = phase(
                where, shapes, 2 * i, grouped(near_x, far_x), at=ats[i], w=w,
                weight=weight, attn="whole", out=out,
            )
        y = arrived(done, counts[1], y) if k == 1 else after(done, y)[0]
        y, near_y = send(y, ring.along()) if k < last - 1 else None, split(y)
        far_y = swapped(near_y)
        groups = grouped(near_x, far_x, near_y, far_y)
        if k == last - 1:
            w, out, done = phase(
                where, shapes, 2 * (i + 1), grouped(near_y, far_y), at=ats[i + 1], w=w,
                weight=weight, attn="whole", out=out,
            )
        else:
            w, out, done = phase(
                where, shapes, 2 * i, groups, at=ats[i], w=w,
                weight=weight, attn="whole", out=out,
            )

    (x,) = after(done, x)
    near = split(x)
    far = swapped(near)
    begin = 2 * steps - 2
    w, done = phase(where, shapes, begin, grouped(near), at=ats[-2], w=w)
    w, squares = phase(where, shapes, begin, grouped(far), at=ats[-1], w=w, squares="new")

    pieces = [group[3] for group in grouped(near, far)]
    parts = [
        [(0, half, 0, pieces[0]), (half, half // 2, 0, pieces[1])],
        [(half + half // 2, half // 2, half // 2, pieces[1])],
    ]
    for late, masks in enumerate(rounds(devices)):
        squares = exchange(squares, devices, masks)
        if late == 0:
            before, done = phase(
                where, shapes, begin, parts[0], weight=weight, attn="first"
            )
            (squares,) = after(done, squares)
        elif late == 1:
            out, done = phase(
                where, shapes, begin, parts[1], weight=weight, attn="last",
                before=before, out=out,
            )
    return out, scaled(w, squares)


def solution(mesh):
    placed = (
        P("group", "dp"),
        P(("group", "dp"), None),
        P("dp", None),
        P("dp"),
        P(("group", "dp")),
    )
    ring = Ring(mesh.shape["dp"], 2 if mesh.shape["group"] == 2 else 1)
    return jax.shard_map(
        functools.partial(on_device, ring),
        mesh=mesh,
        in_specs=placed,
        out_specs=(P("group", "dp"), P(("group", "dp"), None)),
        check_vma=False,
    )
```
